32 devices in a mesh: row: 4 (over y, core), col: 8 (over z, x).
Axes of the slice: x: 2, y: 2, z: 4, core: 2. Of those that a mesh axis runs over, the one named last changes fastest.
Arguments:
- features: bfloat16 [6, 32, 32, 512], P(None, 'row', 'col'), may hold values from -13 to 13
- priors: bfloat16 [2, 6, 32, 32, 512], P(None, None, 'row', 'col'), may hold values from 0 to 13
- domain: int32 [6], replicated, may hold values from 0 to 1, as said below
- shared_w: bfloat16 [3, 3, 3, 512, 512], replicated, may hold values from -0.09375 to 0.09375
- shared_gain: float32 [3, 512], replicated, may hold values from 0.5 to 1.5
- shared_bias: float32 [3, 512], replicated, may hold values from -3 to 3
- first_w: bfloat16 [2, 1024, 512], replicated, may hold values from -0.1875 to 0.1875
- second_w: bfloat16 [2, 512, 512], replicated, may hold values from -0.25 to 0.25
- task_conv: bfloat16 [2, 3, 3, 512, 512], replicated, may hold values from -0.09375 to 0.09375
- task_gain: float32 [2, 3, 512], replicated, may hold values from 0.5 to 1.5
- task_bias: float32 [2, 3, 512], replicated, may hold values from -3 to 3
- shared_cot: bfloat16 [6, 16, 16, 512], P(None, 'row', 'col'), may hold values from -6 to 6
- task_cot: bfloat16 [2, 6, 16, 16, 512], P(None, None, 'row', 'col'), may hold values from -6 to 6
Outputs:
- shared_out: bfloat16 [6, 16, 16, 512], P(None, 'row', 'col')
- task_out: bfloat16 [2, 6, 16, 16, 512], P(None, None, 'row', 'col')
- grad_features: float32 [6, 32, 32, 512], P(None, 'row', 'col')
- grad_priors: float32 [2, 6, 32, 32, 512], P(None, None, 'row', 'col')
- grad_shared_w: float32 [3, 3, 3, 512, 512], replicated
- grad_shared_gain: float32 [3, 512], replicated
- grad_shared_bias: float32 [3, 512], replicated
- grad_first_w: float32 [2, 1024, 512], replicated
- grad_second_w: float32 [2, 512, 512], replicated
- grad_task_conv: float32 [2, 3, 3, 512, 512], replicated
- grad_task_gain: float32 [2, 3, 512], replicated
- grad_task_bias: float32 [2, 3, 512], replicated
The draws below stay inside these ranges and needn't reach their ends.
Inputs may be any that keep to these rules, and one draw needn't show every extreme that they name: `domain`: every one of the 2 domains names at least one image.
All inputs are finite; a program needn't handle non-finite values.
Results may differ from the reference program's by a relative error of at most 0.015.
Values may be sent and summed in bfloat16 or wider, within the bound.
No kernel may reach another device: no remote copies, remote signals or barrier semaphores. Data moves between devices by JAX's collectives and lax.ppermute only.
A program may use at most 256 MiB of HBM per device.

```python
import math
from functools import partial
import jax
import jax.numpy as jnp
from jax import lax

CH = 512
TASKS = 2
CONVS = 3
DOMAINS = 2
IMAGES = 6
H = 32
W = 32


def ramp_scale(growth):
    row_pos = jnp.arange(H, dtype=jnp.float32) / (H - 1)
    across = jnp.arange(W, dtype=jnp.float32) / (W - 1)
    exponent = row_pos[:, None] + across[None, :] - 1.0
    return jnp.exp(math.log(growth) * exponent)[None, :, :, None]


def draw_features(key, part):
    layout = (IMAGES, H, W, CH)
    fresh = jax.random.fold_in(key, 21)
    values = jnp.clip(jax.random.normal(fresh, layout, jnp.float32), -4.0, 4.0)
    growth = 3.2
    return (values * ramp_scale(growth)).astype(jnp.bfloat16)


def draw_priors(key, part):
    layout = (TASKS, IMAGES, H, W, CH)
    fresh = jax.random.fold_in(key, 22)
    values = jnp.abs(jnp.clip(jax.random.normal(fresh, layout, jnp.float32), -4.0, 4.0))
    growth = 3.2
    return (values * ramp_scale(growth)).astype(jnp.bfloat16)


def draw_domain(key, part):
    order = jax.random.permutation(jax.random.fold_in(key, 23), IMAGES)
    border = jax.random.randint(jax.random.fold_in(key, 24), (), 1, IMAGES)
    return jnp.where(order < border, 1, 0).astype(jnp.int32)


def levels(stream_key, shape, shards, low, top_value):
    def one(position, parts):
        draws = jax.random.uniform(jax.random.fold_in(jax.random.fold_in(stream_key, 6), position), (parts,), jnp.float32, low / len(shards), top_value / len(shards))
        return jnp.repeat(jnp.exp(draws), shape[position] // parts).reshape((-1,) + (1,) * (len(shape) - position - 1))

    level = one(*shards[0])
    for cut in shards[1:]:
        level = level * one(*cut)
    return level


def normal_values(rng, shape, width, limit, split=(), kind=jnp.bfloat16):
    drawn = width * jax.random.normal(rng, shape, jnp.float32)
    if split:
        drawn = drawn * levels(rng, shape, split, -0.22, 0.18)
    return jnp.clip(drawn, -limit, limit).astype(kind)


def setup_inputs(seed: int = 0) -> dict:
    key_list = jax.random.split(jax.random.key(seed), 14)
    features = draw_features(jax.random.fold_in(key_list[13], 71), 0)
    priors = draw_priors(jax.random.fold_in(key_list[13], 71), 0)
    domain = draw_domain(jax.random.fold_in(key_list[13], 71), 0)
    shared_w = normal_values(key_list[3], (CONVS, 3, 3, CH, CH), (9 * CH) ** -0.5, 0.09375)
    shared_gain = jnp.clip(1.0 + 0.1 * jax.random.normal(key_list[4], (CONVS, CH), jnp.float32), 0.5, 1.5)
    shared_bias = normal_values(key_list[5], (CONVS, CH), 0.5, 3.0, (), jnp.float32)
    first_w = normal_values(key_list[6], (TASKS, 2 * CH, CH), (2 * CH) ** -0.5, 0.1875)
    second_w = normal_values(key_list[7], (TASKS, CH, CH), CH ** -0.5, 0.25)
    task_conv = normal_values(key_list[8], (TASKS, 3, 3, CH, CH), (9 * CH) ** -0.5, 0.09375)
    task_gain = jnp.clip(1.0 + 0.1 * jax.random.normal(key_list[9], (TASKS, 3, CH), jnp.float32), 0.5, 1.5)
    task_bias = normal_values(key_list[10], (TASKS, 3, CH), 0.5, 3.0, (), jnp.float32)
    shared_cot = normal_values(key_list[11], (IMAGES, H // 2, W // 2, CH), 1.0, 6.0, ((1, 4), (2, 8)))
    task_cot = normal_values(key_list[12], (TASKS, IMAGES, H // 2, W // 2, CH), 1.0, 6.0, ((2, 4), (3, 8)))
    return dict(features=features, priors=priors, domain=domain, shared_w=shared_w, shared_gain=shared_gain, shared_bias=shared_bias, first_w=first_w, second_w=second_w, task_conv=task_conv, task_gain=task_gain, task_bias=task_bias, shared_cot=shared_cot, task_cot=task_cot)


EPSILON = 1e-05
HIGHEST = lax.Precision.HIGHEST

@jax.custom_vjp
def low(v):
    return lax.optimization_barrier(v.astype(jnp.bfloat16)).astype(jnp.float32)

@jax.custom_vjp
def low_back(v):
    return v

def low_keep(v):
    return (low(v), None)

def low_pass(kept, grad):
    return (grad,)

def back_keep(v):
    return (v, None)

def back_low(kept, grad):
    return (low(grad),)
low.defvjp(low_keep, low_pass)
low_back.defvjp(back_keep, back_low)

def convolve(values, kernel):
    return lax.conv_general_dilated(values, kernel, (1, 1), ((1, 1), (1, 1)), dimension_numbers=('NHWC', 'HWIO', 'NHWC'), precision=HIGHEST)

def project(values, weight):
    return jnp.einsum('bhwc,cd->bhwd', values, weight, precision=HIGHEST)

def normalize(values, norm_gain, norm_bias, member, counts):
    totals = jnp.einsum('bk,bhwc->kc', member, values, precision=HIGHEST)
    average = totals / counts[:, None]
    centered = values - jnp.einsum('bk,kc->bc', member, average, precision=HIGHEST)[:, None, None, :]
    spread = jnp.einsum('bk,bhwc->kc', member, centered * centered, precision=HIGHEST) / counts[:, None]
    inverse = jnp.einsum('bk,kc->bc', member, lax.rsqrt(spread + EPSILON), precision=HIGHEST)
    return centered * inverse[:, None, None, :] * norm_gain + norm_bias

def mean_pool(values):
    images, height, breadth, channels = values.shape
    return lax.optimization_barrier(jnp.mean(values.reshape(images, height // 2, 2, breadth // 2, 2, channels), axis=(2, 4)))

def forward(member, counts, features, priors, shared_w, shared_gain, shared_bias, first_w, second_w, task_conv, task_gain, task_bias):
    current = features
    activations = []
    for conv_index in range(CONVS):
        product = low_back(convolve(current, shared_w[conv_index]))
        current = jax.nn.silu(normalize(product, shared_gain[conv_index], shared_bias[conv_index], member, counts))
        if conv_index + 1 < CONVS:
            current = low(current)
        activations.append(current)
    first_act = activations[0]
    last_act = activations[-1]
    task_outs = []
    for task_index in range(TASKS):
        joined = jnp.concatenate([first_act, priors[task_index]], axis=-1)
        hidden = low_back(project(joined, first_w[task_index]))
        hidden = low(jax.nn.silu(normalize(hidden, task_gain[task_index, 0], task_bias[task_index, 0], member, counts)))
        gate_pre = low_back(project(hidden, second_w[task_index]))
        attention = jax.nn.sigmoid(normalize(gate_pre, task_gain[task_index, 1], task_bias[task_index, 1], member, counts))
        masked = low(attention * last_act)
        refined = low_back(convolve(masked, task_conv[task_index]))
        refined = jax.nn.silu(normalize(refined, task_gain[task_index, 2], task_bias[task_index, 2], member, counts))
        task_outs.append(mean_pool(refined))
    return (mean_pool(last_act), jnp.stack(task_outs))

def reference(features, priors, domain, shared_w, shared_gain, shared_bias, first_w, second_w, task_conv, task_gain, task_bias, shared_cot, task_cot):
    member = (domain[:, None] == jnp.arange(DOMAINS, dtype=jnp.int32)[None, :]).astype(jnp.float32)
    counts = lax.optimization_barrier(jnp.sum(member, axis=0)) * (H * W)
    outputs, pullback = jax.vjp(partial(forward, member, counts), features.astype(jnp.float32), priors.astype(jnp.float32), shared_w.astype(jnp.float32), shared_gain, shared_bias, first_w.astype(jnp.float32), second_w.astype(jnp.float32), task_conv.astype(jnp.float32), task_gain, task_bias)
    grads = pullback((shared_cot.astype(jnp.float32), task_cot.astype(jnp.float32)))
    return (outputs[0].astype(jnp.bfloat16), outputs[1].astype(jnp.bfloat16), grads[0], grads[1], grads[2], grads[3], grads[4], grads[5], grads[6], grads[7], grads[8], grads[9])
```

```python
import jax
import jax.numpy as jnp
import numpy as np
from jax import lax
from jax.sharding import Mesh, PartitionSpec as P

TASKS = 2
CONVS = 3
DOMAINS = 2
CORES = 2

EPSILON = 1e-05
HIGHEST = lax.Precision.HIGHEST
ALL = ("y", "c", "z", "x")
ROW = ("y", "c")
COL = ("z", "x")
CHIPS = ("y", "z", "x")


def size_of(axes):
    total = 1
    for axis in axes:
        total *= lax.axis_size(axis)
    return total


def exchange(value, axes):
    count = size_of(axes)
    return [value] + [
        lax.ppermute(value, axes, [(i, i ^ k) for i in range(count)]) for k in range(1, count)
    ]


def tree_sum(values):
    while len(values) > 1:
        values = [a + b for a, b in zip(values[::2], values[1::2])]
    return values[0]


STAGES = (("c",), ("y", "x"), ("z",))


def total_stats(average, squares, number):
    for axes in STAGES:
        both = exchange(jnp.stack([average, squares]), axes)
        averages = [b[0] for b in both]
        average = tree_sum(averages) * (1.0 / len(both))
        squares = tree_sum([b[1] for b in both]) + number * tree_sum(
            [(a - average) * (a - average) for a in averages]
        )
        number = number * len(both)
    return average, squares / number


def total_sums(value):
    for axes in STAGES:
        value = tree_sum(exchange(value, axes))
    return value


def halo(tile, pad=1):
    for axes, dim in ((ROW, 0), (COL, 1)):
        count, length = size_of(axes), tile.shape[dim]
        up = [(i, i + 1) for i in range(count - 1)]
        down = [(i + 1, i) for i in range(count - 1)]
        before = lax.ppermute(lax.slice_in_dim(tile, length - pad, length, axis=dim), axes, up)
        after = lax.ppermute(lax.slice_in_dim(tile, 0, pad, axis=dim), axes, down)
        tile = jnp.concatenate([before, tile, after], axis=dim)
    return tile


def inner(tile):
    return tile[1:-1, 1:-1]


def convolve(padded, kernel):
    return lax.conv_general_dilated(
        padded,
        kernel,
        (1, 1),
        "VALID",
        dimension_numbers=("HWNC", "HWIO", "HWNC"),
        preferred_element_type=jnp.float32,
    )


def convolve_back(padded_grad, kernel):
    return lax.conv_general_dilated(
        padded_grad,
        jnp.flip(kernel, (0, 1)),
        (1, 1),
        "VALID",
        dimension_numbers=("HWNC", "HWOI", "HWNC"),
        preferred_element_type=jnp.float32,
    )


def project(values, weight):
    return jnp.einsum("hwnc,cd->hwnd", values, weight, preferred_element_type=jnp.float32)


def project_back(values, weight):
    return jnp.einsum("hwnd,cd->hwnc", values, weight, preferred_element_type=jnp.float32)


def outer(values, grads):
    return jnp.einsum("hwnc,hwnd->cd", values, grads, preferred_element_type=jnp.float32)


def silu_slope(pre_act):
    logistic = jax.nn.sigmoid(pre_act)
    return logistic * (1.0 + pre_act * (1.0 - logistic))


def domain_totals(member, values):
    return jnp.dot(member.T, jnp.sum(values, axis=(0, 1)), precision=HIGHEST)


def per_image(member, stats):
    return jnp.dot(member, stats, precision=HIGHEST)[None, None]


def local_stats(member, tile, number):
    average = domain_totals(member, tile) / number
    centered = tile - per_image(member, average)
    return average, domain_totals(member, centered * centered)


def forward_stats(member, tiles, number):
    local = [local_stats(member, tile, number) for tile in tiles]
    average, variance = total_stats(
        jnp.stack([a for a, _ in local]), jnp.stack([s for _, s in local]), number[None]
    )
    return average, lax.rsqrt(variance + EPSILON)


def backward_sums(member, pairs):
    local = [
        jnp.stack([domain_totals(member, dy), domain_totals(member, dy * form)])
        for dy, form in pairs
    ]
    return total_sums(jnp.stack(local))


def backward_input(member, dy, form, inverse, gain, sums, counts):
    plain = per_image(member, sums[0] / counts[:, None])
    cross = per_image(member, sums[1] / counts[:, None])
    return per_image(member, inverse) * gain * (dy - plain - form * cross)


def mean_pool(values):
    h, w, n, c = values.shape
    return jnp.mean(values.reshape(h // 2, 2, w // 2, 2, n, c), axis=(1, 3))


def mean_pool_back(grad_out):
    h, w, n, c = grad_out.shape
    spread = jnp.broadcast_to(
        0.25 * grad_out[:, None, :, None].astype(jnp.float32), (h, 2, w, 2, n, c)
    )
    return spread.reshape(2 * h, 2 * w, n, c)


def to_blocks(tile, by):
    counts = [lax.axis_size(a) for a in CHIPS]
    blocks = 1
    for axis in by:
        blocks *= lax.axis_size(axis)
    h, w, n, c = tile.shape
    cut = jnp.moveaxis(tile.reshape(h, w, n, blocks, c // blocks), 3, 0)
    shape = [s if a in by else 1 for a, s in zip(CHIPS, counts)]
    cut = jnp.broadcast_to(cut.reshape(*shape, *cut.shape[1:]), (*counts, *cut.shape[1:]))
    cut = cut.reshape(-1, *cut.shape[3:])
    got = lax.all_to_all(cut, CHIPS, 0, 0)
    ny, nz, nx = counts
    got = got.reshape(ny, nz, nx, h, w, n, c // blocks)
    got = got.transpose(0, 5, 3, 1, 2, 4, 6)
    return got.reshape(ny * n, h, nz * nx * w, c // blocks)


def share_act(padded):
    return to_blocks(padded[:, 1:-1], ("z",))


def kernel_chunk(act, grads):
    grads = to_blocks(grads, ("y", "x"))
    act = jnp.pad(act, ((0, 0), (0, 0), (1, 1), (0, 0)))
    part = lax.conv_general_dilated(
        act,
        grads,
        (1, 1),
        "VALID",
        dimension_numbers=("CHWN", "IHWO", "HWNC"),
        preferred_element_type=jnp.float32,
    )
    a, b, rows, cols = part.shape
    part = part.reshape(a * b, CORES, rows // CORES, cols)
    me = lax.axis_index("c")
    mine = lax.dynamic_index_in_dim(part, me, 1, keepdims=False)
    other = lax.dynamic_index_in_dim(part, 1 - me, 1, keepdims=False).astype(jnp.bfloat16)
    other = lax.ppermute(other, "c", [(0, 1), (1, 0)])
    return (mine + other.astype(jnp.float32)).astype(jnp.bfloat16)


def gather_kernel(chunk):
    ny, nc, nz, nx = (lax.axis_size(a) for a in ALL)
    taps, rows, cols = chunk.shape
    whole = lax.all_gather(chunk, ALL, axis=0, tiled=False)
    whole = whole.reshape(ny, nc, nz, nx, taps, rows, cols).transpose(4, 2, 1, 5, 0, 3, 6)
    whole = whole.reshape(taps, nz * nc * rows, ny * nx * cols)
    return whole.astype(jnp.float32)


def scatter_matrices(parts):
    m, r, c = parts.shape
    sizes = {a: lax.axis_size(a) for a in ALL}
    per = r // size_of(ALL)
    left = ["m", *ALL, "r", "k"]
    parts = parts.reshape(m, *(sizes[a] for a in ALL), per, c)
    for axes in STAGES:
        rest = [d for d in left if d not in axes]
        parts = parts.transpose([left.index(d) for d in (*axes, *rest)])
        left = rest
        count = size_of(axes)
        parts = parts.reshape(count, *parts.shape[len(axes):])
        me = lax.axis_index(axes)
        got = [lax.dynamic_index_in_dim(parts, me, 0, keepdims=False)]
        for k in range(1, count):
            send = lax.dynamic_index_in_dim(parts, me ^ k, 0, keepdims=False)
            send = lax.ppermute(
                send.astype(jnp.bfloat16), axes, [(i, i ^ k) for i in range(count)]
            )
            got.append(send.astype(jnp.float32))
        parts = tree_sum(got)
    return parts.astype(jnp.bfloat16)


def body(
    features,
    priors,
    domain,
    shared_w,
    shared_gain,
    shared_bias,
    first_w,
    second_w,
    task_conv,
    task_gain,
    task_bias,
    shared_cot,
    task_cot,
):
    images, height, breadth, channels = features.shape
    member = (domain[:, None] == jnp.arange(DOMAINS, dtype=jnp.int32)[None, :]).astype(jnp.float32)
    named = jnp.sum(member, axis=0)[:, None]
    number = named * (height * breadth)
    counts = named[:, 0] * (height * breadth * size_of(ALL))
    row, col = lax.axis_index(ROW), lax.axis_index(COL)
    rows = row * height + jnp.arange(height + 2) - 1
    cols = col * breadth + jnp.arange(breadth + 2) - 1
    inside = (
        ((rows >= 0) & (rows < height * size_of(ROW)))[:, None]
        & ((cols >= 0) & (cols < breadth * size_of(COL)))[None, :]
    )[:, :, None, None]

    def only_inside(tile):
        return jnp.where(inside, tile, 0.0).astype(jnp.bfloat16)

    features = halo(features.transpose(1, 2, 0, 3))
    priors = [halo(priors[t].transpose(1, 2, 0, 3)) for t in range(TASKS)]
    shared_cot = shared_cot.transpose(1, 2, 0, 3)
    task_cot = [halo(task_cot[t].transpose(1, 2, 0, 3)) for t in range(TASKS)]

    def apply_norm(tile, average, inverse, gain, bias):
        form = (tile - per_image(member, average)) * per_image(member, inverse)
        return form, form * gain + bias

    product = convolve(features, shared_w[0])
    product_halo = halo(product)
    features_blocks = share_act(features)
    average, inverse = forward_stats(member, [product], number)
    inverse1 = inverse[0]
    form1, normed1 = apply_norm(product_halo, average[0], inverse1, shared_gain[0], shared_bias[0])
    act1 = only_inside(jax.nn.silu(normed1))

    product = convolve(act1, shared_w[1])
    product_halo = halo(product)
    hidden = [
        project(act1, first_w[t, :channels]) + project(priors[t], first_w[t, channels:])
        for t in range(TASKS)
    ]
    act1_blocks = share_act(act1)
    average, inverse = forward_stats(member, [product] + [inner(h) for h in hidden], number)
    inverse2, inverse_h = inverse[0], inverse[1:]
    form2, normed2 = apply_norm(product_halo, average[0], inverse2, shared_gain[1], shared_bias[1])
    act2 = only_inside(jax.nn.silu(normed2))
    form_h, normed_h, hidden_act = [], [], []
    for t in range(TASKS):
        form, normed = apply_norm(
            hidden[t], average[1 + t], inverse_h[t], task_gain[t, 0], task_bias[t, 0]
        )
        form_h.append(inner(form))
        normed_h.append(inner(normed))
        hidden_act.append(jax.nn.silu(normed).astype(jnp.bfloat16))

    product = convolve(act2, shared_w[2])
    product_halo = halo(product)
    gate = [project(hidden_act[t], second_w[t]) for t in range(TASKS)]
    act2_blocks = share_act(act2)
    average, inverse = forward_stats(member, [product] + [inner(g) for g in gate], number)
    inverse3, inverse_g = inverse[0], inverse[1:]
    form3, normed3 = apply_norm(product_halo, average[0], inverse3, shared_gain[2], shared_bias[2])
    last = jax.nn.silu(normed3)
    shared_out = mean_pool(inner(last)).astype(jnp.bfloat16)
    form_g, attention, masked = [], [], []
    for t in range(TASKS):
        form, normed = apply_norm(
            gate[t], average[1 + t], inverse_g[t], task_gain[t, 1], task_bias[t, 1]
        )
        form_g.append(inner(form))
        weight = jax.nn.sigmoid(normed)
        attention.append(inner(weight))
        masked.append(only_inside(weight * last))

    refined = [convolve(masked[t], task_conv[t]) for t in range(TASKS)]
    refined_halo = [halo(r) for r in refined]
    masked_blocks = [share_act(m) for m in masked]
    average, inverse_r = forward_stats(member, refined, number)
    form_r, dy_r, task_outs = [], [], []
    for t in range(TASKS):
        form, normed = apply_norm(
            refined_halo[t], average[t], inverse_r[t], task_gain[t, 2], task_bias[t, 2]
        )
        form_r.append(form)
        task_outs.append(mean_pool(inner(jax.nn.silu(normed))).astype(jnp.bfloat16))
        dy_r.append(inner(mean_pool_back(task_cot[t])) * silu_slope(normed))

    sums_r = backward_sums(member, [(inner(dy_r[t]), inner(form_r[t])) for t in range(TASKS)])
    dv_r = [
        only_inside(
            backward_input(
                member, dy_r[t], form_r[t], inverse_r[t], task_gain[t, 2], sums_r[t], counts
            )
        )
        for t in range(TASKS)
    ]
    task_chunks = [kernel_chunk(masked_blocks[t], inner(dv_r[t])) for t in range(TASKS)]
    grad_masked = [convolve_back(dv_r[t], task_conv[t]) for t in range(TASKS)]

    grad_last = mean_pool_back(shared_cot)
    own_last = inner(last)
    dy_g = []
    for t in range(TASKS):
        grad_last = grad_last + grad_masked[t] * attention[t]
        dy_g.append(grad_masked[t] * own_last * attention[t] * (1.0 - attention[t]))
    dy3 = grad_last * silu_slope(inner(normed3))
    dy3_halo = halo(dy3)
    sums = backward_sums(
        member, [(dy3, inner(form3))] + [(dy_g[t], form_g[t]) for t in range(TASKS)]
    )
    sums3, sums_g = sums[0], sums[1:]
    dv3 = only_inside(
        backward_input(member, dy3_halo, form3, inverse3, shared_gain[2], sums3, counts)
    )
    dv_g = [
        backward_input(
            member, dy_g[t], form_g[t], inverse_g[t], task_gain[t, 1], sums_g[t], counts
        ).astype(jnp.bfloat16)
        for t in range(TASKS)
    ]
    chunk3 = kernel_chunk(act2_blocks, inner(dv3))
    grad_act2 = convolve_back(dv3, shared_w[2])

    dy2 = grad_act2 * silu_slope(inner(normed2))
    dy2_halo = halo(dy2)
    dy_h = [project_back(dv_g[t], second_w[t]) * silu_slope(normed_h[t]) for t in range(TASKS)]
    sums = backward_sums(
        member, [(dy2, inner(form2))] + [(dy_h[t], form_h[t]) for t in range(TASKS)]
    )
    sums2, sums_h = sums[0], sums[1:]
    dv2 = only_inside(
        backward_input(member, dy2_halo, form2, inverse2, shared_gain[1], sums2, counts)
    )
    dv_h = [
        backward_input(
            member, dy_h[t], form_h[t], inverse_h[t], task_gain[t, 0], sums_h[t], counts
        ).astype(jnp.bfloat16)
        for t in range(TASKS)
    ]
    chunk2 = kernel_chunk(act1_blocks, inner(dv2))
    grad_act1 = convolve_back(dv2, shared_w[1])
    for t in range(TASKS):
        grad_act1 = grad_act1 + project_back(dv_h[t], first_w[t, :channels])

    dy1 = grad_act1 * silu_slope(inner(normed1))
    dy1_halo = halo(dy1)
    sums1 = backward_sums(member, [(dy1, inner(form1))])[0]
    dv1 = only_inside(
        backward_input(member, dy1_halo, form1, inverse1, shared_gain[0], sums1, counts)
    )
    chunk1 = kernel_chunk(features_blocks, inner(dv1))
    grad_features = convolve_back(dv1, shared_w[0])
    grad_priors = [project_back(dv_h[t], first_w[t, channels:]) for t in range(TASKS)]

    matrices = []
    for t in range(TASKS):
        matrices += [outer(inner(act1), dv_h[t]), outer(inner(priors[t]), dv_h[t])]
    for t in range(TASKS):
        matrices.append(outer(inner(hidden_act[t]), dv_g[t]))
    matrices = scatter_matrices(jnp.stack(matrices))
    matrices = lax.all_gather(matrices, ALL, axis=1, tiled=True).astype(jnp.float32)
    grad_first = matrices[: 2 * TASKS].reshape(TASKS, 2 * channels, channels)
    grad_second = matrices[2 * TASKS :]

    shape = (3, 3, channels, channels)
    grad_task = jnp.stack([gather_kernel(c).reshape(shape) for c in task_chunks])
    grad_shared = jnp.stack([gather_kernel(c).reshape(shape) for c in (chunk1, chunk2, chunk3)])

    shared_sums = jnp.sum(jnp.stack([sums1, sums2, sums3]), axis=2)
    task_sums = jnp.sum(jnp.stack([sums_h, sums_g, sums_r], axis=1), axis=3)

    def images_first(tile):
        return tile.transpose(2, 0, 1, 3)

    return (
        images_first(shared_out),
        jnp.stack([images_first(o) for o in task_outs]),
        images_first(grad_features),
        jnp.stack([images_first(g) for g in grad_priors]),
        grad_shared,
        shared_sums[:, 1],
        shared_sums[:, 0],
        grad_first,
        grad_second,
        grad_task,
        task_sums[:, :, 1],
        task_sums[:, :, 0],
    )


def solution(mesh):
    rows, cols = mesh.shape["row"], mesh.shape["col"]
    along_y = rows // CORES
    along_x = along_y
    grid = np.asarray(mesh.devices).reshape(along_y, CORES, cols // along_x, along_x)
    split = Mesh(grid, ALL)
    return jax.shard_map(
        body,
        mesh=split,
        in_specs=(
            P(None, ROW, COL, None),
            P(None, None, ROW, COL, None),
            P(),
            P(),
            P(),
            P(),
            P(),
            P(),
            P(),
            P(),
            P(),
            P(None, ROW, COL, None),
            P(None, None, ROW, COL, None),
        ),
        out_specs=(
            P(None, ROW, COL, None),
            P(None, None, ROW, COL, None),
            P(None, ROW, COL, None),
            P(None, None, ROW, COL, None),
            P(),
            P(),
            P(),
            P(),
            P(),
            P(),
            P(),
            P(),
        ),
        check_vma=False,
    )
```

```python
import functools

import jax
import jax.numpy as jnp
from jax import lax
from jax.experimental import pallas as pl
from jax.experimental.pallas import tpu as pltpu
from jax.sharding import PartitionSpec as P

TASKS = 2
CONVS = 3
DOMAINS = 2
CORES = 2
REP = 4

EPSILON = 1e-05
HIGHEST = lax.Precision.HIGHEST
BOTH = ("row", "col")


class Place:
    def __init__(self):
        self.rows, self.cols = lax.axis_size("row"), lax.axis_size("col")
        self.groups = self.cols // REP
        self.mirror = 2 if self.groups == 2 else 0
        self.row, self.col = lax.axis_index("row"), lax.axis_index("col")
        self.group, self.rep = self.col // REP, self.col % REP
        self.block = self.rep ^ (self.mirror * (self.group % 2))

    def across(self, k):
        return (k * REP) ^ (self.mirror if k % 2 else 0)

    def swap(self, value, row_bits, col_bits):
        pairs = [
            (i, ((i // self.cols) ^ row_bits) * self.cols + ((i % self.cols) ^ col_bits))
            for i in range(self.rows * self.cols)
        ]
        return lax.ppermute(value, BOTH, pairs)

    def stages(self):
        bits = []
        k = 2
        while k < self.rows:
            bits.append((k, 0))
            k *= 2
        k = 1
        while k < self.groups:
            bits.append((0, self.across(k)))
            k *= 2
        steps = [[(1, 0)]]
        for i in range(0, len(bits), 2):
            pair = bits[i : i + 2]
            if len(pair) == 2:
                (a, b), (c, d) = pair
                pair = [(a, b), (c, d), (a ^ c, b ^ d)]
            steps.append(pair)
        return steps

    def gather(self, tile, axis):
        width = tile.shape[axis]
        shape = list(tile.shape)
        shape[axis] = width * REP
        whole = jnp.zeros(shape, tile.dtype)
        for k in range(REP):
            piece = tile if k == 0 else self.swap(tile, 0, k)
            whole = lax.dynamic_update_slice_in_dim(whole, piece, (self.rep ^ k) * width, axis)
        return whole

    def own(self, tile, axis, extra=0):
        width = (tile.shape[axis] - extra) // REP
        return lax.dynamic_slice_in_dim(tile, self.rep * width, width + extra, axis)

    def halo(self, tiles, pads):
        def edges(dim):
            low, high = [], []
            for tile, pad in zip(tiles, pads):
                axis = tile.ndim - 4 + dim
                length = tile.shape[axis]
                low.append(lax.slice_in_dim(tile, 0, pad, axis=axis))
                high.append(lax.slice_in_dim(tile, length - pad, length, axis=axis))
            shapes = [t.shape for t in low]
            if len(tiles) == 1:
                return low[0], high[0], lambda whole: [whole]

            def join(pieces):
                return jnp.concatenate([p.reshape(-1, *p.shape[-2:]) for p in pieces])

            def split(whole):
                pieces, at = [], 0
                for shape in shapes:
                    count = 1
                    for s in shape[:-2]:
                        count *= s
                    pieces.append(whole[at : at + count].reshape(shape))
                    at += count
                return pieces

            return join(low), join(high), split

        def attach(before, after, split, dim):
            return [
                jnp.concatenate([b, tile, a], axis=tile.ndim - 4 + dim)
                for b, tile, a in zip(split(before), tiles, split(after))
            ]

        low, high, split = edges(0)
        even = self.row % 2 == 0
        near = lax.ppermute(
            jnp.where(even, high, low), "row", [(i, i ^ 1) for i in range(self.rows)]
        )
        pairs = []
        for i in range(1, self.rows - 1, 2):
            pairs += [(i, i + 1), (i + 1, i)]
        far = lax.ppermute(jnp.where(even, low, high), "row", pairs)
        tiles = attach(jnp.where(even, far, near), jnp.where(even, near, far), split, 0)

        low, high, split = edges(1)
        even = self.group % 2 == 0
        near = self.swap(jnp.where(even, high, low), 0, self.across(1))
        far = jnp.zeros_like(near)
        if self.groups > 2:
            pairs = []
            for i in range(self.cols - REP):
                if (i // REP) % 2:
                    pairs += [(i, i + REP), (i + REP, i)]
            far = lax.ppermute(jnp.where(even, low, high), "col", pairs)
        return attach(jnp.where(even, far, near), jnp.where(even, near, far), split, 1)

    def inside(self, height, breadth, pad):
        rows = self.row * height + jnp.arange(height + 2 * pad) - pad
        cols = self.group * breadth + jnp.arange(breadth + 2 * pad) - pad
        return (
            ((rows >= 0) & (rows < height * self.rows))[:, None]
            & ((cols >= 0) & (cols < breadth * self.groups))[None, :]
        )[:, :, None, None]

    def scatter(self, parts):
        m, rows, c = parts.shape
        per = rows // (self.rows * self.groups)
        halves = self.rows // CORES
        parts = parts.reshape(m, halves, CORES, self.groups, per, c)
        core, half = self.row % CORES, self.row // CORES

        def pick(value, index, axis):
            return lax.dynamic_index_in_dim(value, index, axis, keepdims=False)

        other = self.swap(pick(parts, 1 - core, 2).astype(jnp.bfloat16), 1, 0)
        parts = pick(parts, core, 2) + other.astype(jnp.float32)
        got = []
        for a in range(halves):
            for b in range(self.groups):
                piece = pick(pick(parts, half ^ a, 1), self.group ^ b, 1)
                if a or b:
                    piece = self.swap(piece.astype(jnp.bfloat16), a * CORES, self.across(b))
                got.append(piece.astype(jnp.float32))
        return tree_sum(got).astype(jnp.bfloat16)


def tree_sum(values):
    while len(values) > 1:
        values = [a + b for a, b in zip(values[::2], values[1::2])]
    return values[0]


def total_stats(place, average, squares, number):
    for step in place.stages():
        own = jnp.stack([average, squares])
        both = [own] + [place.swap(own, *bits) for bits in step]
        averages = [b[0] for b in both]
        average = tree_sum(averages) * (1.0 / len(both))
        squares = tree_sum([b[1] for b in both]) + number * tree_sum(
            [(a - average) * (a - average) for a in averages]
        )
        number = number * len(both)
    return average, squares / number


def total_sums(place, value):
    for step in place.stages():
        value = tree_sum([value] + [place.swap(value, *bits) for bits in step])
    return value


def inner(tile):
    return tile[1:-1, 1:-1]


def convolve(padded, kernel):
    return lax.conv_general_dilated(
        padded,
        kernel,
        (1, 1),
        "VALID",
        dimension_numbers=("HWNC", "HWIO", "HWNC"),
        preferred_element_type=jnp.float32,
    )


def convolve_back(padded_grad, kernel):
    return lax.conv_general_dilated(
        padded_grad,
        jnp.flip(kernel, (0, 1)),
        (1, 1),
        "VALID",
        dimension_numbers=("HWNC", "HWOI", "HWNC"),
        preferred_element_type=jnp.float32,
    )


def project(values, weight):
    return jnp.einsum("hwnc,cd->hwnd", values, weight, preferred_element_type=jnp.float32)


def project_back(values, weight):
    return jnp.einsum("hwnd,cd->hwnc", values, weight, preferred_element_type=jnp.float32)


def silu_slope(pre_act):
    logistic = jax.nn.sigmoid(pre_act)
    return logistic * (1.0 + pre_act * (1.0 - logistic))


def domain_totals(member, values):
    return jnp.dot(member.T, jnp.sum(values, axis=(0, 1)), precision=HIGHEST)


def per_image(member, stats):
    return jnp.dot(member, stats, precision=HIGHEST)[None, None]


def local_stats(member, tile, number):
    average = domain_totals(member, tile) / number
    centered = tile - per_image(member, average)
    return average, domain_totals(member, centered * centered)


def forward_stats(place, member, tiles, number):
    local = [local_stats(member, tile, number) for tile in tiles]
    average, variance = total_stats(
        place, jnp.stack([a for a, _ in local]), jnp.stack([s for _, s in local]), number[None]
    )
    return average, lax.rsqrt(variance + EPSILON)


def backward_sums(place, member, pairs):
    local = [
        jnp.stack([domain_totals(member, dy), domain_totals(member, dy * form)])
        for dy, form in pairs
    ]
    return total_sums(place, jnp.stack(local))


def backward_input(member, dy, form, inverse, gain, sums, counts):
    plain = per_image(member, sums[0] / counts[:, None])
    cross = per_image(member, sums[1] / counts[:, None])
    return per_image(member, inverse) * gain * (dy - plain - form * cross)


def mean_pool(values):
    h, w, n, c = values.shape
    return jnp.mean(values.reshape(h // 2, 2, w // 2, 2, n, c), axis=(1, 3))


def mean_pool_back(grad_out):
    h, w, n, c = grad_out.shape
    spread = jnp.broadcast_to(
        0.25 * grad_out[:, None, :, None].astype(jnp.float32), (h, 2, w, 2, n, c)
    )
    return spread.reshape(2 * h, 2 * w, n, c)


def kernel_part(act, grads):
    part = lax.conv_general_dilated(
        act,
        grads,
        (1, 1),
        "VALID",
        dimension_numbers=("HWCN", "HWIO", "HWNC"),
        preferred_element_type=jnp.float32,
    )
    return part.reshape(-1, *part.shape[2:])


def matrix_part(act, grads):
    return jnp.einsum("hwnc,hwnd->cd", act, grads, preferred_element_type=jnp.float32)[None]


def spread_kernel(groups, *refs):
    *sources, target = refs
    for g, source in enumerate(sources):
        rows, _, _, _, per, _ = source.shape
        for r in range(rows):
            at = (r * groups + g) * per
            target[:, at : at + per, :] = source[r, 0, 0].astype(jnp.float32)


def spread(place, gathered, start, count, step):
    rows, groups, _, _, per, c = gathered.shape
    block = rows * groups * per

    def source(g):
        return pl.BlockSpec(
            (rows, 1, 1, step, per, c),
            lambda i, b: (0, g, b ^ (place.mirror * (g % 2)), start // step + i, 0, 0),
        )

    return pl.pallas_call(
        functools.partial(spread_kernel, groups),
        out_shape=jax.ShapeDtypeStruct((count, REP * block, c), jnp.float32),
        grid=(count // step, REP),
        in_specs=[source(g) for g in range(groups)],
        out_specs=pl.BlockSpec((step, block, c), lambda i, b: (i, b, 0)),
        compiler_params=pltpu.CompilerParams(vmem_limit_bytes=32 * 1024 * 1024),
        cost_estimate=pl.CostEstimate(
            flops=0, bytes_accessed=6 * count * REP * block * c, transcendentals=0
        ),
        name="spread",
    )(*([gathered] * groups))


def gather_rows(place, chunk):
    whole = lax.all_gather(chunk, BOTH)
    return whole.reshape(place.rows, place.groups, REP, *chunk.shape)


def body(
    features,
    priors,
    domain,
    shared_w,
    shared_gain,
    shared_bias,
    first_w,
    second_w,
    task_conv,
    task_gain,
    task_bias,
    shared_cot,
    task_cot,
):
    place = Place()
    images, height, breadth, channels = features.shape
    wide = breadth * REP
    member = (domain[:, None] == jnp.arange(DOMAINS, dtype=jnp.int32)[None, :]).astype(jnp.float32)
    named = jnp.sum(member, axis=0)[:, None]
    number = named * (height * wide)
    counts = named[:, 0] * (height * wide * place.rows * place.groups)
    inside = place.inside(height, wide, 1)

    def only_inside(tile):
        return jnp.where(inside, tile, 0.0).astype(jnp.bfloat16)

    def mine(act):
        size = channels // REP
        return lax.dynamic_slice_in_dim(act, place.block * size, size, act.ndim - 1)

    features = place.gather(features.transpose(1, 2, 0, 3), 1)
    (features,) = place.halo([features], [2])
    priors = priors.transpose(0, 2, 3, 1, 4)
    cots = jnp.concatenate([task_cot, shared_cot[None]]).transpose(0, 2, 3, 1, 4)
    half_h, half_w = height // 2, breadth // 2
    small = TASKS * height
    rest = jnp.concatenate(
        [
            priors.reshape(small, breadth, images, channels),
            cots.reshape(-1, breadth, images, channels),
        ]
    )
    rest = place.gather(rest[:, None], 1)
    priors = rest[:small].reshape(TASKS, height, REP * breadth, images, channels)
    priors = rest[:small].reshape(TASKS, height, wide, images, channels)
    cots = (
        rest[small:]
        .reshape(TASKS + 1, half_h // 2, REP, 2, half_w, images, channels)
        .transpose(0, 1, 3, 2, 4, 5, 6)
        .reshape(TASKS + 1, half_h, REP * half_w, images, channels)
    )
    task_cot, shared_cot = cots[:TASKS], cots[TASKS]
    priors, shared_cot = place.halo([priors, shared_cot], [1, 1])

    def apply_norm(tile, average, inverse, gain, bias):
        form = (tile - per_image(member, average)) * per_image(member, inverse)
        return form, form * gain + bias

    product = convolve(features, shared_w[0])
    average, inverse = forward_stats(place, member, [inner(product)], number)
    inverse1 = inverse[0]
    form1, normed1 = apply_norm(product, average[0], inverse1, shared_gain[0], shared_bias[0])
    act1 = only_inside(jax.nn.silu(normed1))

    product = convolve(act1, shared_w[1])
    hidden = [
        project(act1, first_w[t, :channels]) + project(priors[t], first_w[t, channels:])
        for t in range(TASKS)
    ]
    average, inverse = forward_stats(
        place, member, [product] + [inner(h) for h in hidden], number
    )
    inverse2, inverse_h = inverse[0], inverse[1:]
    form2, normed2 = apply_norm(product, average[0], inverse2, shared_gain[1], shared_bias[1])
    (act2,) = place.halo([jax.nn.silu(normed2).astype(jnp.bfloat16)], [2])
    form_h, normed_h, hidden_act = [], [], []
    for t in range(TASKS):
        form, normed = apply_norm(
            hidden[t], average[1 + t], inverse_h[t], task_gain[t, 0], task_bias[t, 0]
        )
        form_h.append(form)
        normed_h.append(normed)
        hidden_act.append(jax.nn.silu(normed).astype(jnp.bfloat16))

    product = convolve(act2, shared_w[2])
    gate = [project(hidden_act[t], second_w[t]) for t in range(TASKS)]
    average, inverse = forward_stats(
        place, member, [inner(product)] + [inner(g) for g in gate], number
    )
    inverse3, inverse_g = inverse[0], inverse[1:]
    form3, normed3 = apply_norm(product, average[0], inverse3, shared_gain[2], shared_bias[2])
    last = jax.nn.silu(normed3)
    shared_out = mean_pool(place.own(inner(last), 1)).astype(jnp.bfloat16)
    form_g, attention, masked = [], [], []
    for t in range(TASKS):
        form, normed = apply_norm(
            gate[t], average[1 + t], inverse_g[t], task_gain[t, 1], task_bias[t, 1]
        )
        form_g.append(form)
        attention.append(jax.nn.sigmoid(normed))
        masked.append(only_inside(attention[t] * last))

    refined = [convolve(masked[t], task_conv[t]) for t in range(TASKS)]
    average, inverse_r = forward_stats(place, member, refined, number)
    form_r, dy_r, task_outs = [], [], []
    for t in range(TASKS):
        form, normed = apply_norm(
            refined[t], average[t], inverse_r[t], task_gain[t, 2], task_bias[t, 2]
        )
        form_r.append(form)
        task_outs.append(mean_pool(place.own(jax.nn.silu(normed), 1)).astype(jnp.bfloat16))
        dy_r.append(mean_pool_back(task_cot[t]) * silu_slope(normed))

    sums_r = backward_sums(place, member, [(dy_r[t], form_r[t]) for t in range(TASKS)])
    dv_r = jnp.stack(
        [
            backward_input(
                member, dy_r[t], form_r[t], inverse_r[t], task_gain[t, 2], sums_r[t], counts
            ).astype(jnp.bfloat16)
            for t in range(TASKS)
        ]
    )
    task_parts = [kernel_part(mine(masked[t]), dv_r[t]) for t in range(TASKS)]
    task_rows = gather_rows(place, place.scatter(jnp.concatenate(task_parts)))
    (dv_r,) = place.halo([dv_r], [2])
    grad_masked = [convolve_back(dv_r[t], task_conv[t]) for t in range(TASKS)]

    grad_last = inner(mean_pool_back(shared_cot))
    dy_g = []
    for t in range(TASKS):
        grad_last = grad_last + grad_masked[t] * attention[t]
        dy_g.append(grad_masked[t] * last * attention[t] * (1.0 - attention[t]))
    dy3 = grad_last * silu_slope(normed3)
    sums = backward_sums(
        place,
        member,
        [(inner(dy3), inner(form3))] + [(inner(dy_g[t]), inner(form_g[t])) for t in range(TASKS)],
    )
    sums3, sums_g = sums[0], sums[1:]
    dv3 = only_inside(
        backward_input(member, dy3, form3, inverse3, shared_gain[2], sums3, counts)
    )
    dv_g = [
        backward_input(
            member, dy_g[t], form_g[t], inverse_g[t], task_gain[t, 1], sums_g[t], counts
        ).astype(jnp.bfloat16)
        for t in range(TASKS)
    ]
    grad_act2 = convolve_back(dv3, shared_w[2])
    parts3 = [kernel_part(mine(inner(act2)), inner(dv3))]
    parts_s = [matrix_part(mine(inner(hidden_act[t])), inner(dv_g[t])) for t in range(TASKS)]

    dy2 = grad_act2 * silu_slope(normed2)
    dy_h = [project_back(dv_g[t], second_w[t]) * silu_slope(normed_h[t]) for t in range(TASKS)]
    sums = backward_sums(
        place,
        member,
        [(dy2, form2)] + [(inner(dy_h[t]), inner(form_h[t])) for t in range(TASKS)],
    )
    sums2, sums_h = sums[0], sums[1:]
    dv2 = backward_input(
        member, dy2, form2, inverse2, shared_gain[1], sums2, counts
    ).astype(jnp.bfloat16)
    parts2 = [kernel_part(mine(act1), dv2)]
    (dv2,) = place.halo([dv2], [2])
    dv_h = [
        backward_input(
            member, dy_h[t], form_h[t], inverse_h[t], task_gain[t, 0], sums_h[t], counts
        ).astype(jnp.bfloat16)
        for t in range(TASKS)
    ]
    grad_act1 = convolve_back(dv2, shared_w[1])
    for t in range(TASKS):
        grad_act1 = grad_act1 + project_back(dv_h[t], first_w[t, :channels])
    parts_f = []
    for t in range(TASKS):
        parts_f.append(matrix_part(mine(inner(act1)), inner(dv_h[t])))
        parts_f.append(matrix_part(mine(inner(priors[t])), inner(dv_h[t])))

    dy1 = grad_act1 * silu_slope(normed1)
    sums1 = backward_sums(place, member, [(inner(dy1), inner(form1))])[0]
    dv1 = only_inside(
        backward_input(member, dy1, form1, inverse1, shared_gain[0], sums1, counts)
    )
    parts1 = [kernel_part(mine(inner(features)), inner(dv1))]
    grad_features = convolve_back(place.own(dv1, 1, 2), shared_w[0])
    grad_priors = [
        project_back(place.own(inner(dv_h[t]), 1), first_w[t, channels:]) for t in range(TASKS)
    ]

    chunk = jnp.concatenate(
        [
            place.scatter(jnp.concatenate(parts_f + parts_s)),
            place.scatter(jnp.concatenate(parts1)),
            place.scatter(jnp.concatenate(parts2)),
            place.scatter(jnp.concatenate(parts3)),
        ]
    )
    rest_rows = gather_rows(place, chunk)
    taps = 9
    grad_first = spread(place, rest_rows, 0, 2 * TASKS, 2)
    grad_second = spread(place, rest_rows, 2 * TASKS, TASKS, 2)
    grad_shared = spread(place, rest_rows, 3 * TASKS, CONVS * taps, 3)
    grad_task = spread(place, task_rows, 0, TASKS * taps, 3)

    shared_sums = jnp.sum(jnp.stack([sums1, sums2, sums3]), axis=2)
    task_sums = jnp.sum(jnp.stack([sums_h, sums_g, sums_r], axis=1), axis=3)

    def images_first(tile):
        return tile.transpose(2, 0, 1, 3)

    return (
        images_first(shared_out),
        jnp.stack([images_first(o) for o in task_outs]),
        images_first(grad_features),
        jnp.stack([images_first(g) for g in grad_priors]),
        grad_shared.reshape(shared_w.shape),
        shared_sums[:, 1],
        shared_sums[:, 0],
        grad_first.reshape(first_w.shape),
        grad_second.reshape(second_w.shape),
        grad_task.reshape(task_conv.shape),
        task_sums[:, :, 1],
        task_sums[:, :, 0],
    )


def solution(mesh):
    return jax.shard_map(
        body,
        mesh=mesh,
        in_specs=(
            P(None, "row", "col", None),
            P(None, None, "row", "col", None),
            P(),
            P(),
            P(),
            P(),
            P(),
            P(),
            P(),
            P(),
            P(),
            P(None, "row", "col", None),
            P(None, None, "row", "col", None),
        ),
        out_specs=(
            P(None, "row", "col", None),
            P(None, None, "row", "col", None),
            P(None, "row", "col", None),
            P(None, None, "row", "col", None),
            P(),
            P(),
            P(),
            P(),
            P(),
            P(),
            P(),
            P(),
        ),
        check_vma=False,
    )
```

```python
import functools

import jax
import jax.numpy as jnp
from jax import lax
from jax.experimental import pallas as pl
from jax.experimental.pallas import tpu as pltpu
from jax.sharding import PartitionSpec as P

TASKS = 2
CONVS = 3
DOMAINS = 2
CORES = 2
REP = 4
TAPS = 9
LANES = 128
ROWS, WIDTH = 16, 256
PAD = 16

EPSILON = 1e-05
BOTH = ("row", "col")
MIB = 1024 * 1024


class Place:
    def __init__(self):
        self.rows, self.cols = lax.axis_size("row"), lax.axis_size("col")
        self.groups = self.cols // REP
        self.row, self.col = lax.axis_index("row"), lax.axis_index("col")
        self.group, self.rep = self.col // REP, self.col % REP

    def swap(self, value, row_bits, col_bits):
        pairs = [
            (i, ((i // self.cols) ^ row_bits) * self.cols + ((i % self.cols) ^ col_bits))
            for i in range(self.rows * self.cols)
        ]
        return lax.ppermute(value, BOTH, pairs)

    def stages(self):
        bits = []
        k = 2
        while k < self.rows:
            bits.append((k, 0))
            k *= 2
        k = 1
        while k < self.groups:
            bits.append((0, k * REP))
            k *= 2
        steps = [[(1, 0)]]
        for i in range(0, len(bits), 2):
            pair = bits[i : i + 2]
            if len(pair) == 2:
                (a, b), (c, d) = pair
                pair = [(a, b), (c, d), (a ^ c, b ^ d)]
            steps.append(pair)
        return steps

    def pieces(self, tile):
        return [tile] + [self.swap(tile, 0, k) for k in range(1, REP)]

    def gather(self, tile, axis):
        return self.join(self.pieces(tile), axis)

    def join(self, pieces, axis):
        bit = 1
        while bit < REP:
            odd = (self.rep & bit) != 0
            pieces = [jnp.where(odd, pieces[j ^ bit], pieces[j]) for j in range(REP)]
            bit *= 2
        return jnp.concatenate(pieces, axis=axis)

    def halo_rows(self, low, high):
        even = self.row % 2 == 0
        near = lax.ppermute(
            jnp.where(even, high, low), "row", [(i, i ^ 1) for i in range(self.rows)]
        )
        pairs = []
        for i in range(1, self.rows - 1, 2):
            pairs += [(i, i + 1), (i + 1, i)]
        far = lax.ppermute(jnp.where(even, low, high), "row", pairs)
        return jnp.where(even, far, near), jnp.where(even, near, far)

    def halo_cols(self, low, high):
        even = self.group % 2 == 0
        near = self.swap(jnp.where(even, high, low), 0, REP)
        far = jnp.zeros_like(near)
        if self.groups > 2:
            pairs = []
            for i in range(self.cols - REP):
                if (i // REP) % 2:
                    pairs += [(i, i + REP), (i + REP, i)]
            far = lax.ppermute(jnp.where(even, low, high), "col", pairs)
        return jnp.where(even, far, near), jnp.where(even, near, far)

    def halo(self, tiles, pad, images):
        size = pad * images
        count = len(tiles)

        def columns(tiles):
            def edge(at):
                edges = [t[..., at, :].reshape(-1, size, t.shape[-1]) for t in tiles]
                extra = -(size * count) % 8
                if extra:
                    edges.append(jnp.zeros((edges[0].shape[0], extra, edges[0].shape[-1]), edges[0].dtype))
                edges = jnp.concatenate(edges, axis=1)
                return edges.reshape(-1, edges.shape[-1])

            got = self.halo_cols(edge(slice(0, size)), edge(slice(-size, None)))
            shape = tiles[0].shape
            width = -(-(size * count) // 8) * 8
            got = [x.reshape(-1, width, x.shape[-1]) for x in got]
            return [
                [x[:, t * size : (t + 1) * size].reshape(*shape[:-2], size, shape[-1]) for x in got]
                for t in range(count)
            ]

        sides = columns(tiles)
        ends = self.halo_rows(
            jnp.stack([t[..., :pad, :, :] for t in tiles]),
            jnp.stack([t[..., -pad:, :, :] for t in tiles]),
        )
        ends = [(ends[0][t], ends[1][t]) for t in range(count)]
        corners = columns([jnp.concatenate(e, axis=-3) for e in ends])
        whole = []
        for tile, (above, below), side, corner in zip(tiles, ends, sides, corners):
            tile = jnp.concatenate([above, tile, below], axis=-3)
            before, after = (
                jnp.concatenate([x[..., :pad, :, :], y, x[..., pad:, :, :]], axis=-3)
                for x, y in zip(corner, side)
            )
            fill = jnp.zeros((*tile.shape[:-2], pad * PAD - 2 * size, tile.shape[-1]), tile.dtype)
            whole.append(jnp.concatenate([before, tile, after, fill], axis=-2))
        return whole

    def scatter_core(self, parts):
        m, rows, c = parts.shape
        per = rows // (self.rows * self.groups)
        parts = parts.reshape(m, self.rows // CORES, CORES, self.groups, per, c)
        core = self.row % CORES
        other = lax.dynamic_index_in_dim(parts, 1 - core, 2, keepdims=False)
        other = self.swap(other.astype(jnp.bfloat16), 1, 0)
        mine = lax.dynamic_index_in_dim(parts, core, 2, keepdims=False)
        return mine + other.astype(jnp.float32)

    def scatter_chips(self, parts):
        halves = self.rows // CORES
        cut = parts.shape[0] * 2 // 3

        def along_row(parts, axis=1):
            half = self.row // CORES
            got = []
            for a in range(halves):
                piece = lax.dynamic_index_in_dim(parts, half ^ a, axis, keepdims=False)
                if a:
                    piece = self.swap(piece.astype(jnp.bfloat16), a * CORES, 0)
                got.append(piece.astype(jnp.float32))
            return tree_sum(got)

        def along_col(parts, axis):
            got = []
            for b in range(self.groups):
                piece = lax.dynamic_index_in_dim(parts, self.group ^ b, axis, keepdims=False)
                if b:
                    piece = self.swap(piece.astype(jnp.bfloat16), 0, b * REP)
                got.append(piece.astype(jnp.float32))
            return tree_sum(got)

        first, last = along_row(parts[:cut]), along_col(parts[cut:], 2)
        first, last = lax.optimization_barrier((first, last))
        first, last = along_col(first, 1), along_row(last)
        return jnp.concatenate([first, last]).astype(jnp.bfloat16)


def tree_sum(values):
    while len(values) > 1:
        values = [a + b for a, b in zip(values[::2], values[1::2])]
    return values[0]


def total_stats(place, local, number):
    for step in place.stages():
        both = [local] + [place.swap(local, *bits) for bits in step]
        averages = [b[0] for b in both]
        average = tree_sum(averages) * (1.0 / len(both))
        squares = tree_sum([b[1] for b in both]) + number * tree_sum(
            [(a - average) * (a - average) for a in averages]
        )
        local = jnp.stack([average, squares])
        number = number * len(both)
    return jnp.stack([local[0], local[1] / number])


def total_sums(place, value):
    for step in place.stages():
        value = tree_sum([value] + [place.swap(value, *bits) for bits in step])
    return value


def sweep(rows, c, step):
    for lane in range(0, c, WIDTH):

        @pl.loop(0, rows // ROWS)
        def block(i):
            step(pl.ds(pl.multiple_of(i * ROWS, ROWS), ROWS), slice(lane, lane + WIDTH))


def own_lines(tile_ref):
    h = tile_ref.shape[0]
    border = (h - 8) // 2
    return border, h - border


def wide(column):
    return jnp.broadcast_to(column, (column.shape[0], WIDTH))


class Norm:
    def __init__(self, sel_ref, stat_ref, gb_ref, i, at):
        rows, self.lanes = at
        self.first = wide(sel_ref[rows, 0:1]) > 0.5
        self.average = self.by_row(stat_ref[0, i, :, self.lanes])
        self.inverse = self.by_row(lax.rsqrt(stat_ref[1, i, :, self.lanes] + EPSILON))
        self.gain = gb_ref[i, 0:1, self.lanes]
        self.half_gain, self.half_bias = 0.5 * self.gain, 0.5 * gb_ref[i, 1:2, self.lanes]

    def by_row(self, pair):
        return jnp.where(self.first, pair[0:1], pair[1:2])

    def form(self, value):
        return (value - self.average) * self.inverse

    def half(self, form):
        return form * self.half_gain + self.half_bias

    def fold(self):
        self.times = self.inverse * self.half_gain
        self.plus = self.half_bias - self.average * self.times
        return self

    def __call__(self, value):
        return value * self.times + self.plus

    def set_sums(self, sums_ref, scal_ref, i):
        plain, cross = (
            self.by_row(
                jnp.concatenate(
                    [sums_ref[i, j, k : k + 1, self.lanes] * scal_ref[2 + k] for k in range(DOMAINS)]
                )
            )
            for j in range(2)
        )
        self.scale = self.inverse * self.gain
        self.plain, self.cross = plain, cross

    def back(self, dy, value):
        return self.scale * (dy - self.plain - self.form(value) * self.cross)


def sigmoid(t):
    return 0.5 * jnp.tanh(t) + 0.5


def silu(t):
    return t + t * jnp.tanh(t)


def silu_slope(t, h):
    return (0.5 + 0.5 * h) * (1.0 + t * (1.0 - h))


def slope(t):
    return silu_slope(t, jnp.tanh(t))


def seen(sel_ref, scal_ref, rows, lines):
    column = wide(sel_ref[rows, 3:4])
    return [column * scal_ref[4]] + [column] * (lines - 2) + [column * scal_ref[5]]


def add_by_domain(sel_ref, rows, values, out, lanes):
    for k in range(DOMAINS):
        out[k : k + 1, lanes] += jnp.sum(
            values * wide(sel_ref[rows, 1 + k : 2 + k]), axis=0, keepdims=True
        )


def local_stats(tile_ref, sel_ref, scal_ref, out_ref, i):
    _, r, c = tile_ref.shape
    lines = range(*own_lines(tile_ref))
    out_ref[:, i] = jnp.zeros((2, DOMAINS, c), jnp.float32)

    def total(rows, lanes):
        value = tree_sum([tile_ref[h, rows, lanes] for h in lines])
        add_by_domain(sel_ref, rows, value, out_ref.at[0, i], lanes)

    sweep(r, c, total)
    for k in range(DOMAINS):
        out_ref[0, i, k : k + 1] = out_ref[0, i, k : k + 1] * scal_ref[k]

    def square(rows, lanes):
        average = jnp.where(
            wide(sel_ref[rows, 0:1]) > 0.5, out_ref[0, i, 0:1, lanes], out_ref[0, i, 1:2, lanes]
        )
        apart = [tile_ref[h, rows, lanes] - average for h in lines]
        add_by_domain(sel_ref, rows, tree_sum([a * a for a in apart]), out_ref.at[1, i], lanes)

    sweep(r, c, square)


def fetch(w_ref, wv_ref, sem, start, back=False):
    c = w_ref.shape[-1]
    copies = []
    for t in range(TAPS):
        part = pl.ds((t % 3) * c, c)
        if back:
            source, target = w_ref.at[start + TAPS - 1 - t], wv_ref.at[t // 3, :, part]
        else:
            source, target = w_ref.at[start + t], wv_ref.at[t // 3, part, :]
        copies.append(pltpu.make_async_copy(source, target, sem.at[t]))
        copies[-1].start()
    return copies


def convolve(x_ref, xs_ref, wv_ref, copies, o_ref, images, back=False):
    hp, rp, c = x_ref.shape
    r = rp - PAD
    m = (hp - 2) * r
    for b in range(3):
        xs_ref[:, b * c : (b + 1) * c] = x_ref[:, b * images : b * images + r, :].reshape(hp * r, c)
    for a in range(3):
        for b in range(3):
            copies[3 * a + b].wait()
        part = lax.dot_general(
            xs_ref[a * r : a * r + m, :],
            wv_ref[a],
            (((1,), (1 if back else 0,)), ((), ())),
            preferred_element_type=jnp.float32,
        ).reshape(o_ref.shape)
        o_ref[...] = part if a == 0 else o_ref[...] + part


def flat(ref):
    h, r, c = ref.shape
    return ref[...].reshape(h * r, c)


def matmul(a, b):
    return jnp.dot(a, b, preferred_element_type=jnp.float32)


def matmul_back(a, b):
    return lax.dot_general(a, b, (((1,), (1,)), ((), ())), preferred_element_type=jnp.float32)


def first_kernel(images, tap, x_ref, w_ref, sel_ref, scal_ref, p_ref, st_ref, xs_ref, wv_ref, sem):
    copies = fetch(w_ref, wv_ref, sem, tap)
    convolve(x_ref, xs_ref, wv_ref, copies, p_ref, images)
    local_stats(p_ref, sel_ref, scal_ref, st_ref, 0)


def second_kernel(
    images, p1_ref, w_ref, st1_ref, gb_ref, sel_ref, sel0_ref, scal_ref,
    act_ref, p2_ref, st_ref, xs_ref, wv_ref, sem,
):
    copies = fetch(w_ref, wv_ref, sem, TAPS)
    lines, r, c = p1_ref.shape

    def activate(rows, lanes):
        norm = Norm(sel_ref, st1_ref, gb_ref, 0, (rows, lanes)).fold()
        for h, inside in enumerate(seen(sel_ref, scal_ref, rows, lines)):
            act_ref[h, rows, lanes] = (silu(norm(p1_ref[h, rows, lanes])) * inside).astype(
                jnp.bfloat16
            )

    sweep(r, c, activate)
    convolve(act_ref, xs_ref, wv_ref, copies, p2_ref, images)
    local_stats(p2_ref, sel0_ref, scal_ref, st_ref, 0)


def hidden_kernel(act_ref, pr_ref, fw_ref, sel_ref, scal_ref, h0_ref, h1_ref, st_ref):
    lines, r, c = act_ref.shape
    for t, h_ref in enumerate((h0_ref, h1_ref)):
        value = matmul(flat(act_ref), fw_ref[t, :c])
        h_ref[...] = (value + matmul(pr_ref[t].reshape(lines * r, c), fw_ref[t, c:])).reshape(
            h_ref.shape
        )
        local_stats(h_ref, sel_ref, scal_ref, st_ref, t)


def act_kernel(which, p_ref, st_ref, gb_ref, sel_ref, act_ref):
    lines, r, c = p_ref.shape

    def activate(rows, lanes):
        norm = Norm(sel_ref, st_ref, gb_ref, which, (rows, lanes)).fold()
        for h in range(lines):
            act_ref[h, rows, lanes] = silu(norm(p_ref[h, rows, lanes])).astype(jnp.bfloat16)

    sweep(r, c, activate)


def gate_kernel(
    h0_ref, h1_ref, sw_ref, st2_ref, gb_ref, sel_ref, scal_ref, a0_ref, a1_ref, g0_ref, g1_ref, st_ref,
):
    for t, (h_ref, a_ref, g_ref) in enumerate(((h0_ref, a0_ref, g0_ref), (h1_ref, a1_ref, g1_ref))):
        act_kernel(1 + t, h_ref, st2_ref, gb_ref, sel_ref, a_ref)
        g_ref[...] = matmul(flat(a_ref), sw_ref[t]).reshape(g_ref.shape)
        local_stats(g_ref, sel_ref, scal_ref, st_ref, t)


def fourth_kernel(
    images, p3_ref, g0_ref, g1_ref, w_ref, st3_ref, gb_ref, sel_ref, sel0_ref, scal_ref,
    m0_ref, m1_ref, r0_ref, r1_ref, st_ref, xs_ref, wv_ref, sem, wv2_ref, sem2,
):
    copies = [fetch(w_ref, wv_ref, sem, 0), fetch(w_ref, wv2_ref, sem2, TAPS)]
    lines, r, c = p3_ref.shape

    def mask(rows, lanes):
        norm = Norm(sel_ref, st3_ref, gb_ref, 0, (rows, lanes)).fold()
        gates = [
            Norm(sel_ref, st3_ref, gb_ref, 1 + t, (rows, lanes)).fold() for t in range(TASKS)
        ]
        for h, inside in enumerate(seen(sel_ref, scal_ref, rows, lines)):
            last = silu(norm(p3_ref[h, rows, lanes])) * inside
            for gate, g_ref, m_ref in zip(gates, (g0_ref, g1_ref), (m0_ref, m1_ref)):
                attention = sigmoid(gate(g_ref[h, rows, lanes]))
                m_ref[h, rows, lanes] = (attention * last).astype(jnp.bfloat16)

    sweep(r, c, mask)
    convolve(m0_ref, xs_ref, wv_ref, copies[0], r0_ref, images)
    convolve(m1_ref, xs_ref, wv2_ref, copies[1], r1_ref, images)
    local_stats(r0_ref, sel0_ref, scal_ref, st_ref, 0)
    local_stats(r1_ref, sel0_ref, scal_ref, st_ref, 1)


def store_sums(sel_ref, rows, lanes, out_ref, i, dys, forms):
    add_by_domain(sel_ref, rows, tree_sum(list(dys)), out_ref.at[i, 0], lanes)
    cross = tree_sum([dy * form for dy, form in zip(dys, forms)])
    add_by_domain(sel_ref, rows, cross, out_ref.at[i, 1], lanes)


def upsample(up_ref, low_ref, out_ref):
    for h in range(low_ref.shape[0]):
        out_ref[h] = matmul(up_ref[...], low_ref[h])


def refined_sums_kernel(
    r0_ref, r1_ref, c0_ref, c1_ref, up_ref, st_ref, gb_ref, sel_ref, out_ref, dy_ref, low_ref
):
    lines, r, c = r0_ref.shape
    out_ref[...] = jnp.zeros_like(out_ref)
    for t, (r_ref, c_ref) in enumerate(((r0_ref, c0_ref), (r1_ref, c1_ref))):
        upsample(up_ref, c_ref, low_ref)

        def sums(rows, lanes):
            norm = Norm(sel_ref, st_ref, gb_ref, t, (rows, lanes))
            dys, forms = [], []
            for h in range(lines):
                forms.append(norm.form(r_ref[h, rows, lanes]))
                dys.append(low_ref[h // 2, rows, lanes] * slope(norm.half(forms[-1])))
                dy_ref[t, h, rows, lanes] = dys[-1]
            store_sums(sel_ref, rows, lanes, out_ref, t, dys, forms)

        sweep(r, c, sums)


def refined_back_kernel(
    r0_ref, r1_ref, dy_ref, st_ref, gb_ref, sums_ref, sel_ref, scal_ref, dv0_ref, dv1_ref
):
    for t, (r_ref, dv_ref) in enumerate(((r0_ref, dv0_ref), (r1_ref, dv1_ref))):
        back_kernel(
            t, False, dy_ref.at[t], r_ref, st_ref, gb_ref, sums_ref, sel_ref, scal_ref, dv_ref
        )


def conv_back_kernel(images, start, x_ref, w_ref, o_ref, xs_ref, wv_ref, sem):
    copies = fetch(w_ref, wv_ref, sem, start, True)
    convolve(x_ref, xs_ref, wv_ref, copies, o_ref, images, True)


def masked_back_kernel(
    images, dv_ref, w_ref, grad_ref, p3_ref, g0_ref, g1_ref, cot_ref, up_ref, st3_ref, gb_ref,
    sel_ref, dy3_ref, dy0_ref, dy1_ref, sums_ref, xs_ref, wv_ref, sem, low_ref,
):
    copies = fetch(w_ref, wv_ref, sem, TAPS, True)
    convolve(dv_ref, xs_ref, wv_ref, copies, dy1_ref, images, True)
    lines, r, c = p3_ref.shape
    own = slice(*own_lines(p3_ref))
    upsample(up_ref, cot_ref, low_ref)
    sums_ref[...] = jnp.zeros_like(sums_ref)

    def step(rows, lanes):
        norm = Norm(sel_ref, st3_ref, gb_ref, 0, (rows, lanes))
        gates = [Norm(sel_ref, st3_ref, gb_ref, 1 + t, (rows, lanes)) for t in range(TASKS)]
        dys, forms = [[], [], []], [[], [], []]
        for h in range(lines):
            form = norm.form(p3_ref[h, rows, lanes])
            half = norm.half(form)
            tanh = jnp.tanh(half)
            last = half + half * tanh
            grad_last = low_ref[(h + 1) // 2, rows, lanes]
            for i, (gate, g_ref, from_ref, d_ref) in enumerate(
                zip(gates, (g0_ref, g1_ref), (grad_ref, dy1_ref), (dy0_ref, dy1_ref))
            ):
                gate_form = gate.form(g_ref[h, rows, lanes])
                attention = sigmoid(gate.half(gate_form))
                grad = from_ref[h, rows, lanes] * attention
                grad_last = grad_last + grad
                dy = grad * last * (1.0 - attention)
                d_ref[h, rows, lanes] = dy
                dys[1 + i].append(dy)
                forms[1 + i].append(gate_form)
            dy = grad_last * silu_slope(half, tanh)
            dy3_ref[h, rows, lanes] = dy
            dys[0].append(dy)
            forms[0].append(form)
        for i in range(3):
            store_sums(sel_ref, rows, lanes, sums_ref, i, dys[i][own], forms[i][own])

    sweep(r, c, step)


def slope_sums(which, out_at, grad_ref, add_ref, p_ref, st_ref, gb_ref, sel_ref, sums_ref):
    lines, r, c = p_ref.shape
    own = slice(*own_lines(p_ref))

    def step(rows, lanes):
        norm = Norm(sel_ref, st_ref, gb_ref, which, (rows, lanes))
        dys, forms = [], []
        for h in range(lines):
            form = norm.form(p_ref[h, rows, lanes])
            grad = grad_ref[h, rows, lanes]
            if add_ref is not None:
                grad = grad + add_ref[h, rows, lanes]
            dy = grad * slope(norm.half(form))
            grad_ref[h, rows, lanes] = dy
            dys.append(dy)
            forms.append(form)
        store_sums(sel_ref, rows, lanes, sums_ref, out_at, dys[own], forms[own])

    sweep(r, c, step)


def back_kernel(which, masked, dy_ref, p_ref, st_ref, gb_ref, sums_ref, sel_ref, scal_ref, dv_ref):
    lines, r, c = p_ref.shape

    def step(rows, lanes):
        norm = Norm(sel_ref, st_ref, gb_ref, which, (rows, lanes))
        norm.set_sums(sums_ref, scal_ref, which)
        inside = seen(sel_ref, scal_ref, rows, lines)
        for h in range(lines):
            dv = norm.back(dy_ref[h, rows, lanes], p_ref[h, rows, lanes])
            if masked:
                dv = dv * inside[h]
            dv_ref[h, rows, lanes] = dv.astype(jnp.bfloat16)

    sweep(r, c, step)


def third_back_kernel(
    images, dy3_ref, p3_ref, p2_ref, w_ref, st3_ref, gb3_ref, sums_ref, st2_ref, gb2_ref,
    sel_ref, sel0_ref, scal_ref, dv3_ref, dy2_ref, out_ref, xs_ref, wv_ref, sem,
):
    copies = fetch(w_ref, wv_ref, sem, 2 * TAPS, True)
    back_kernel(0, True, dy3_ref, p3_ref, st3_ref, gb3_ref, sums_ref, sel_ref, scal_ref, dv3_ref)
    convolve(dv3_ref, xs_ref, wv_ref, copies, dy2_ref, images, True)
    out_ref[...] = jnp.zeros_like(out_ref)
    slope_sums(0, 0, dy2_ref, None, p2_ref, st2_ref, gb2_ref, sel0_ref, out_ref)


def gate_back_kernel(
    dy0_ref, dy1_ref, g0_ref, g1_ref, h0_ref, h1_ref, sw_ref, st3_ref, gb3_ref, sums_ref,
    st2_ref, gb2_ref, sel_ref, scal_ref, dv0_ref, dv1_ref, dh0_ref, dh1_ref, out_ref,
):
    out_ref[...] = jnp.zeros_like(out_ref)
    for t, (dy_ref, g_ref, dv_ref, h_ref, dh_ref) in enumerate(
        (
            (dy0_ref, g0_ref, dv0_ref, h0_ref, dh0_ref),
            (dy1_ref, g1_ref, dv1_ref, h1_ref, dh1_ref),
        )
    ):
        back_kernel(
            1 + t, False, dy_ref, g_ref, st3_ref, gb3_ref, sums_ref, sel_ref, scal_ref, dv_ref
        )
        dh_ref[...] = matmul_back(flat(dv_ref), sw_ref[t]).reshape(dh_ref.shape)
        slope_sums(1 + t, t, dh_ref, None, h_ref, st2_ref, gb2_ref, sel_ref, out_ref)


def hidden_back_kernel(
    dyh0_ref, dyh1_ref, h0_ref, h1_ref, fw_ref, st_ref, gb_ref, sums_ref, sel_ref, scal_ref,
    dv0_ref, dv1_ref, grad_ref,
):
    _, _, c = h0_ref.shape
    for t, (dy_ref, h_ref, dv_ref) in enumerate(
        ((dyh0_ref, h0_ref, dv0_ref), (dyh1_ref, h1_ref, dv1_ref))
    ):
        back_kernel(1 + t, False, dy_ref, h_ref, st_ref, gb_ref, sums_ref, sel_ref, scal_ref, dv_ref)
        value = matmul_back(flat(dv_ref), fw_ref[t, :c]).reshape(grad_ref.shape)
        grad_ref[...] = value if t == 0 else grad_ref[...] + value


def second_back_kernel(
    images, dv2_ref, w_ref, add_ref, p1_ref, st_ref, gb_ref, sel_ref,
    dy_ref, sums_ref, xs_ref, wv_ref, sem,
):
    copies = fetch(w_ref, wv_ref, sem, TAPS, True)
    convolve(dv2_ref, xs_ref, wv_ref, copies, dy_ref, images, True)
    sums_ref[...] = jnp.zeros_like(sums_ref)
    slope_sums(0, 0, dy_ref, add_ref, p1_ref, st_ref, gb_ref, sel_ref, sums_ref)


def parts_kernel(plan, images, block_ref, *refs):
    *sources, out_ref, xs_ref = refs
    at = 0
    for x, g, conv in plan:
        x_ref, g_ref = sources[x], sources[g]
        border = (g_ref.shape[0] - 8) // 2
        cols = g_ref.shape[1] - border * PAD
        k = 8 * cols
        grad = g_ref[border : border + 8, border * images : border * images + cols, :]
        grad = grad.reshape(k, grad.shape[-1])
        border = (x_ref.shape[0] - 8) // 2
        taps = [(a, b) for a in (-1, 0, 1) for b in (-1, 0, 1)] if conv else [(0, 0)]
        for t, (a, b) in enumerate(taps):
            start = (border + b) * images
            xs_ref[:, t * LANES : (t + 1) * LANES] = x_ref[
                border + a : border + a + 8, start : start + cols, :
            ].reshape(k, LANES)
        size = len(taps) * LANES
        part = lax.dot_general(
            xs_ref[:, :size], grad, (((0,), (0,)), ((), ())), preferred_element_type=jnp.float32
        )
        out_ref[at : at + len(taps)] = part.reshape(len(taps), LANES, part.shape[-1])
        at += len(taps)


def parts(place, plan, images, acts, grads):
    c = grads[0].shape[-1]
    count = sum(TAPS if conv else 1 for _, _, conv in plan)

    def act_spec(x):
        return pl.BlockSpec((*x.shape[:2], LANES), lambda i, b: (0, 0, b[0]))

    def grad_spec(x):
        return pl.BlockSpec(x.shape, lambda i, b: (0, 0, 0))

    return pl.pallas_call(
        functools.partial(parts_kernel, plan, images),
        out_shape=jax.ShapeDtypeStruct((count, LANES, c), jnp.float32),
        grid_spec=pltpu.PrefetchScalarGridSpec(
            num_scalar_prefetch=1,
            grid=(1,),
            in_specs=[act_spec(x) for x in acts] + [grad_spec(x) for x in grads],
            out_specs=pl.BlockSpec((count, LANES, c), lambda i, b: (0, 0, 0)),
            scratch_shapes=[pltpu.VMEM((8 * 16 * images, TAPS * LANES), jnp.bfloat16)],
        ),
        compiler_params=pltpu.CompilerParams(vmem_limit_bytes=32 * MIB),
        name="parts",
    )(place.rep.astype(jnp.int32)[None], *acts, *grads)


def spread_kernel(groups, sources_per, *refs):
    sources, targets = refs[: groups * sources_per], refs[groups * sources_per :]
    at = 0
    places = [(target, i) for target in targets for i in range(target.shape[0])]
    for s in range(sources_per):
        for i in range(sources[0].shape[3]):
            target, m = places[s * sources[0].shape[3] + i]
            for g in range(groups):
                source = sources[s * groups + g]
                rows, _, _, _, per, _ = source.shape
                for r in range(rows):
                    at = (r * groups + g) * per
                    target[m, at : at + per, :] = source[r, 0, 0, i].astype(jnp.float32)


def spread(place, gathered, start, counts, step):
    rows, groups, _, _, per, c = gathered.shape
    block = rows * groups * per
    sources = 1 if len(counts) == 1 else sum(counts) // step

    def source(s, g):
        return pl.BlockSpec(
            (rows, 1, 1, step, per, c),
            lambda i, b: (0, g, b, start // step + s + i, 0, 0),
        )

    takes = [step] if len(counts) == 1 else counts
    return pl.pallas_call(
        functools.partial(spread_kernel, groups, sources),
        out_shape=[jax.ShapeDtypeStruct((n, REP * block, c), jnp.float32) for n in counts],
        grid=(sum(counts) // (step * sources), REP),
        in_specs=[source(s, g) for s in range(sources) for g in range(groups)],
        out_specs=[pl.BlockSpec((n, block, c), lambda i, b: (i, b, 0)) for n in takes],
        compiler_params=pltpu.CompilerParams(vmem_limit_bytes=58 * MIB),
        cost_estimate=pl.CostEstimate(
            flops=0, bytes_accessed=6 * sum(counts) * REP * block * c, transcendentals=0
        ),
        name="spread",
    )(*([gathered] * (groups * sources)))


def gather_rows(place, chunk):
    whole = lax.all_gather(chunk, BOTH)
    return whole.reshape(place.rows, place.groups, REP, *chunk.shape)


VMEM_SPEC = pl.BlockSpec(memory_space=pltpu.VMEM)
SMEM_SPEC = pl.BlockSpec(memory_space=pltpu.SMEM)
HBM_SPEC = pl.BlockSpec(memory_space=pltpu.HBM)


def call(kernel, name, ins, outs, shift=None, weights=0, back=False, extra=(), limit=32):
    specs = {"v": VMEM_SPEC, "s": SMEM_SPEC, "a": HBM_SPEC}
    c = outs[0][0][-1]
    scratch = []
    if shift:
        scratch.append(pltpu.VMEM(shift, jnp.bfloat16))
    for _ in range(weights):
        taps = (3, c, 3 * c) if back else (3, 3 * c, c)
        scratch += [pltpu.VMEM(taps, jnp.bfloat16), pltpu.SemaphoreType.DMA((TAPS,))]
    scratch += [pltpu.VMEM(e, jnp.float32) for e in extra]
    return pl.pallas_call(
        kernel,
        out_shape=[jax.ShapeDtypeStruct(*o) for o in outs],
        in_specs=[specs[k] for _, k in ins],
        out_specs=[VMEM_SPEC] * len(outs),
        scratch_shapes=scratch,
        compiler_params=pltpu.CompilerParams(vmem_limit_bytes=limit * MIB),
        name=name,
    )(*[a for a, _ in ins])


def body(
    features,
    priors,
    domain,
    shared_w,
    shared_gain,
    shared_bias,
    first_w,
    second_w,
    task_conv,
    task_gain,
    task_bias,
    shared_cot,
    task_cot,
):
    place = Place()
    images, height, breadth, c = features.shape
    wide = breadth * REP
    f32, bf16 = jnp.float32, jnp.bfloat16
    member = (domain[:, None] == jnp.arange(DOMAINS, dtype=jnp.int32)[None, :]).astype(f32)
    named = jnp.sum(member, axis=0)
    number = named * (height * wide)
    counts = number * (place.rows * place.groups)
    scal = jnp.concatenate(
        [
            1.0 / number,
            1.0 / counts,
            (place.row > 0).astype(f32)[None],
            (place.row < place.rows - 1).astype(f32)[None],
        ]
    )

    rows0, rows1, rows2 = wide * images, wide * images + PAD, wide * images + 2 * PAD
    tile0, tile1, tile2 = (
        (height, rows0, c), (height + 2, rows1, c), (height + 4, rows2, c),
    )
    shift1 = ((height + 2) * rows0, 3 * c)
    shift2 = ((height + 4) * rows1, 3 * c)

    def selectors(rows, border):
        r = jnp.arange(rows)
        w, image = r // images - border, r % images
        of = member[image]
        own = ((w >= 0) & (w < wide)).astype(f32)
        col = place.group * wide + w
        seen = (col >= 0) & (col < wide * place.groups) & (w < wide + border)
        table = [of[:, 0], of[:, 0] * own, of[:, 1] * own, seen.astype(f32)]
        return jnp.stack(table + [jnp.zeros_like(own)] * 4, axis=1)

    sel0, sel1 = selectors(rows0, 0), selectors(rows1, 1)
    gains = jnp.stack([shared_gain, shared_bias], axis=1)
    task_gains = jnp.stack([task_gain, task_bias], axis=2)
    gb1 = gains[0][None]
    gb2 = jnp.stack([gains[1], task_gains[0, 0], task_gains[1, 0]])
    gb3 = jnp.stack([gains[2], task_gains[0, 1], task_gains[1, 1]])
    gbr = task_gains[:, 2]
    shared_taps = shared_w.reshape(CONVS * TAPS, c, c)
    task_taps = task_conv.reshape(TASKS * TAPS, c, c)

    features = features.transpose(1, 2, 0, 3).reshape(height, breadth * images, c)
    (features,) = place.halo([place.gather(features, 1)], 2, images)
    priors = priors.transpose(0, 2, 3, 1, 4).reshape(TASKS, height, breadth * images, c)
    priors = place.pieces(priors)
    half_h, half_w = height // 2, breadth // 2

    def spreader(rows, border):
        r = jnp.arange(rows)
        source = (r // images + border) // 2 * images + r % images
        size = (REP * half_w) * images + border * PAD
        return (0.25 * (source[:, None] == jnp.arange(size)[None])).astype(bf16)

    up0, up1 = spreader(rows0, 0), spreader(rows1, 1)

    p1, local = call(
        functools.partial(first_kernel, images, 0), "first",
        [(features, "v"), (shared_taps, "a"), (sel1, "v"), (scal, "s")],
        [(tile1, f32), ((2, 1, DOMAINS, c), f32)],
        shift=shift2, weights=1, limit=46,
    )
    p1, priors = lax.optimization_barrier((p1, priors))
    (priors,) = place.halo([place.join(priors, 2)], 1, images)
    stats1 = total_stats(place, local, number[None, :, None])

    act1, p2, local = call(
        functools.partial(second_kernel, images), "second",
        [
            (p1, "v"), (shared_taps, "a"), (stats1, "v"), (gb1, "v"), (sel1, "v"), (sel0, "v"),
            (scal, "s"),
        ],
        [(tile1, bf16), (tile0, f32), ((2, 1, DOMAINS, c), f32)],
        shift=shift1, weights=1, limit=44,
    )
    h0, h1, local_h = call(
        hidden_kernel, "hidden",
        [(act1, "v"), (priors, "v"), (first_w, "v"), (sel1, "v"), (scal, "s")],
        [(tile1, f32), (tile1, f32), ((2, TASKS, DOMAINS, c), f32)], limit=12,
    )
    local = jnp.concatenate([local, local_h], axis=1)
    stats2 = total_stats(place, local, number[None, :, None])
    stats2, task_cot, shared_cot = lax.optimization_barrier((stats2, task_cot, shared_cot))
    (act2,) = call(
        functools.partial(act_kernel, 0), "act",
        [(p2, "v"), (stats2, "v"), (gb2, "v"), (sel0, "v")],
        [(tile0, bf16)], limit=4,
    )
    (act2,) = place.halo([act2], 2, images)
    act2, task_cot, shared_cot = lax.optimization_barrier((act2, task_cot, shared_cot))
    cots = jnp.concatenate([task_cot, shared_cot[None]]).transpose(0, 2, 3, 1, 4)
    cots = place.pieces(cots.reshape(TASKS + 1, half_h, half_w * images, c))
    hidden0, hidden1, g0, g1, local_g = call(
        gate_kernel, "gate",
        [
            (h0, "v"), (h1, "v"), (second_w, "v"), (stats2, "v"), (gb2, "v"), (sel1, "v"),
            (scal, "s"),
        ],
        [
            (tile1, bf16), (tile1, bf16), (tile1, f32), (tile1, f32),
            ((2, TASKS, DOMAINS, c), f32),
        ],
        limit=10,
    )

    p3, local = call(
        functools.partial(first_kernel, images, 2 * TAPS), "third",
        [(act2, "v"), (shared_taps, "a"), (sel1, "v"), (scal, "s")],
        [(tile1, f32), ((2, 1, DOMAINS, c), f32)],
        shift=shift2, weights=1, limit=46,
    )
    stats3 = total_stats(
        place, jnp.concatenate([local, local_g], axis=1), number[None, :, None]
    )

    m0, m1, r0, r1, local = call(
        functools.partial(fourth_kernel, images), "fourth",
        [
            (p3, "v"), (g0, "v"), (g1, "v"), (task_taps, "a"), (stats3, "v"), (gb3, "v"),
            (sel1, "v"), (sel0, "v"), (scal, "s"),
        ],
        [
            (tile1, bf16), (tile1, bf16), (tile0, f32), (tile0, f32),
            ((2, TASKS, DOMAINS, c), f32),
        ],
        shift=shift1, weights=2, limit=44,
    )
    local, cots = lax.optimization_barrier((local, cots))
    cots = place.join(cots, 2)
    statsr = total_stats(place, local, number[None, :, None])

    local, dy_r = call(
        refined_sums_kernel, "refined_sums",
        [
            (r0, "v"), (r1, "v"), (cots[0], "v"), (cots[1], "v"), (up0, "v"), (statsr, "v"),
            (gbr, "v"), (sel0, "v"),
        ],
        [((TASKS, 2, DOMAINS, c), f32), ((TASKS, *tile0), f32)],
        extra=[(half_h, rows0, c)], limit=6,
    )
    sums_r = total_sums(place, local)
    dv_r = call(
        refined_back_kernel, "refined_back",
        [
            (r0, "v"), (r1, "v"), (dy_r, "v"), (statsr, "v"), (gbr, "v"), (sums_r, "v"),
            (sel0, "v"), (scal, "s"),
        ],
        [(tile0, bf16), (tile0, bf16)], limit=4,
    )
    (shared_low,) = place.halo([cots[TASKS]], 1, images)
    dv_halo = place.halo(dv_r, 2, images)
    part = parts(
        place, ((0, 2, True), (1, 3, True)), images, [m0, m1], dv_r
    )
    dv_halo, part, shared_low = lax.optimization_barrier((dv_halo, part, shared_low))
    part = place.scatter_core(part)
    (grad0,) = call(
        functools.partial(conv_back_kernel, images, 0), "masked_back0",
        [(dv_halo[0], "v"), (task_taps, "a")], [(tile1, f32)],
        shift=shift2, weights=1, back=True, limit=44,
    )
    grad0, part = lax.optimization_barrier((grad0, part))
    task_chunk = place.scatter_chips(part)
    dy3, dyg0, dyg1, local = call(
        functools.partial(masked_back_kernel, images), "masked_back1",
        [
            (dv_halo[1], "v"), (task_taps, "a"), (grad0, "v"), (p3, "v"), (g0, "v"), (g1, "v"),
            (shared_low, "v"), (up1, "v"), (stats3, "v"), (gb3, "v"), (sel1, "v"),
        ],
        [(tile1, f32), (tile1, f32), (tile1, f32), ((3, 2, DOMAINS, c), f32)],
        shift=shift2, weights=1, back=True, extra=[(half_h + 2, rows1, c)], limit=40,
    )
    local, task_chunk = lax.optimization_barrier((local, task_chunk))
    task_rows = gather_rows(place, task_chunk)

    sums3 = total_sums(place, local)
    dv3, dy2, local = call(
        functools.partial(third_back_kernel, images), "third_back",
        [
            (dy3, "v"), (p3, "v"), (p2, "v"), (shared_taps, "a"), (stats3, "v"), (gb3, "v"),
            (sums3, "v"), (stats2, "v"), (gb2, "v"), (sel1, "v"), (sel0, "v"), (scal, "s"),
        ],
        [(tile1, bf16), (tile0, f32), ((1, 2, DOMAINS, c), f32)],
        shift=shift1, weights=1, back=True, limit=40,
    )
    dvg0, dvg1, dyh0, dyh1, local_h = call(
        gate_back_kernel, "gate_back",
        [
            (dyg0, "v"), (dyg1, "v"), (g0, "v"), (g1, "v"), (h0, "v"), (h1, "v"),
            (second_w, "v"), (stats3, "v"), (gb3, "v"), (sums3, "v"), (stats2, "v"), (gb2, "v"),
            (sel1, "v"), (scal, "s"),
        ],
        [
            (tile1, bf16), (tile1, bf16), (tile1, f32), (tile1, f32),
            ((TASKS, 2, DOMAINS, c), f32),
        ],
        limit=10,
    )
    part3 = parts(
        place, ((0, 3, False), (1, 4, False), (2, 5, True)), images,
        [hidden0, hidden1, act2], [dvg0, dvg1, dv3],
    )
    part3 = place.scatter_core(part3)

    sums2 = total_sums(place, jnp.concatenate([local, local_h]))
    (dv2,) = call(
        functools.partial(back_kernel, 0, False), "second_dv",
        [
            (dy2, "v"), (p2, "v"), (stats2, "v"), (gb2, "v"), (sums2, "v"), (sel0, "v"),
            (scal, "s"),
        ],
        [(tile0, bf16)], limit=4,
    )
    (dv2_halo,) = place.halo([dv2], 2, images)
    dv2_halo, part3 = lax.optimization_barrier((dv2_halo, part3))
    chunk3 = place.scatter_chips(part3)
    dvh0, dvh1, grad_hidden = call(
        hidden_back_kernel, "hidden_back",
        [
            (dyh0, "v"), (dyh1, "v"), (h0, "v"), (h1, "v"), (first_w, "v"), (stats2, "v"),
            (gb2, "v"), (sums2, "v"), (sel1, "v"), (scal, "s"),
        ],
        [(tile1, bf16), (tile1, bf16), (tile1, f32)], limit=10,
    )
    dy1, local = call(
        functools.partial(second_back_kernel, images), "second_back",
        [
            (dv2_halo, "v"), (shared_taps, "a"), (grad_hidden, "v"), (p1, "v"), (stats1, "v"),
            (gb1, "v"), (sel1, "v"),
        ],
        [(tile1, f32), ((1, 2, DOMAINS, c), f32)],
        shift=shift2, weights=1, back=True, limit=40,
    )
    part2 = parts(
        place,
        ((0, 3, False), (1, 3, False), (0, 4, False), (2, 4, False), (0, 5, True)),
        images, [act1, priors[0], priors[1]], [dvh0, dvh1, dv2],
    )
    part2 = place.scatter_core(part2)
    local, part2, chunk3 = lax.optimization_barrier((local, part2, chunk3))

    sums1 = total_sums(place, local)
    (dv1,) = call(
        functools.partial(back_kernel, 0, True), "first_dv",
        [
            (dy1, "v"), (p1, "v"), (stats1, "v"), (gb1, "v"), (sums1, "v"), (sel1, "v"),
            (scal, "s"),
        ],
        [(tile1, bf16)], limit=4,
    )
    part1 = place.scatter_core(parts(place, ((0, 1, True),), images, [features], [dv1]))
    chunk1 = place.scatter_chips(jnp.concatenate([part1, part2[2 * TASKS :], part2[: 2 * TASKS]]))
    rest_rows = gather_rows(
        place,
        jnp.concatenate(
            [chunk1[: 2 * TAPS], chunk3[TASKS:], chunk1[2 * TAPS :], chunk3[:TASKS]]
        ),
    )
    chunk1, dv1, p3, r0, r1, dvh0, dvh1 = lax.optimization_barrier(
        (chunk1, dv1, p3, r0, r1, dvh0, dvh1)
    )

    def own(tile, border):
        width = (breadth + 2 * border) * images
        return lax.dynamic_slice_in_dim(tile, place.rep * breadth * images, width, tile.ndim - 2)

    def pooled(value, stat, gb):
        of = jnp.tile(member, (breadth, 1))
        average = jnp.where(of[:, :1] > 0.5, stat[0, :1], stat[0, 1:])
        inverse = lax.rsqrt(jnp.where(of[:, :1] > 0.5, stat[1, :1], stat[1, 1:]) + EPSILON)
        normed = (value - average) * inverse * gb[0] + gb[1]
        out = jax.nn.silu(normed).reshape(half_h, 2, half_w, 2, images, c)
        return jnp.mean(out, axis=(1, 3)).transpose(2, 0, 1, 3).astype(bf16)

    own3 = own(p3[1:-1, images : images + rows0], 0)
    shared_out = pooled(own3, stats3[:, 0], gb3[0])
    task_out = jnp.stack([pooled(own((r0, r1)[t], 0), statsr[:, t], gbr[t]) for t in range(TASKS)])

    near = own(dv1[:, : rows0 + 2 * images], 1).reshape(height + 2, breadth + 2, images, c)
    grad_features = lax.conv_general_dilated(
        near,
        jnp.flip(shared_w[0], (0, 1)),
        (1, 1),
        "VALID",
        dimension_numbers=("HWNC", "HWOI", "HWNC"),
        preferred_element_type=f32,
    ).transpose(2, 0, 1, 3)
    grad_priors = []
    for t, dv in enumerate((dvh0, dvh1)):
        mine = own(dv[1:-1, images : images + rows0], 0)
        value = jnp.einsum("hrd,cd->hrc", mine, first_w[t, c:], preferred_element_type=f32)
        grad_priors.append(value.reshape(height, breadth, images, c).transpose(2, 0, 1, 3))

    (grad_task,) = spread(place, task_rows, 0, [TASKS * TAPS], 9)
    (grad_shared,) = spread(place, rest_rows, 0, [CONVS * TAPS], 9)
    grad_first, grad_second = spread(place, rest_rows, CONVS * TAPS, [2 * TASKS, TASKS], 3)

    shared_sums = jnp.sum(jnp.stack([sums1[0], sums2[0], sums3[0]]), axis=2)
    task_sums = jnp.sum(jnp.stack([sums2[1:], sums3[1:], sums_r], axis=1), axis=3)
    return (
        shared_out,
        task_out,
        grad_features,
        jnp.stack(grad_priors),
        grad_shared.reshape(shared_w.shape),
        shared_sums[:, 1],
        shared_sums[:, 0],
        grad_first.reshape(first_w.shape),
        grad_second.reshape(second_w.shape),
        grad_task.reshape(task_conv.shape),
        task_sums[:, :, 1],
        task_sums[:, :, 0],
    )


def solution(mesh):
    return jax.shard_map(
        body,
        mesh=mesh,
        in_specs=(
            P(None, "row", "col", None),
            P(None, None, "row", "col", None),
            P(),
            P(),
            P(),
            P(),
            P(),
            P(),
            P(),
            P(),
            P(),
            P(None, "row", "col", None),
            P(None, None, "row", "col", None),
        ),
        out_specs=(
            P(None, "row", "col", None),
            P(None, None, "row", "col", None),
            P(None, "row", "col", None),
            P(None, None, "row", "col", None),
            P(),
            P(),
            P(),
            P(),
            P(),
            P(),
            P(),
            P(),
        ),
        check_vma=False,
    )
```

```python
import functools

import jax
import jax.numpy as jnp
from jax import lax
from jax.experimental import pallas as pl
from jax.experimental.pallas import tpu as pltpu
from jax.sharding import PartitionSpec as P

TASKS = 2
CONVS = 3
DOMAINS = 2
CORES = 2
REP = 4
TAPS = 9
LANES = 128
ROWS = 16
PAD = 16

EPSILON = 1e-05
BOTH = ("row", "col")
MIB = 1024 * 1024


class Place:
    def __init__(self):
        self.rows, self.cols = lax.axis_size("row"), lax.axis_size("col")
        self.groups = self.cols // REP
        self.row, self.col = lax.axis_index("row"), lax.axis_index("col")
        self.group, self.rep = self.col // REP, self.col % REP

    def swap(self, value, row_bits, col_bits):
        pairs = [
            (i, ((i // self.cols) ^ row_bits) * self.cols + ((i % self.cols) ^ col_bits))
            for i in range(self.rows * self.cols)
        ]
        return lax.ppermute(value, BOTH, pairs)

    def stages(self):
        bits = []
        k = 2
        while k < self.rows:
            bits.append((k, 0))
            k *= 2
        k = 1
        while k < self.groups:
            bits.append((0, k * REP))
            k *= 2
        steps = [[(1, 0)]]
        for i in range(0, len(bits), 2):
            pair = bits[i : i + 2]
            if len(pair) == 2:
                (a, b), (c, d) = pair
                pair = [(a, b), (c, d), (a ^ c, b ^ d)]
            steps.append(pair)
        return steps

    def pieces(self, tile):
        return [tile] + [self.swap(tile, 0, k) for k in range(1, REP)]

    def gather(self, tile, axis):
        return self.join(self.pieces(tile), axis)

    def join(self, pieces, axis):
        bit = 1
        while bit < REP:
            odd = (self.rep & bit) != 0
            pieces = [jnp.where(odd, pieces[j ^ bit], pieces[j]) for j in range(REP)]
            bit *= 2
        return jnp.concatenate(pieces, axis=axis)

    def halo_rows(self, low, high):
        even = self.row % 2 == 0
        near = lax.ppermute(
            jnp.where(even, high, low), "row", [(i, i ^ 1) for i in range(self.rows)]
        )
        pairs = []
        for i in range(1, self.rows - 1, 2):
            pairs += [(i, i + 1), (i + 1, i)]
        far = lax.ppermute(jnp.where(even, low, high), "row", pairs)
        return jnp.where(even, far, near), jnp.where(even, near, far)

    def halo_cols(self, low, high):
        even = self.group % 2 == 0
        near = self.swap(jnp.where(even, high, low), 0, REP)
        far = jnp.zeros_like(near)
        if self.groups > 2:
            pairs = []
            for i in range(self.cols - REP):
                if (i // REP) % 2:
                    pairs += [(i, i + REP), (i + REP, i)]
            far = lax.ppermute(jnp.where(even, low, high), "col", pairs)
        return jnp.where(even, far, near), jnp.where(even, near, far)

    def halo(self, tiles, pad, images):
        size = pad * images
        count = len(tiles)

        def columns(tiles):
            def edge(at):
                edges = [t[..., at, :].reshape(-1, size, t.shape[-1]) for t in tiles]
                extra = -(size * count) % 8
                if extra:
                    edges.append(jnp.zeros((edges[0].shape[0], extra, edges[0].shape[-1]), edges[0].dtype))
                edges = jnp.concatenate(edges, axis=1)
                return edges.reshape(-1, edges.shape[-1])

            got = self.halo_cols(edge(slice(0, size)), edge(slice(-size, None)))
            shape = tiles[0].shape
            width = -(-(size * count) // 8) * 8
            got = [x.reshape(-1, width, x.shape[-1]) for x in got]
            return [
                [x[:, t * size : (t + 1) * size].reshape(*shape[:-2], size, shape[-1]) for x in got]
                for t in range(count)
            ]

        sides = columns(tiles)
        ends = self.halo_rows(
            jnp.stack([t[..., :pad, :, :] for t in tiles]),
            jnp.stack([t[..., -pad:, :, :] for t in tiles]),
        )
        ends = [(ends[0][t], ends[1][t]) for t in range(count)]
        corners = columns([jnp.concatenate(e, axis=-3) for e in ends])
        whole = []
        for tile, (above, below), side, corner in zip(tiles, ends, sides, corners):
            tile = jnp.concatenate([above, tile, below], axis=-3)
            before, after = (
                jnp.concatenate([x[..., :pad, :, :], y, x[..., pad:, :, :]], axis=-3)
                for x, y in zip(corner, side)
            )
            fill = jnp.zeros((*tile.shape[:-2], pad * PAD - 2 * size, tile.shape[-1]), tile.dtype)
            whole.append(jnp.concatenate([before, tile, after, fill], axis=-2))
        return whole

    def scatter_core(self, parts):
        m, rows, c = parts.shape
        per = rows // (self.rows * self.groups)
        parts = parts.reshape(m, self.rows // CORES, CORES, self.groups, per, c)
        core = self.row % CORES
        other = lax.dynamic_index_in_dim(parts, 1 - core, 2, keepdims=False)
        other = self.swap(other.astype(jnp.bfloat16), 1, 0)
        mine = lax.dynamic_index_in_dim(parts, core, 2, keepdims=False)
        return mine + other.astype(jnp.float32)

    def scatter_chips(self, parts, beside=()):
        halves = self.rows // CORES
        cut = parts.shape[0] * 2 // 3

        def along_row(parts, axis=1):
            half = self.row // CORES
            got = []
            for a in range(halves):
                piece = lax.dynamic_index_in_dim(parts, half ^ a, axis, keepdims=False)
                if a:
                    piece = self.swap(piece.astype(jnp.bfloat16), a * CORES, 0)
                got.append(piece.astype(jnp.float32))
            return tree_sum(got)

        def along_col(parts, axis):
            got = []
            for b in range(self.groups):
                piece = lax.dynamic_index_in_dim(parts, self.group ^ b, axis, keepdims=False)
                if b:
                    piece = self.swap(piece.astype(jnp.bfloat16), 0, b * REP)
                got.append(piece.astype(jnp.float32))
            return tree_sum(got)

        parts = along_row(parts[:cut]), along_col(parts[cut:], 2)
        parts, beside = lax.optimization_barrier((parts, beside))
        parts = along_col(parts[0], 1), along_row(parts[1])
        return jnp.concatenate(parts).astype(jnp.bfloat16), beside

    def gather_swaps(self, chunk, beside):
        half = chunk.shape[-1] // 2
        line = jnp.stack([chunk, self.swap(chunk, 0, 2)])
        line = jnp.stack([line, self.swap(line, 0, 4)])
        first, last = line[..., :half], line[..., half:]
        along_y, along_x = self.swap(first, 2, 0), self.swap(last, 0, 1)
        first, last = jnp.stack([first, along_y]), jnp.stack([last, along_x])
        along_x, along_y = self.swap(first, 0, 1), self.swap(last, 2, 0)
        first, last = jnp.stack([first, along_x]), jnp.stack([last, along_y])
        first, last, beside = lax.optimization_barrier((first, last, beside))
        return beside, first, self.swap(first, 1, 0), last, self.swap(last, 1, 0)


def tree_sum(values):
    while len(values) > 1:
        values = [a + b for a, b in zip(values[::2], values[1::2])]
    return values[0]


def total_stats(place, local, number):
    for step in place.stages():
        both = [local] + [place.swap(local, *bits) for bits in step]
        averages = [b[0] for b in both]
        average = tree_sum(averages) * (1.0 / len(both))
        squares = tree_sum([b[1] for b in both]) + number * tree_sum(
            [(a - average) * (a - average) for a in averages]
        )
        local = jnp.stack([average, squares])
        number = number * len(both)
    return jnp.stack([local[0], local[1] / number])


def total_sums(place, value):
    for step in place.stages():
        value = tree_sum([value] + [place.swap(value, *bits) for bits in step])
    return value


def row_blocks(i):
    return pl.ds(pl.multiple_of(i * ROWS, ROWS), ROWS)


def sweep(rows, c, setup):
    for lane in range(0, c, LANES):
        step = setup(slice(lane, lane + LANES))

        @pl.loop(0, rows // ROWS)
        def block(i):
            step(row_blocks(i))


def sweep_sums(sel_ref, rows, c, count, setup, store):
    for lane in range(0, c, LANES):
        lanes = slice(lane, lane + LANES)
        step = setup(lanes)

        def block(i, sums):
            at = row_blocks(i)
            added = []
            for j, value in enumerate(step(at)):
                for k in range(DOMAINS):
                    part = value * sel_ref[1 + k, at]
                    added.append(sums[j * DOMAINS + k] + tree_sum([part[r : r + 8] for r in range(0, ROWS, 8)]))
            return tuple(added)

        zero = jnp.zeros((8, LANES), jnp.float32)
        sums = lax.fori_loop(0, rows // ROWS, block, (zero,) * (count * DOMAINS))
        for j in range(count):
            for k in range(DOMAINS):
                store(j, k, lanes, jnp.sum(sums[j * DOMAINS + k], axis=0, keepdims=True))


def own_lines(tile_ref):
    h = tile_ref.shape[0]
    border = (h - 8) // 2
    return border, h - border


class Norm:
    def __init__(self, stat_ref, gb_ref, i, lanes):
        self.average = [stat_ref[0, i, k : k + 1, lanes] for k in range(DOMAINS)]
        self.inverse = [
            lax.rsqrt(stat_ref[1, i, k : k + 1, lanes] + EPSILON) for k in range(DOMAINS)
        ]
        self.gain = gb_ref[i, 0:1, lanes]
        self.half_gain, self.half_bias = 0.5 * self.gain, 0.5 * gb_ref[i, 1:2, lanes]
        self.lanes = lanes

    def half(self, form):
        return form * self.half_gain + self.half_bias

    def forms(self, first):
        average, inverse = jnp.where(first, *self.average), jnp.where(first, *self.inverse)
        return lambda value: (value - average) * inverse

    def halves(self, first):
        times = [inverse * self.half_gain for inverse in self.inverse]
        plus = [self.half_bias - a * t for a, t in zip(self.average, times)]
        times, plus = jnp.where(first, *times), jnp.where(first, *plus)
        return lambda value: value * times + plus

    def backs(self, first, sums_ref, scal_ref, i):
        scale = [inverse * self.gain for inverse in self.inverse]
        plain, cross = (
            [sums_ref[i, j, k : k + 1, self.lanes] * scal_ref[2 + k] for k in range(DOMAINS)]
            for j in range(2)
        )
        slant = [s * x * inverse for s, x, inverse in zip(scale, cross, self.inverse)]
        plus = [a * e - s * p for a, e, s, p in zip(self.average, slant, scale, plain)]
        scale, slant, plus = (jnp.where(first, *pair) for pair in (scale, slant, plus))
        return lambda dy, value: scale * dy + (plus - slant * value)


def is_first(sel_ref, rows):
    return sel_ref[0, rows] > 0.5


def sigmoid(t):
    return 0.5 * jnp.tanh(t) + 0.5


def silu(t):
    return t + t * jnp.tanh(t)


def silu_slope(t, h):
    return (0.5 + 0.5 * h) * (1.0 + t * (1.0 - h))


def slope(t):
    return silu_slope(t, jnp.tanh(t))


def seen(sel_ref, scal_ref, rows, lines):
    column = sel_ref[3, rows]
    return [column * scal_ref[4]] + [column] * (lines - 2) + [column * scal_ref[5]]


def local_stats(tile_ref, sel_ref, scal_ref, out_ref, i):
    _, r, c = tile_ref.shape
    lines = range(*own_lines(tile_ref))

    def total(lanes):
        return lambda rows: [tree_sum([tile_ref[h, rows, lanes] for h in lines])]

    def keep_average(_, k, lanes, value):
        out_ref[0, i, k : k + 1, lanes] = value * scal_ref[k]

    sweep_sums(sel_ref, r, c, 1, total, keep_average)

    def square(lanes):
        averages = [out_ref[0, i, k : k + 1, lanes] for k in range(DOMAINS)]

        def step(rows):
            average = jnp.where(is_first(sel_ref, rows), *averages)
            apart = [tile_ref[h, rows, lanes] - average for h in lines]
            return [tree_sum([a * a for a in apart])]

        return step

    def keep_square(_, k, lanes, value):
        out_ref[1, i, k : k + 1, lanes] = value

    sweep_sums(sel_ref, r, c, 1, square, keep_square)


def fetch(w_ref, wv_ref, sem, start, back=False):
    c = w_ref.shape[-1]
    copies = []
    for t in range(TAPS):
        part = pl.ds((t % 3) * c, c)
        if back:
            source, target = w_ref.at[start + TAPS - 1 - t], wv_ref.at[t // 3, :, part]
        else:
            source, target = w_ref.at[start + t], wv_ref.at[t // 3, part, :]
        copies.append(pltpu.make_async_copy(source, target, sem.at[t]))
        copies[-1].start()
    return copies


def convolve(x_ref, xs_ref, wv_ref, copies, o_ref, images, back=False):
    hp, rp, c = x_ref.shape
    r = rp - PAD
    m = (hp - 2) * r
    for b in range(3):
        xs_ref[:, b * c : (b + 1) * c] = x_ref[:, b * images : b * images + r, :].reshape(hp * r, c)
    for a in range(3):
        for b in range(3):
            copies[3 * a + b].wait()
        part = lax.dot_general(
            xs_ref[a * r : a * r + m, :],
            wv_ref[a],
            (((1,), (1 if back else 0,)), ((), ())),
            preferred_element_type=jnp.float32,
        ).reshape(o_ref.shape)
        o_ref[...] = part if a == 0 else o_ref[...] + part


def flat(ref):
    h, r, c = ref.shape
    return ref[...].reshape(h * r, c)


def matmul(a, b):
    return jnp.dot(a, b, preferred_element_type=jnp.float32)


def matmul_back(a, b):
    return lax.dot_general(a, b, (((1,), (1,)), ((), ())), preferred_element_type=jnp.float32)


def first_kernel(images, tap, x_ref, w_ref, sel_ref, scal_ref, p_ref, st_ref, xs_ref, wv_ref, sem):
    copies = fetch(w_ref, wv_ref, sem, tap)
    convolve(x_ref, xs_ref, wv_ref, copies, p_ref, images)
    local_stats(p_ref, sel_ref, scal_ref, st_ref, 0)


def second_kernel(
    images, p1_ref, w_ref, st1_ref, gb_ref, sel_ref, sel0_ref, scal_ref,
    act_ref, p2_ref, st_ref, xs_ref, wv_ref, sem,
):
    copies = fetch(w_ref, wv_ref, sem, TAPS)
    lines, r, c = p1_ref.shape

    def activate(lanes):
        norm = Norm(st1_ref, gb_ref, 0, lanes)

        def step(rows):
            half = norm.halves(is_first(sel_ref, rows))
            for h, inside in enumerate(seen(sel_ref, scal_ref, rows, lines)):
                act_ref[h, rows, lanes] = (silu(half(p1_ref[h, rows, lanes])) * inside).astype(
                    jnp.bfloat16
                )

        return step

    sweep(r, c, activate)
    convolve(act_ref, xs_ref, wv_ref, copies, p2_ref, images)
    local_stats(p2_ref, sel0_ref, scal_ref, st_ref, 0)


def hidden_kernel(act_ref, pr_ref, fw_ref, sel_ref, scal_ref, h0_ref, h1_ref, st_ref):
    lines, r, c = act_ref.shape
    for t, h_ref in enumerate((h0_ref, h1_ref)):
        value = matmul(flat(act_ref), fw_ref[t, :c])
        h_ref[...] = (value + matmul(pr_ref[t].reshape(lines * r, c), fw_ref[t, c:])).reshape(
            h_ref.shape
        )
        local_stats(h_ref, sel_ref, scal_ref, st_ref, t)


def act_kernel(which, p_ref, st_ref, gb_ref, sel_ref, act_ref):
    lines, r, c = p_ref.shape

    def activate(lanes):
        norm = Norm(st_ref, gb_ref, which, lanes)

        def step(rows):
            half = norm.halves(is_first(sel_ref, rows))
            for h in range(lines):
                act_ref[h, rows, lanes] = silu(half(p_ref[h, rows, lanes])).astype(jnp.bfloat16)

        return step

    sweep(r, c, activate)


def gate_kernel(
    h0_ref, h1_ref, sw_ref, st2_ref, gb_ref, sel_ref, scal_ref, a0_ref, a1_ref, g0_ref, g1_ref, st_ref,
):
    for t, (h_ref, a_ref, g_ref) in enumerate(((h0_ref, a0_ref, g0_ref), (h1_ref, a1_ref, g1_ref))):
        act_kernel(1 + t, h_ref, st2_ref, gb_ref, sel_ref, a_ref)
        g_ref[...] = matmul(flat(a_ref), sw_ref[t]).reshape(g_ref.shape)
        local_stats(g_ref, sel_ref, scal_ref, st_ref, t)


def fourth_kernel(
    images, p3_ref, g0_ref, g1_ref, w_ref, st3_ref, gb_ref, sel_ref, sel0_ref, scal_ref,
    m0_ref, m1_ref, r0_ref, r1_ref, st_ref, xs_ref, wv_ref, sem, wv2_ref, sem2,
):
    copies = [fetch(w_ref, wv_ref, sem, 0), fetch(w_ref, wv2_ref, sem2, TAPS)]
    lines, r, c = p3_ref.shape

    def mask(lanes):
        norms = [Norm(st3_ref, gb_ref, i, lanes) for i in range(1 + TASKS)]

        def step(rows):
            first = is_first(sel_ref, rows)
            half, *gates = [norm.halves(first) for norm in norms]
            for h, inside in enumerate(seen(sel_ref, scal_ref, rows, lines)):
                last = silu(half(p3_ref[h, rows, lanes])) * inside
                for gate, g_ref, m_ref in zip(gates, (g0_ref, g1_ref), (m0_ref, m1_ref)):
                    attention = sigmoid(gate(g_ref[h, rows, lanes]))
                    m_ref[h, rows, lanes] = (attention * last).astype(jnp.bfloat16)

        return step

    sweep(r, c, mask)
    convolve(m0_ref, xs_ref, wv_ref, copies[0], r0_ref, images)
    convolve(m1_ref, xs_ref, wv2_ref, copies[1], r1_ref, images)
    local_stats(r0_ref, sel0_ref, scal_ref, st_ref, 0)
    local_stats(r1_ref, sel0_ref, scal_ref, st_ref, 1)


def dy_sums(dys, forms):
    return [tree_sum(list(dys)), tree_sum([dy * form for dy, form in zip(dys, forms)])]


def keep_sums(out_ref, at):
    def store(j, k, lanes, value):
        out_ref[at + j // 2, j % 2, k : k + 1, lanes] = value

    return store


def upsample(up_ref, low_ref, out_ref):
    for h in range(low_ref.shape[0]):
        out_ref[h] = matmul(up_ref[...], low_ref[h])


def refined_sums_kernel(
    r0_ref, r1_ref, c0_ref, c1_ref, up_ref, st_ref, gb_ref, sel_ref, out_ref, dy_ref, low_ref
):
    lines, r, c = r0_ref.shape
    for t, (r_ref, c_ref) in enumerate(((r0_ref, c0_ref), (r1_ref, c1_ref))):
        upsample(up_ref, c_ref, low_ref)

        def sums(lanes):
            norm = Norm(st_ref, gb_ref, t, lanes)

            def step(rows):
                form_of = norm.forms(is_first(sel_ref, rows))
                dys, forms = [], []
                for h in range(lines):
                    forms.append(form_of(r_ref[h, rows, lanes]))
                    dys.append(low_ref[h // 2, rows, lanes] * slope(norm.half(forms[-1])))
                    dy_ref[t, h, rows, lanes] = dys[-1]
                return dy_sums(dys, forms)

            return step

        sweep_sums(sel_ref, r, c, 2, sums, keep_sums(out_ref, t))


def refined_back_kernel(
    r0_ref, r1_ref, dy_ref, st_ref, gb_ref, sums_ref, sel_ref, scal_ref, dv0_ref, dv1_ref
):
    for t, (r_ref, dv_ref) in enumerate(((r0_ref, dv0_ref), (r1_ref, dv1_ref))):
        back_kernel(
            t, False, dy_ref.at[t], r_ref, st_ref, gb_ref, sums_ref, sel_ref, scal_ref, dv_ref
        )


def conv_back_kernel(images, start, x_ref, w_ref, o_ref, xs_ref, wv_ref, sem):
    copies = fetch(w_ref, wv_ref, sem, start, True)
    convolve(x_ref, xs_ref, wv_ref, copies, o_ref, images, True)


def masked_back_kernel(
    images, dv_ref, w_ref, grad_ref, p3_ref, g0_ref, g1_ref, cot_ref, up_ref, st3_ref, gb_ref,
    sel_ref, dy3_ref, dy0_ref, dy1_ref, sums_ref, xs_ref, wv_ref, sem, low_ref,
):
    copies = fetch(w_ref, wv_ref, sem, TAPS, True)
    convolve(dv_ref, xs_ref, wv_ref, copies, dy1_ref, images, True)
    lines, r, c = p3_ref.shape
    own = slice(*own_lines(p3_ref))
    upsample(up_ref, cot_ref, low_ref)

    def setup(lanes):
        norms = [Norm(st3_ref, gb_ref, i, lanes) for i in range(1 + TASKS)]

        def step(rows):
            first = is_first(sel_ref, rows)
            form_of = [norm.forms(first) for norm in norms]
            dys, forms = [[], [], []], [[], [], []]
            for h in range(lines):
                form = form_of[0](p3_ref[h, rows, lanes])
                half = norms[0].half(form)
                tanh = jnp.tanh(half)
                last = half + half * tanh
                grad_last = low_ref[(h + 1) // 2, rows, lanes]
                for i, (g_ref, from_ref, d_ref) in enumerate(
                    ((g0_ref, grad_ref, dy0_ref), (g1_ref, dy1_ref, dy1_ref)), 1
                ):
                    gate_form = form_of[i](g_ref[h, rows, lanes])
                    attention = sigmoid(norms[i].half(gate_form))
                    grad = from_ref[h, rows, lanes] * attention
                    grad_last = grad_last + grad
                    dy = grad * last * (1.0 - attention)
                    d_ref[h, rows, lanes] = dy
                    dys[i].append(dy)
                    forms[i].append(gate_form)
                dy = grad_last * silu_slope(half, tanh)
                dy3_ref[h, rows, lanes] = dy
                dys[0].append(dy)
                forms[0].append(form)
            return [x for d, f in zip(dys, forms) for x in dy_sums(d[own], f[own])]

        return step

    sweep_sums(sel_ref, r, c, 6, setup, keep_sums(sums_ref, 0))


def slope_sums(which, out_at, grad_ref, add_ref, p_ref, st_ref, gb_ref, sel_ref, sums_ref):
    lines, r, c = p_ref.shape
    own = slice(*own_lines(p_ref))

    def setup(lanes):
        norm = Norm(st_ref, gb_ref, which, lanes)

        def step(rows):
            form_of = norm.forms(is_first(sel_ref, rows))
            dys, forms = [], []
            for h in range(lines):
                form = form_of(p_ref[h, rows, lanes])
                grad = grad_ref[h, rows, lanes]
                if add_ref is not None:
                    grad = grad + add_ref[h, rows, lanes]
                dy = grad * slope(norm.half(form))
                grad_ref[h, rows, lanes] = dy
                dys.append(dy)
                forms.append(form)
            return dy_sums(dys[own], forms[own])

        return step

    sweep_sums(sel_ref, r, c, 2, setup, keep_sums(sums_ref, out_at))


def back_kernel(which, masked, dy_ref, p_ref, st_ref, gb_ref, sums_ref, sel_ref, scal_ref, dv_ref):
    lines, r, c = p_ref.shape

    def setup(lanes):
        norm = Norm(st_ref, gb_ref, which, lanes)

        def step(rows):
            back = norm.backs(is_first(sel_ref, rows), sums_ref, scal_ref, which)
            inside = seen(sel_ref, scal_ref, rows, lines)
            for h in range(lines):
                dv = back(dy_ref[h, rows, lanes], p_ref[h, rows, lanes])
                if masked:
                    dv = dv * inside[h]
                dv_ref[h, rows, lanes] = dv.astype(jnp.bfloat16)

        return step

    sweep(r, c, setup)


def third_back_kernel(
    images, dy3_ref, p3_ref, p2_ref, w_ref, st3_ref, gb3_ref, sums_ref, st2_ref, gb2_ref,
    sel_ref, sel0_ref, scal_ref, dv3_ref, dy2_ref, out_ref, xs_ref, wv_ref, sem,
):
    copies = fetch(w_ref, wv_ref, sem, 2 * TAPS, True)
    back_kernel(0, True, dy3_ref, p3_ref, st3_ref, gb3_ref, sums_ref, sel_ref, scal_ref, dv3_ref)
    convolve(dv3_ref, xs_ref, wv_ref, copies, dy2_ref, images, True)
    slope_sums(0, 0, dy2_ref, None, p2_ref, st2_ref, gb2_ref, sel0_ref, out_ref)


def gate_back_kernel(
    dy0_ref, dy1_ref, g0_ref, g1_ref, h0_ref, h1_ref, sw_ref, st3_ref, gb3_ref, sums_ref,
    st2_ref, gb2_ref, sel_ref, scal_ref, dv0_ref, dv1_ref, dh0_ref, dh1_ref, out_ref,
):
    for t, (dy_ref, g_ref, dv_ref, h_ref, dh_ref) in enumerate(
        (
            (dy0_ref, g0_ref, dv0_ref, h0_ref, dh0_ref),
            (dy1_ref, g1_ref, dv1_ref, h1_ref, dh1_ref),
        )
    ):
        back_kernel(
            1 + t, False, dy_ref, g_ref, st3_ref, gb3_ref, sums_ref, sel_ref, scal_ref, dv_ref
        )
        dh_ref[...] = matmul_back(flat(dv_ref), sw_ref[t]).reshape(dh_ref.shape)
        slope_sums(1 + t, t, dh_ref, None, h_ref, st2_ref, gb2_ref, sel_ref, out_ref)


def hidden_back_kernel(
    dyh0_ref, dyh1_ref, h0_ref, h1_ref, fw_ref, st_ref, gb_ref, sums_ref, sel_ref, scal_ref,
    dv0_ref, dv1_ref, grad_ref,
):
    _, _, c = h0_ref.shape
    for t, (dy_ref, h_ref, dv_ref) in enumerate(
        ((dyh0_ref, h0_ref, dv0_ref), (dyh1_ref, h1_ref, dv1_ref))
    ):
        back_kernel(1 + t, False, dy_ref, h_ref, st_ref, gb_ref, sums_ref, sel_ref, scal_ref, dv_ref)
        value = matmul_back(flat(dv_ref), fw_ref[t, :c]).reshape(grad_ref.shape)
        grad_ref[...] = value if t == 0 else grad_ref[...] + value


def second_back_kernel(
    images, dv2_ref, w_ref, add_ref, p1_ref, st_ref, gb_ref, sel_ref,
    dy_ref, sums_ref, xs_ref, wv_ref, sem,
):
    copies = fetch(w_ref, wv_ref, sem, TAPS, True)
    convolve(dv2_ref, xs_ref, wv_ref, copies, dy_ref, images, True)
    slope_sums(0, 0, dy_ref, add_ref, p1_ref, st_ref, gb_ref, sel_ref, sums_ref)


def parts_kernel(plan, images, block_ref, *refs):
    *sources, out_ref, xs_ref = refs
    at = 0
    for x, g, conv in plan:
        x_ref, g_ref = sources[x], sources[g]
        border = (g_ref.shape[0] - 8) // 2
        cols = g_ref.shape[1] - border * PAD
        k = 8 * cols
        grad = g_ref[border : border + 8, border * images : border * images + cols, :]
        grad = grad.reshape(k, grad.shape[-1])
        border = (x_ref.shape[0] - 8) // 2
        taps = [(a, b) for a in (-1, 0, 1) for b in (-1, 0, 1)] if conv else [(0, 0)]
        for t, (a, b) in enumerate(taps):
            start = (border + b) * images
            xs_ref[:, t * LANES : (t + 1) * LANES] = x_ref[
                border + a : border + a + 8, start : start + cols, :
            ].reshape(k, LANES)
        size = len(taps) * LANES
        part = lax.dot_general(
            xs_ref[:, :size], grad, (((0,), (0,)), ((), ())), preferred_element_type=jnp.float32
        )
        out_ref[at : at + len(taps)] = part.reshape(len(taps), LANES, part.shape[-1])
        at += len(taps)


def parts(place, plan, images, acts, grads):
    c = grads[0].shape[-1]
    count = sum(TAPS if conv else 1 for _, _, conv in plan)

    def act_spec(x):
        return pl.BlockSpec((*x.shape[:2], LANES), lambda i, b: (0, 0, b[0]))


    return pl.pallas_call(
        functools.partial(parts_kernel, plan, images),
        out_shape=jax.ShapeDtypeStruct((count, LANES, c), jnp.float32),
        grid_spec=pltpu.PrefetchScalarGridSpec(
            num_scalar_prefetch=1,
            grid=(1,),
            in_specs=[act_spec(x) for x in acts] + [VMEM_SPEC] * len(grads),
            out_specs=VMEM_SPEC,
            scratch_shapes=[pltpu.VMEM((8 * 16 * images, TAPS * LANES), jnp.bfloat16)],
        ),
        compiler_params=pltpu.CompilerParams(vmem_limit_bytes=12 * MIB),
        name="parts",
    )(place.rep.astype(jnp.int32)[None], *acts, *grads)


def spread_kernel(groups, sources_per, skip, *refs):
    sources, targets = refs[: groups * sources_per], refs[groups * sources_per + skip :]
    at = 0
    places = [(target, i) for target in targets for i in range(target.shape[0])]
    for s in range(sources_per):
        for i in range(sources[0].shape[3]):
            target, m = places[s * sources[0].shape[3] + i]
            for g in range(groups):
                source = sources[s * groups + g]
                rows, _, _, _, per, _ = source.shape
                for r in range(rows):
                    at = (r * groups + g) * per
                    target[m, at : at + per, :] = source[r, 0, 0, i].astype(jnp.float32)


def spread(place, gathered, start, counts, step, into=None):
    rows, groups, _, _, per, c = gathered.shape
    block = rows * groups * per
    sources = 1 if len(counts) == 1 else sum(counts) // step

    def source(s, g):
        return pl.BlockSpec(
            (rows, 1, 1, step, per, c),
            lambda i, b: (0, g, b, start // step + s + i, 0, 0),
        )

    takes = [step] if len(counts) == 1 else counts
    old = [] if into is None else [into]
    at = into.shape[0] - counts[0] if old else 0
    return pl.pallas_call(
        functools.partial(spread_kernel, groups, sources, len(old)),
        out_shape=[jax.ShapeDtypeStruct((n + at, REP * block, c), jnp.float32) for n in counts],
        grid=(sum(counts) // (step * sources), REP),
        in_specs=[source(s, g) for s in range(sources) for g in range(groups)]
        + [pl.BlockSpec(memory_space=pl.ANY)] * len(old),
        out_specs=[pl.BlockSpec((n, block, c), lambda i, b: (at // step + i, b, 0)) for n in takes],
        input_output_aliases={groups * sources: 0} if old else {},
        compiler_params=pltpu.CompilerParams(vmem_limit_bytes=58 * MIB),
        cost_estimate=pl.CostEstimate(
            flops=0, bytes_accessed=6 * sum(counts) * REP * block * c, transcendentals=0
        ),
        name="spread",
    )(*([gathered] * (groups * sources)), *old)


def place_kernel(place_ref, *refs):
    *sources, target = refs
    per, half = sources[0].shape[-2:]
    row, col = place_ref[0], place_ref[1]
    for r in range(4):
        for q in range(8):
            apart_r, apart_q = r ^ row, q ^ col
            y, x, high, low = apart_r // 2, apart_q % 2, apart_q // 4, apart_q // 2 % 2
            same = apart_r % 2 == 0
            at = ((q % REP) * 8 + r * 2 + q // REP) * per
            first = jnp.where(same, sources[0][x, y, high, low], sources[1][x, y, high, low])
            last = jnp.where(same, sources[2][y, x, high, low], sources[3][y, x, high, low])
            target[:, at : at + per, :half] = first.astype(jnp.float32)
            target[:, at : at + per, half:] = last.astype(jnp.float32)


def place_swapped(place, swapped, total, step):
    m, per, half = swapped[0].shape[-3:]
    rows = place.rows * place.cols * per
    here = jnp.stack([place.row, place.col]).astype(jnp.int32)

    def source(part):
        return pl.BlockSpec(
            (*part.shape[:4], step, per, half), lambda i, here: (0, 0, 0, 0, i, 0, 0)
        )

    return pl.pallas_call(
        place_kernel,
        out_shape=jax.ShapeDtypeStruct((total, rows, 2 * half), jnp.float32),
        grid_spec=pltpu.PrefetchScalarGridSpec(
            num_scalar_prefetch=1,
            grid=(m // step,),
            in_specs=[source(p) for p in swapped],
            out_specs=pl.BlockSpec((step, rows, 2 * half), lambda i, here: (i, 0, 0)),
        ),
        compiler_params=pltpu.CompilerParams(vmem_limit_bytes=32 * MIB),
        cost_estimate=pl.CostEstimate(
            flops=0, bytes_accessed=12 * m * rows * half, transcendentals=0
        ),
        name="place",
    )(here, *swapped)


def gather_rows(place, chunk):
    whole = lax.all_gather(chunk, BOTH)
    return whole.reshape(place.rows, place.groups, REP, *chunk.shape)


VMEM_SPEC = pl.BlockSpec(memory_space=pltpu.VMEM)
SMEM_SPEC = pl.BlockSpec(memory_space=pltpu.SMEM)
HBM_SPEC = pl.BlockSpec(memory_space=pltpu.HBM)


def call(kernel, name, ins, outs, shift=None, weights=0, back=False, extra=(), limit=32):
    specs = {"v": VMEM_SPEC, "s": SMEM_SPEC, "a": HBM_SPEC}
    c = outs[0][0][-1]
    scratch = []
    if shift:
        scratch.append(pltpu.VMEM(shift, jnp.bfloat16))
    for _ in range(weights):
        taps = (3, c, 3 * c) if back else (3, 3 * c, c)
        scratch += [pltpu.VMEM(taps, jnp.bfloat16), pltpu.SemaphoreType.DMA((TAPS,))]
    scratch += [pltpu.VMEM(e, jnp.float32) for e in extra]
    return pl.pallas_call(
        kernel,
        out_shape=[jax.ShapeDtypeStruct(*o) for o in outs],
        in_specs=[specs[k] for _, k in ins],
        out_specs=[VMEM_SPEC] * len(outs),
        scratch_shapes=scratch,
        compiler_params=pltpu.CompilerParams(vmem_limit_bytes=limit * MIB),
        name=name,
    )(*[a for a, _ in ins])


def body(
    features,
    priors,
    domain,
    shared_w,
    shared_gain,
    shared_bias,
    first_w,
    second_w,
    task_conv,
    task_gain,
    task_bias,
    shared_cot,
    task_cot,
):
    place = Place()
    images, height, breadth, c = features.shape
    wide = breadth * REP
    f32, bf16 = jnp.float32, jnp.bfloat16
    member = (domain[:, None] == jnp.arange(DOMAINS, dtype=jnp.int32)[None, :]).astype(f32)
    named = jnp.sum(member, axis=0)
    number = named * (height * wide)
    counts = number * (place.rows * place.groups)
    scal = jnp.concatenate(
        [
            1.0 / number,
            1.0 / counts,
            (place.row > 0).astype(f32)[None],
            (place.row < place.rows - 1).astype(f32)[None],
        ]
    )

    rows0, rows1, rows2 = wide * images, wide * images + PAD, wide * images + 2 * PAD
    tile0, tile1, tile2 = (
        (height, rows0, c), (height + 2, rows1, c), (height + 4, rows2, c),
    )
    shift1 = ((height + 2) * rows0, 3 * c)
    shift2 = ((height + 4) * rows1, 3 * c)

    def selectors(rows, border):
        r = jnp.arange(rows)
        w, image = r // images - border, r % images
        of = member[image]
        own = ((w >= 0) & (w < wide)).astype(f32)
        col = place.group * wide + w
        seen = (col >= 0) & (col < wide * place.groups) & (w < wide + border)
        table = jnp.stack([of[:, 0], of[:, 0] * own, of[:, 1] * own, seen.astype(f32)])
        return jnp.broadcast_to(table[:, :, None], (4, rows, LANES))

    sel0, sel1 = selectors(rows0, 0), selectors(rows1, 1)
    gains = jnp.stack([shared_gain, shared_bias], axis=1)
    task_gains = jnp.stack([task_gain, task_bias], axis=2)
    gb1 = gains[0][None]
    gb2 = jnp.stack([gains[1], task_gains[0, 0], task_gains[1, 0]])
    gb3 = jnp.stack([gains[2], task_gains[0, 1], task_gains[1, 1]])
    gbr = task_gains[:, 2]
    shared_taps = shared_w.reshape(CONVS * TAPS, c, c)
    task_taps = task_conv.reshape(TASKS * TAPS, c, c)

    features = features.transpose(1, 2, 0, 3).reshape(height, breadth * images, c)
    (features,) = place.halo([place.gather(features, 1)], 2, images)
    priors = priors.transpose(0, 2, 3, 1, 4).reshape(TASKS, height, breadth * images, c)
    priors = place.pieces(priors)
    half_h, half_w = height // 2, breadth // 2

    def spreader(rows, border):
        r = jnp.arange(rows)
        source = (r // images + border) // 2 * images + r % images
        size = (REP * half_w) * images + border * PAD
        return (0.25 * (source[:, None] == jnp.arange(size)[None])).astype(bf16)

    up0, up1 = spreader(rows0, 0), spreader(rows1, 1)

    p1, local = call(
        functools.partial(first_kernel, images, 0), "first",
        [(features, "v"), (shared_taps, "a"), (sel1, "v"), (scal, "s")],
        [(tile1, f32), ((2, 1, DOMAINS, c), f32)],
        shift=shift2, weights=1, limit=46,
    )
    p1, priors = lax.optimization_barrier((p1, priors))
    (priors,) = place.halo([place.join(priors, 2)], 1, images)
    stats1 = total_stats(place, local, number[None, :, None])

    act1, p2, local = call(
        functools.partial(second_kernel, images), "second",
        [
            (p1, "v"), (shared_taps, "a"), (stats1, "v"), (gb1, "v"), (sel1, "v"), (sel0, "v"),
            (scal, "s"),
        ],
        [(tile1, bf16), (tile0, f32), ((2, 1, DOMAINS, c), f32)],
        shift=shift1, weights=1, limit=44,
    )
    h0, h1, local_h = call(
        hidden_kernel, "hidden",
        [(act1, "v"), (priors, "v"), (first_w, "v"), (sel1, "v"), (scal, "s")],
        [(tile1, f32), (tile1, f32), ((2, TASKS, DOMAINS, c), f32)], limit=12,
    )
    local = jnp.concatenate([local, local_h], axis=1)
    stats2 = total_stats(place, local, number[None, :, None])
    stats2, task_cot, shared_cot = lax.optimization_barrier((stats2, task_cot, shared_cot))
    (act2,) = call(
        functools.partial(act_kernel, 0), "act",
        [(p2, "v"), (stats2, "v"), (gb2, "v"), (sel0, "v")],
        [(tile0, bf16)], limit=4,
    )
    (act2,) = place.halo([act2], 2, images)
    act2, task_cot, shared_cot = lax.optimization_barrier((act2, task_cot, shared_cot))
    cots = jnp.concatenate([task_cot, shared_cot[None]]).transpose(0, 2, 3, 1, 4)
    cots = place.pieces(cots.reshape(TASKS + 1, half_h, half_w * images, c))
    hidden0, hidden1, g0, g1, local_g = call(
        gate_kernel, "gate",
        [
            (h0, "v"), (h1, "v"), (second_w, "v"), (stats2, "v"), (gb2, "v"), (sel1, "v"),
            (scal, "s"),
        ],
        [
            (tile1, bf16), (tile1, bf16), (tile1, f32), (tile1, f32),
            ((2, TASKS, DOMAINS, c), f32),
        ],
        limit=10,
    )

    p3, local = call(
        functools.partial(first_kernel, images, 2 * TAPS), "third",
        [(act2, "v"), (shared_taps, "a"), (sel1, "v"), (scal, "s")],
        [(tile1, f32), ((2, 1, DOMAINS, c), f32)],
        shift=shift2, weights=1, limit=46,
    )
    stats3 = total_stats(
        place, jnp.concatenate([local, local_g], axis=1), number[None, :, None]
    )

    m0, m1, r0, r1, local = call(
        functools.partial(fourth_kernel, images), "fourth",
        [
            (p3, "v"), (g0, "v"), (g1, "v"), (task_taps, "a"), (stats3, "v"), (gb3, "v"),
            (sel1, "v"), (sel0, "v"), (scal, "s"),
        ],
        [
            (tile1, bf16), (tile1, bf16), (tile0, f32), (tile0, f32),
            ((2, TASKS, DOMAINS, c), f32),
        ],
        shift=shift1, weights=2, limit=44,
    )
    local, cots = lax.optimization_barrier((local, cots))
    cots = place.join(cots, 2)
    statsr = total_stats(place, local, number[None, :, None])

    local, dy_r = call(
        refined_sums_kernel, "refined_sums",
        [
            (r0, "v"), (r1, "v"), (cots[0], "v"), (cots[1], "v"), (up0, "v"), (statsr, "v"),
            (gbr, "v"), (sel0, "v"),
        ],
        [((TASKS, 2, DOMAINS, c), f32), ((TASKS, *tile0), f32)],
        extra=[(half_h, rows0, c)], limit=6,
    )
    sums_r = total_sums(place, local)
    dv_r = call(
        refined_back_kernel, "refined_back",
        [
            (r0, "v"), (r1, "v"), (dy_r, "v"), (statsr, "v"), (gbr, "v"), (sums_r, "v"),
            (sel0, "v"), (scal, "s"),
        ],
        [(tile0, bf16), (tile0, bf16)], limit=4,
    )
    (shared_low,) = place.halo([cots[TASKS]], 1, images)
    dv_halo = place.halo(dv_r, 2, images)
    part = parts(
        place, ((0, 2, True), (1, 3, True)), images, [m0, m1], dv_r
    )
    part = place.scatter_core(part)
    dv_halo, part, shared_low = lax.optimization_barrier((dv_halo, part, shared_low))
    (grad0,) = call(
        functools.partial(conv_back_kernel, images, 0), "masked_back0",
        [(dv_halo[0], "v"), (task_taps, "a")], [(tile1, f32)],
        shift=shift2, weights=1, back=True, limit=44,
    )
    task_chunk, grad0 = place.scatter_chips(part, grad0)
    dy3, dyg0, dyg1, local = call(
        functools.partial(masked_back_kernel, images), "masked_back1",
        [
            (dv_halo[1], "v"), (task_taps, "a"), (grad0, "v"), (p3, "v"), (g0, "v"), (g1, "v"),
            (shared_low, "v"), (up1, "v"), (stats3, "v"), (gb3, "v"), (sel1, "v"),
        ],
        [(tile1, f32), (tile1, f32), (tile1, f32), ((3, 2, DOMAINS, c), f32)],
        shift=shift2, weights=1, back=True, extra=[(half_h + 2, rows1, c)], limit=40,
    )
    local, task_chunk = lax.optimization_barrier((local, task_chunk))
    task_rows = gather_rows(place, task_chunk)

    sums3 = total_sums(place, local)
    dv3, dy2, local = call(
        functools.partial(third_back_kernel, images), "third_back",
        [
            (dy3, "v"), (p3, "v"), (p2, "v"), (shared_taps, "a"), (stats3, "v"), (gb3, "v"),
            (sums3, "v"), (stats2, "v"), (gb2, "v"), (sel1, "v"), (sel0, "v"), (scal, "s"),
        ],
        [(tile1, bf16), (tile0, f32), ((1, 2, DOMAINS, c), f32)],
        shift=shift1, weights=1, back=True, limit=40,
    )
    dvg0, dvg1, dyh0, dyh1, local_h = call(
        gate_back_kernel, "gate_back",
        [
            (dyg0, "v"), (dyg1, "v"), (g0, "v"), (g1, "v"), (h0, "v"), (h1, "v"),
            (second_w, "v"), (stats3, "v"), (gb3, "v"), (sums3, "v"), (stats2, "v"), (gb2, "v"),
            (sel1, "v"), (scal, "s"),
        ],
        [
            (tile1, bf16), (tile1, bf16), (tile1, f32), (tile1, f32),
            ((TASKS, 2, DOMAINS, c), f32),
        ],
        limit=10,
    )
    part3 = parts(
        place, ((0, 3, False), (1, 4, False), (2, 5, True)), images,
        [hidden0, hidden1, act2], [dvg0, dvg1, dv3],
    )
    part3 = place.scatter_core(part3)

    sums2 = total_sums(place, jnp.concatenate([local, local_h]))
    (dv2,) = call(
        functools.partial(back_kernel, 0, False), "second_dv",
        [
            (dy2, "v"), (p2, "v"), (stats2, "v"), (gb2, "v"), (sums2, "v"), (sel0, "v"),
            (scal, "s"),
        ],
        [(tile0, bf16)], limit=4,
    )
    (dv2_halo,) = place.halo([dv2], 2, images)
    dvh0, dvh1, grad_hidden = call(
        hidden_back_kernel, "hidden_back",
        [
            (dyh0, "v"), (dyh1, "v"), (h0, "v"), (h1, "v"), (first_w, "v"), (stats2, "v"),
            (gb2, "v"), (sums2, "v"), (sel1, "v"), (scal, "s"),
        ],
        [(tile1, bf16), (tile1, bf16), (tile1, f32)], limit=10,
    )
    part2 = parts(
        place,
        ((0, 5, True), (0, 3, False), (1, 3, False), (0, 4, False), (2, 4, False)),
        images, [act1, priors[0], priors[1]], [dvh0, dvh1, dv2],
    )
    part2 = place.scatter_core(part2)
    dv2_halo, grad_hidden, part2, part3 = lax.optimization_barrier(
        (dv2_halo, grad_hidden, part2, part3)
    )
    part = jnp.concatenate([part2[:TAPS], part3[TASKS:], part2[TAPS:], part3[:TASKS]])
    part, _ = place.scatter_chips(part)
    dy1, local = call(
        functools.partial(second_back_kernel, images), "second_back",
        [
            (dv2_halo, "v"), (shared_taps, "a"), (grad_hidden, "v"), (p1, "v"), (stats1, "v"),
            (gb1, "v"), (sel1, "v"),
        ],
        [(tile1, f32), ((1, 2, DOMAINS, c), f32)],
        shift=shift2, weights=1, back=True, limit=40,
    )

    sums1 = total_sums(place, local)
    sums1, part = lax.optimization_barrier((sums1, part))
    rest_rows = gather_rows(place, part)
    (dv1,) = call(
        functools.partial(back_kernel, 0, True), "first_dv",
        [
            (dy1, "v"), (p1, "v"), (stats1, "v"), (gb1, "v"), (sums1, "v"), (sel1, "v"),
            (scal, "s"),
        ],
        [(tile1, bf16)], limit=4,
    )
    part1 = place.scatter_core(parts(place, ((0, 1, True),), images, [features], [dv1]))
    chunk1, _ = place.scatter_chips(part1)
    chunk1, dv1, p3, r0, r1, dvh0, dvh1 = lax.optimization_barrier(
        (chunk1, dv1, p3, r0, r1, dvh0, dvh1)
    )

    def own(tile, border):
        width = (breadth + 2 * border) * images
        return lax.dynamic_slice_in_dim(tile, place.rep * breadth * images, width, tile.ndim - 2)

    def pooled(value, stat, gb):
        of = jnp.tile(member, (breadth, 1))
        average = jnp.where(of[:, :1] > 0.5, stat[0, :1], stat[0, 1:])
        inverse = lax.rsqrt(jnp.where(of[:, :1] > 0.5, stat[1, :1], stat[1, 1:]) + EPSILON)
        normed = (value - average) * inverse * gb[0] + gb[1]
        out = jax.nn.silu(normed).reshape(half_h, 2, half_w, 2, images, c)
        return jnp.mean(out, axis=(1, 3)).transpose(2, 0, 1, 3).astype(bf16)

    own3 = own(p3[1:-1, images : images + rows0], 0)
    shared_out = pooled(own3, stats3[:, 0], gb3[0])
    task_out = jnp.stack([pooled(own((r0, r1)[t], 0), statsr[:, t], gbr[t]) for t in range(TASKS)])

    near = own(dv1[:, : rows0 + 2 * images], 1).reshape(height + 2, breadth + 2, images, c)
    grad_features = lax.conv_general_dilated(
        near,
        jnp.flip(shared_w[0], (0, 1)),
        (1, 1),
        "VALID",
        dimension_numbers=("HWNC", "HWOI", "HWNC"),
        preferred_element_type=f32,
    ).transpose(2, 0, 1, 3)
    grad_priors = []
    for t, dv in enumerate((dvh0, dvh1)):
        mine = own(dv[1:-1, images : images + rows0], 0)
        value = jnp.einsum("hrd,cd->hrc", mine, first_w[t, c:], preferred_element_type=f32)
        grad_priors.append(value.reshape(height, breadth, images, c).transpose(2, 0, 1, 3))

    (grad_task,) = spread(place, task_rows, 0, [TASKS * TAPS], 9)
    beside = (grad_task, shared_out, task_out, grad_features, grad_priors)
    late = (CONVS - 1) * TAPS
    if place.rows == 4 and place.cols == 8:
        beside, *swapped = place.gather_swaps(chunk1, beside)
        grad_task, shared_out, task_out, grad_features, grad_priors = beside
        grad_shared = place_swapped(place, swapped, CONVS * TAPS, 3)
    else:
        (grad_shared,) = spread(place, gather_rows(place, chunk1), 0, [TAPS], 9)
        grad_shared = jnp.pad(grad_shared, ((0, late), (0, 0), (0, 0)))
    (grad_shared,) = spread(place, rest_rows, 0, [late], 9, grad_shared)
    grad_first, grad_second = spread(place, rest_rows, late, [2 * TASKS, TASKS], 3)

    shared_sums = jnp.sum(jnp.stack([sums1[0], sums2[0], sums3[0]]), axis=2)
    task_sums = jnp.sum(jnp.stack([sums2[1:], sums3[1:], sums_r], axis=1), axis=3)
    return (
        shared_out,
        task_out,
        grad_features,
        jnp.stack(grad_priors),
        grad_shared.reshape(shared_w.shape),
        shared_sums[:, 1],
        shared_sums[:, 0],
        grad_first.reshape(first_w.shape),
        grad_second.reshape(second_w.shape),
        grad_task.reshape(task_conv.shape),
        task_sums[:, :, 1],
        task_sums[:, :, 0],
    )


def solution(mesh):
    return jax.shard_map(
        body,
        mesh=mesh,
        in_specs=(
            P(None, "row", "col", None),
            P(None, None, "row", "col", None),
            P(),
            P(),
            P(),
            P(),
            P(),
            P(),
            P(),
            P(),
            P(),
            P(None, "row", "col", None),
            P(None, None, "row", "col", None),
        ),
        out_specs=(
            P(None, "row", "col", None),
            P(None, None, "row", "col", None),
            P(None, "row", "col", None),
            P(None, None, "row", "col", None),
            P(),
            P(),
            P(),
            P(),
            P(),
            P(),
            P(),
            P(),
        ),
        check_vma=False,
    )
```

```python
import functools

import jax
import jax.numpy as jnp
from jax import lax
from jax.experimental import pallas as pl
from jax.experimental.pallas import tpu as pltpu
from jax.sharding import PartitionSpec as P

TASKS = 2
CONVS = 3
DOMAINS = 2
CORES = 2
REP = 4
TAPS = 9
LANES = 128
ROWS = 16
PAD = 16

EPSILON = 1e-05
BOTH = ("row", "col")
MIB = 1024 * 1024


class Place:
    def __init__(self):
        self.rows, self.cols = lax.axis_size("row"), lax.axis_size("col")
        self.groups = self.cols // REP
        self.row, self.col = lax.axis_index("row"), lax.axis_index("col")
        self.group, self.rep = self.col // REP, self.col % REP

    def swap(self, value, row_bits, col_bits):
        pairs = [
            (i, ((i // self.cols) ^ row_bits) * self.cols + ((i % self.cols) ^ col_bits))
            for i in range(self.rows * self.cols)
        ]
        return lax.ppermute(value, BOTH, pairs)

    def stages(self):
        bits = []
        k = 2
        while k < self.rows:
            bits.append((k, 0))
            k *= 2
        k = 1
        while k < self.groups:
            bits.append((0, k * REP))
            k *= 2
        steps = [[(1, 0)]]
        for i in range(0, len(bits), 2):
            pair = bits[i : i + 2]
            if len(pair) == 2:
                (a, b), (c, d) = pair
                pair = [(a, b), (c, d), (a ^ c, b ^ d)]
            steps.append(pair)
        return steps

    def pieces(self, tile):
        return [tile] + [self.swap(tile, 0, k) for k in range(1, REP)]

    def gather(self, tile, axis):
        return self.join(self.pieces(tile), axis)

    def join(self, pieces, axis):
        bit = 1
        while bit < REP:
            odd = (self.rep & bit) != 0
            pieces = [jnp.where(odd, pieces[j ^ bit], pieces[j]) for j in range(REP)]
            bit *= 2
        return jnp.concatenate(pieces, axis=axis)

    def halo_rows(self, low, high):
        even = self.row % 2 == 0
        near = lax.ppermute(
            jnp.where(even, high, low), "row", [(i, i ^ 1) for i in range(self.rows)]
        )
        pairs = []
        for i in range(1, self.rows - 1, 2):
            pairs += [(i, i + 1), (i + 1, i)]
        far = lax.ppermute(jnp.where(even, low, high), "row", pairs)
        return jnp.where(even, far, near), jnp.where(even, near, far)

    def halo_cols(self, low, high):
        even = self.group % 2 == 0
        near = self.swap(jnp.where(even, high, low), 0, REP)
        far = jnp.zeros_like(near)
        if self.groups > 2:
            pairs = []
            for i in range(self.cols - REP):
                if (i // REP) % 2:
                    pairs += [(i, i + REP), (i + REP, i)]
            far = lax.ppermute(jnp.where(even, low, high), "col", pairs)
        return jnp.where(even, far, near), jnp.where(even, near, far)

    def halo(self, tiles, pad, images):
        size = pad * images
        count = len(tiles)

        def columns(tiles):
            def edge(at):
                edges = [t[..., at, :].reshape(-1, size, t.shape[-1]) for t in tiles]
                extra = -(size * count) % 8
                if extra:
                    edges.append(jnp.zeros((edges[0].shape[0], extra, edges[0].shape[-1]), edges[0].dtype))
                edges = jnp.concatenate(edges, axis=1)
                return edges.reshape(-1, edges.shape[-1])

            got = self.halo_cols(edge(slice(0, size)), edge(slice(-size, None)))
            shape = tiles[0].shape
            width = -(-(size * count) // 8) * 8
            got = [x.reshape(-1, width, x.shape[-1]) for x in got]
            return [
                [x[:, t * size : (t + 1) * size].reshape(*shape[:-2], size, shape[-1]) for x in got]
                for t in range(count)
            ]

        sides = columns(tiles)
        ends = self.halo_rows(
            jnp.stack([t[..., :pad, :, :] for t in tiles]),
            jnp.stack([t[..., -pad:, :, :] for t in tiles]),
        )
        ends = [(ends[0][t], ends[1][t]) for t in range(count)]
        corners = columns([jnp.concatenate(e, axis=-3) for e in ends])
        whole = []
        for tile, (above, below), side, corner in zip(tiles, ends, sides, corners):
            tile = jnp.concatenate([above, tile, below], axis=-3)
            before, after = (
                jnp.concatenate([x[..., :pad, :, :], y, x[..., pad:, :, :]], axis=-3)
                for x, y in zip(corner, side)
            )
            fill = jnp.zeros((*tile.shape[:-2], pad * PAD - 2 * size, tile.shape[-1]), tile.dtype)
            whole.append(jnp.concatenate([before, tile, after, fill], axis=-2))
        return whole

    def scatter_core(self, parts):
        m, rows, c = parts.shape
        per = rows // (self.rows * self.groups)
        parts = parts.reshape(m, self.rows // CORES, CORES, self.groups, per, c)
        core = self.row % CORES
        other = lax.dynamic_index_in_dim(parts, 1 - core, 2, keepdims=False)
        other = self.swap(other.astype(jnp.bfloat16), 1, 0)
        mine = lax.dynamic_index_in_dim(parts, core, 2, keepdims=False)
        return mine + other.astype(jnp.float32)

    def scatter_chips(self, parts, beside=()):
        halves = self.rows // CORES
        cut = parts.shape[0] * 2 // 3

        def along_row(parts, axis=1):
            half = self.row // CORES
            got = []
            for a in range(halves):
                piece = lax.dynamic_index_in_dim(parts, half ^ a, axis, keepdims=False)
                if a:
                    piece = self.swap(piece.astype(jnp.bfloat16), a * CORES, 0)
                got.append(piece.astype(jnp.float32))
            return tree_sum(got)

        def along_col(parts, axis):
            got = []
            for b in range(self.groups):
                piece = lax.dynamic_index_in_dim(parts, self.group ^ b, axis, keepdims=False)
                if b:
                    piece = self.swap(piece.astype(jnp.bfloat16), 0, b * REP)
                got.append(piece.astype(jnp.float32))
            return tree_sum(got)

        parts = along_row(parts[:cut]), along_col(parts[cut:], 2)
        parts, beside = lax.optimization_barrier((parts, beside))
        parts = along_col(parts[0], 1), along_row(parts[1])
        return jnp.concatenate(parts).astype(jnp.bfloat16), beside

    def gather_swaps(self, chunk, early, beside):
        half = chunk.shape[-1] // 2
        line = jnp.stack([chunk, self.swap(chunk, 0, 2)])
        line, early = lax.optimization_barrier((line, early))
        line = jnp.stack([line, self.swap(line, 0, 4)])
        first, last = line[..., :half], line[..., half:]
        along_y, along_x = self.swap(first, 2, 0), self.swap(last, 0, 1)
        first, last = jnp.stack([first, along_y]), jnp.stack([last, along_x])
        along_x, along_y = self.swap(first, 0, 1), self.swap(last, 2, 0)
        first, last = jnp.stack([first, along_x]), jnp.stack([last, along_y])
        first, last, beside = lax.optimization_barrier((first, last, beside))
        return early, beside, first, self.swap(first, 1, 0), last, self.swap(last, 1, 0)


def tree_sum(values):
    while len(values) > 1:
        values = [a + b for a, b in zip(values[::2], values[1::2])]
    return values[0]


def total_stats(place, local, number):
    for step in place.stages():
        both = [local] + [place.swap(local, *bits) for bits in step]
        averages = [b[0] for b in both]
        average = tree_sum(averages) * (1.0 / len(both))
        squares = tree_sum([b[1] for b in both]) + number * tree_sum(
            [(a - average) * (a - average) for a in averages]
        )
        local = jnp.stack([average, squares])
        number = number * len(both)
    return jnp.stack([local[0], local[1] / number])


def total_sums(place, value):
    for step in place.stages():
        value = tree_sum([value] + [place.swap(value, *bits) for bits in step])
    return value


def row_blocks(i):
    return pl.ds(pl.multiple_of(i * ROWS, ROWS), ROWS)


def sweep(rows, c, setup):
    for lane in range(0, c, LANES):
        step = setup(slice(lane, lane + LANES))

        @pl.loop(0, rows // ROWS)
        def block(i):
            step(row_blocks(i))


def sweep_sums(sel_ref, rows, c, count, setup, store):
    for lane in range(0, c, LANES):
        lanes = slice(lane, lane + LANES)
        step = setup(lanes)

        def block(i, sums):
            at = row_blocks(i)
            added = []
            for j, value in enumerate(step(at)):
                for k in range(DOMAINS):
                    part = value * sel_ref[1 + k, at]
                    added.append(sums[j * DOMAINS + k] + tree_sum([part[r : r + 8] for r in range(0, ROWS, 8)]))
            return tuple(added)

        zero = jnp.zeros((8, LANES), jnp.float32)
        sums = lax.fori_loop(0, rows // ROWS, block, (zero,) * (count * DOMAINS))
        for j in range(count):
            for k in range(DOMAINS):
                store(j, k, lanes, jnp.sum(sums[j * DOMAINS + k], axis=0, keepdims=True))


def own_lines(tile_ref):
    h = tile_ref.shape[0]
    border = (h - 8) // 2
    return border, h - border


class Norm:
    def __init__(self, stat_ref, gb_ref, i, lanes):
        self.average = [stat_ref[0, i, k : k + 1, lanes] for k in range(DOMAINS)]
        self.inverse = [
            lax.rsqrt(stat_ref[1, i, k : k + 1, lanes] + EPSILON) for k in range(DOMAINS)
        ]
        self.gain = gb_ref[i, 0:1, lanes]
        self.half_gain, self.half_bias = 0.5 * self.gain, 0.5 * gb_ref[i, 1:2, lanes]
        self.lanes = lanes

    def half(self, form):
        return form * self.half_gain + self.half_bias

    def forms(self, first):
        average, inverse = jnp.where(first, *self.average), jnp.where(first, *self.inverse)
        return lambda value: (value - average) * inverse

    def halves(self, first):
        times = [inverse * self.half_gain for inverse in self.inverse]
        plus = [self.half_bias - a * t for a, t in zip(self.average, times)]
        times, plus = jnp.where(first, *times), jnp.where(first, *plus)
        return lambda value: value * times + plus

    def backs(self, first, sums_ref, scal_ref, i):
        scale = [inverse * self.gain for inverse in self.inverse]
        plain, cross = (
            [sums_ref[i, j, k : k + 1, self.lanes] * scal_ref[2 + k] for k in range(DOMAINS)]
            for j in range(2)
        )
        slant = [s * x * inverse for s, x, inverse in zip(scale, cross, self.inverse)]
        plus = [a * e - s * p for a, e, s, p in zip(self.average, slant, scale, plain)]
        scale, slant, plus = (jnp.where(first, *pair) for pair in (scale, slant, plus))
        return lambda dy, value: scale * dy + (plus - slant * value)


def is_first(sel_ref, rows):
    return sel_ref[0, rows] > 0.5


def sigmoid(t):
    return 0.5 * jnp.tanh(t) + 0.5


def silu(t):
    return t + t * jnp.tanh(t)


def silu_slope(t, h):
    return (0.5 + 0.5 * h) * (1.0 + t * (1.0 - h))


def slope(t):
    return silu_slope(t, jnp.tanh(t))


def seen(sel_ref, scal_ref, rows, lines):
    column = sel_ref[3, rows]
    return [column * scal_ref[4]] + [column] * (lines - 2) + [column * scal_ref[5]]


def local_stats(tile_ref, sel_ref, scal_ref, out_ref, i):
    _, r, c = tile_ref.shape
    lines = range(*own_lines(tile_ref))

    def total(lanes):
        return lambda rows: [tree_sum([tile_ref[h, rows, lanes] for h in lines])]

    def keep_average(_, k, lanes, value):
        out_ref[0, i, k : k + 1, lanes] = value * scal_ref[k]

    sweep_sums(sel_ref, r, c, 1, total, keep_average)

    def square(lanes):
        averages = [out_ref[0, i, k : k + 1, lanes] for k in range(DOMAINS)]

        def step(rows):
            average = jnp.where(is_first(sel_ref, rows), *averages)
            apart = [tile_ref[h, rows, lanes] - average for h in lines]
            return [tree_sum([a * a for a in apart])]

        return step

    def keep_square(_, k, lanes, value):
        out_ref[1, i, k : k + 1, lanes] = value

    sweep_sums(sel_ref, r, c, 1, square, keep_square)


def fetch(w_ref, wv_ref, sem, start, back=False):
    c = w_ref.shape[-1]
    copies = []
    for t in range(TAPS):
        part = pl.ds((t % 3) * c, c)
        if back:
            source, target = w_ref.at[start + TAPS - 1 - t], wv_ref.at[t // 3, :, part]
        else:
            source, target = w_ref.at[start + t], wv_ref.at[t // 3, part, :]
        copies.append(pltpu.make_async_copy(source, target, sem.at[t]))
        copies[-1].start()
    return copies


def convolve(x_ref, xs_ref, wv_ref, copies, o_ref, images, back=False):
    hp, rp, c = x_ref.shape
    r = rp - PAD
    m = (hp - 2) * r
    for b in range(3):
        xs_ref[:, b * c : (b + 1) * c] = x_ref[:, b * images : b * images + r, :].reshape(hp * r, c)
    for a in range(3):
        for b in range(3):
            copies[3 * a + b].wait()
        part = lax.dot_general(
            xs_ref[a * r : a * r + m, :],
            wv_ref[a],
            (((1,), (1 if back else 0,)), ((), ())),
            preferred_element_type=jnp.float32,
        ).reshape(o_ref.shape)
        o_ref[...] = part if a == 0 else o_ref[...] + part


def flat(ref):
    h, r, c = ref.shape
    return ref[...].reshape(h * r, c)


def matmul(a, b):
    return jnp.dot(a, b, preferred_element_type=jnp.float32)


def matmul_back(a, b):
    return lax.dot_general(a, b, (((1,), (1,)), ((), ())), preferred_element_type=jnp.float32)


def first_kernel(images, tap, x_ref, w_ref, sel_ref, scal_ref, p_ref, st_ref, xs_ref, wv_ref, sem):
    copies = fetch(w_ref, wv_ref, sem, tap)
    convolve(x_ref, xs_ref, wv_ref, copies, p_ref, images)
    local_stats(p_ref, sel_ref, scal_ref, st_ref, 0)


def second_kernel(
    images, p1_ref, w_ref, st1_ref, gb_ref, sel_ref, sel0_ref, scal_ref,
    act_ref, p2_ref, st_ref, xs_ref, wv_ref, sem,
):
    copies = fetch(w_ref, wv_ref, sem, TAPS)
    lines, r, c = p1_ref.shape

    def activate(lanes):
        norm = Norm(st1_ref, gb_ref, 0, lanes)

        def step(rows):
            half = norm.halves(is_first(sel_ref, rows))
            for h, inside in enumerate(seen(sel_ref, scal_ref, rows, lines)):
                act_ref[h, rows, lanes] = (silu(half(p1_ref[h, rows, lanes])) * inside).astype(
                    jnp.bfloat16
                )

        return step

    sweep(r, c, activate)
    convolve(act_ref, xs_ref, wv_ref, copies, p2_ref, images)
    local_stats(p2_ref, sel0_ref, scal_ref, st_ref, 0)


def hidden_kernel(act_ref, pr_ref, fw_ref, sel_ref, scal_ref, h0_ref, h1_ref, st_ref):
    lines, r, c = act_ref.shape
    for t, h_ref in enumerate((h0_ref, h1_ref)):
        value = matmul(flat(act_ref), fw_ref[t, :c])
        h_ref[...] = (value + matmul(pr_ref[t].reshape(lines * r, c), fw_ref[t, c:])).reshape(
            h_ref.shape
        )
        local_stats(h_ref, sel_ref, scal_ref, st_ref, t)


def act_kernel(which, p_ref, st_ref, gb_ref, sel_ref, act_ref):
    lines, r, c = p_ref.shape

    def activate(lanes):
        norm = Norm(st_ref, gb_ref, which, lanes)

        def step(rows):
            half = norm.halves(is_first(sel_ref, rows))
            for h in range(lines):
                act_ref[h, rows, lanes] = silu(half(p_ref[h, rows, lanes])).astype(jnp.bfloat16)

        return step

    sweep(r, c, activate)


def gate_kernel(
    h0_ref, h1_ref, sw_ref, st2_ref, gb_ref, sel_ref, scal_ref, a0_ref, a1_ref, g0_ref, g1_ref, st_ref,
):
    for t, (h_ref, a_ref, g_ref) in enumerate(((h0_ref, a0_ref, g0_ref), (h1_ref, a1_ref, g1_ref))):
        act_kernel(1 + t, h_ref, st2_ref, gb_ref, sel_ref, a_ref)
        g_ref[...] = matmul(flat(a_ref), sw_ref[t]).reshape(g_ref.shape)
        local_stats(g_ref, sel_ref, scal_ref, st_ref, t)


def fourth_kernel(
    images, p3_ref, g0_ref, g1_ref, w_ref, st3_ref, gb_ref, sel_ref, sel0_ref, scal_ref,
    m0_ref, m1_ref, r0_ref, r1_ref, st_ref, xs_ref, wv_ref, sem, wv2_ref, sem2,
):
    copies = [fetch(w_ref, wv_ref, sem, 0), fetch(w_ref, wv2_ref, sem2, TAPS)]
    lines, r, c = p3_ref.shape

    def mask(lanes):
        norms = [Norm(st3_ref, gb_ref, i, lanes) for i in range(1 + TASKS)]

        def step(rows):
            first = is_first(sel_ref, rows)
            half, *gates = [norm.halves(first) for norm in norms]
            for h, inside in enumerate(seen(sel_ref, scal_ref, rows, lines)):
                last = silu(half(p3_ref[h, rows, lanes])) * inside
                for gate, g_ref, m_ref in zip(gates, (g0_ref, g1_ref), (m0_ref, m1_ref)):
                    attention = sigmoid(gate(g_ref[h, rows, lanes]))
                    m_ref[h, rows, lanes] = (attention * last).astype(jnp.bfloat16)

        return step

    sweep(r, c, mask)
    convolve(m0_ref, xs_ref, wv_ref, copies[0], r0_ref, images)
    convolve(m1_ref, xs_ref, wv2_ref, copies[1], r1_ref, images)
    local_stats(r0_ref, sel0_ref, scal_ref, st_ref, 0)
    local_stats(r1_ref, sel0_ref, scal_ref, st_ref, 1)


def dy_sums(dys, forms):
    return [tree_sum(list(dys)), tree_sum([dy * form for dy, form in zip(dys, forms)])]


def keep_sums(out_ref, at):
    def store(j, k, lanes, value):
        out_ref[at + j // 2, j % 2, k : k + 1, lanes] = value

    return store


def upsample(up_ref, low_ref, out_ref):
    for h in range(low_ref.shape[0]):
        out_ref[h] = matmul(up_ref[...], low_ref[h])


def refined_sums_kernel(
    r0_ref, r1_ref, c0_ref, c1_ref, up_ref, st_ref, gb_ref, sel_ref, out_ref, dy_ref, low_ref
):
    lines, r, c = r0_ref.shape
    for t, (r_ref, c_ref) in enumerate(((r0_ref, c0_ref), (r1_ref, c1_ref))):
        upsample(up_ref, c_ref, low_ref)

        def sums(lanes):
            norm = Norm(st_ref, gb_ref, t, lanes)

            def step(rows):
                form_of = norm.forms(is_first(sel_ref, rows))
                dys, forms = [], []
                for h in range(lines):
                    forms.append(form_of(r_ref[h, rows, lanes]))
                    dys.append(low_ref[h // 2, rows, lanes] * slope(norm.half(forms[-1])))
                    dy_ref[t, h, rows, lanes] = dys[-1]
                return dy_sums(dys, forms)

            return step

        sweep_sums(sel_ref, r, c, 2, sums, keep_sums(out_ref, t))


def refined_back_kernel(
    r0_ref, r1_ref, dy_ref, st_ref, gb_ref, sums_ref, sel_ref, scal_ref, dv0_ref, dv1_ref
):
    for t, (r_ref, dv_ref) in enumerate(((r0_ref, dv0_ref), (r1_ref, dv1_ref))):
        back_kernel(
            t, False, dy_ref.at[t], r_ref, st_ref, gb_ref, sums_ref, sel_ref, scal_ref, dv_ref
        )


def conv_back_kernel(images, start, x_ref, w_ref, o_ref, xs_ref, wv_ref, sem):
    copies = fetch(w_ref, wv_ref, sem, start, True)
    convolve(x_ref, xs_ref, wv_ref, copies, o_ref, images, True)


def masked_back_kernel(
    images, dv_ref, w_ref, grad_ref, p3_ref, g0_ref, g1_ref, cot_ref, up_ref, st3_ref, gb_ref,
    sel_ref, dy3_ref, dy0_ref, dy1_ref, sums_ref, xs_ref, wv_ref, sem, low_ref,
):
    copies = fetch(w_ref, wv_ref, sem, TAPS, True)
    convolve(dv_ref, xs_ref, wv_ref, copies, dy1_ref, images, True)
    lines, r, c = p3_ref.shape
    own = slice(*own_lines(p3_ref))
    upsample(up_ref, cot_ref, low_ref)

    def setup(lanes):
        norms = [Norm(st3_ref, gb_ref, i, lanes) for i in range(1 + TASKS)]

        def step(rows):
            first = is_first(sel_ref, rows)
            form_of = [norm.forms(first) for norm in norms]
            dys, forms = [[], [], []], [[], [], []]
            for h in range(lines):
                form = form_of[0](p3_ref[h, rows, lanes])
                half = norms[0].half(form)
                tanh = jnp.tanh(half)
                last = half + half * tanh
                grad_last = low_ref[(h + 1) // 2, rows, lanes]
                for i, (g_ref, from_ref, d_ref) in enumerate(
                    ((g0_ref, grad_ref, dy0_ref), (g1_ref, dy1_ref, dy1_ref)), 1
                ):
                    gate_form = form_of[i](g_ref[h, rows, lanes])
                    attention = sigmoid(norms[i].half(gate_form))
                    grad = from_ref[h, rows, lanes] * attention
                    grad_last = grad_last + grad
                    dy = grad * last * (1.0 - attention)
                    d_ref[h, rows, lanes] = dy
                    dys[i].append(dy)
                    forms[i].append(gate_form)
                dy = grad_last * silu_slope(half, tanh)
                dy3_ref[h, rows, lanes] = dy
                dys[0].append(dy)
                forms[0].append(form)
            return [x for d, f in zip(dys, forms) for x in dy_sums(d[own], f[own])]

        return step

    sweep_sums(sel_ref, r, c, 6, setup, keep_sums(sums_ref, 0))


def slope_sums(which, out_at, grad_ref, add_ref, p_ref, st_ref, gb_ref, sel_ref, sums_ref):
    lines, r, c = p_ref.shape
    own = slice(*own_lines(p_ref))

    def setup(lanes):
        norm = Norm(st_ref, gb_ref, which, lanes)

        def step(rows):
            form_of = norm.forms(is_first(sel_ref, rows))
            dys, forms = [], []
            for h in range(lines):
                form = form_of(p_ref[h, rows, lanes])
                grad = grad_ref[h, rows, lanes]
                if add_ref is not None:
                    grad = grad + add_ref[h, rows, lanes]
                dy = grad * slope(norm.half(form))
                grad_ref[h, rows, lanes] = dy
                dys.append(dy)
                forms.append(form)
            return dy_sums(dys[own], forms[own])

        return step

    sweep_sums(sel_ref, r, c, 2, setup, keep_sums(sums_ref, out_at))


def back_kernel(which, masked, dy_ref, p_ref, st_ref, gb_ref, sums_ref, sel_ref, scal_ref, dv_ref):
    lines, r, c = p_ref.shape

    def setup(lanes):
        norm = Norm(st_ref, gb_ref, which, lanes)

        def step(rows):
            back = norm.backs(is_first(sel_ref, rows), sums_ref, scal_ref, which)
            inside = seen(sel_ref, scal_ref, rows, lines)
            for h in range(lines):
                dv = back(dy_ref[h, rows, lanes], p_ref[h, rows, lanes])
                if masked:
                    dv = dv * inside[h]
                dv_ref[h, rows, lanes] = dv.astype(jnp.bfloat16)

        return step

    sweep(r, c, setup)


def third_back_kernel(
    images, dy3_ref, p3_ref, p2_ref, w_ref, st3_ref, gb3_ref, sums_ref, st2_ref, gb2_ref,
    sel_ref, sel0_ref, scal_ref, dv3_ref, dy2_ref, out_ref, xs_ref, wv_ref, sem,
):
    copies = fetch(w_ref, wv_ref, sem, 2 * TAPS, True)
    back_kernel(0, True, dy3_ref, p3_ref, st3_ref, gb3_ref, sums_ref, sel_ref, scal_ref, dv3_ref)
    convolve(dv3_ref, xs_ref, wv_ref, copies, dy2_ref, images, True)
    slope_sums(0, 0, dy2_ref, None, p2_ref, st2_ref, gb2_ref, sel0_ref, out_ref)


def gate_back_kernel(
    dy0_ref, dy1_ref, g0_ref, g1_ref, h0_ref, h1_ref, sw_ref, st3_ref, gb3_ref, sums_ref,
    st2_ref, gb2_ref, sel_ref, scal_ref, dv0_ref, dv1_ref, dh0_ref, dh1_ref, out_ref,
):
    for t, (dy_ref, g_ref, dv_ref, h_ref, dh_ref) in enumerate(
        (
            (dy0_ref, g0_ref, dv0_ref, h0_ref, dh0_ref),
            (dy1_ref, g1_ref, dv1_ref, h1_ref, dh1_ref),
        )
    ):
        back_kernel(
            1 + t, False, dy_ref, g_ref, st3_ref, gb3_ref, sums_ref, sel_ref, scal_ref, dv_ref
        )
        dh_ref[...] = matmul_back(flat(dv_ref), sw_ref[t]).reshape(dh_ref.shape)
        slope_sums(1 + t, t, dh_ref, None, h_ref, st2_ref, gb2_ref, sel_ref, out_ref)


def hidden_back_kernel(
    dyh0_ref, dyh1_ref, h0_ref, h1_ref, fw_ref, st_ref, gb_ref, sums_ref, sel_ref, scal_ref,
    dv0_ref, dv1_ref, grad_ref,
):
    _, _, c = h0_ref.shape
    for t, (dy_ref, h_ref, dv_ref) in enumerate(
        ((dyh0_ref, h0_ref, dv0_ref), (dyh1_ref, h1_ref, dv1_ref))
    ):
        back_kernel(1 + t, False, dy_ref, h_ref, st_ref, gb_ref, sums_ref, sel_ref, scal_ref, dv_ref)
        value = matmul_back(flat(dv_ref), fw_ref[t, :c]).reshape(grad_ref.shape)
        grad_ref[...] = value if t == 0 else grad_ref[...] + value


def second_back_kernel(
    images, dv2_ref, w_ref, add_ref, p1_ref, st_ref, gb_ref, sel_ref,
    dy_ref, sums_ref, xs_ref, wv_ref, sem,
):
    copies = fetch(w_ref, wv_ref, sem, TAPS, True)
    convolve(dv2_ref, xs_ref, wv_ref, copies, dy_ref, images, True)
    slope_sums(0, 0, dy_ref, add_ref, p1_ref, st_ref, gb_ref, sel_ref, sums_ref)


def parts_kernel(plan, images, block_ref, *refs):
    *sources, out_ref, xs_ref = refs
    at = 0
    for x, g, conv in plan:
        x_ref, g_ref = sources[x], sources[g]
        border = (g_ref.shape[0] - 8) // 2
        cols = g_ref.shape[1] - border * PAD
        k = 8 * cols
        grad = g_ref[border : border + 8, border * images : border * images + cols, :]
        grad = grad.reshape(k, grad.shape[-1])
        border = (x_ref.shape[0] - 8) // 2
        taps = [(a, b) for a in (-1, 0, 1) for b in (-1, 0, 1)] if conv else [(0, 0)]
        for t, (a, b) in enumerate(taps):
            start = (border + b) * images
            xs_ref[:, t * LANES : (t + 1) * LANES] = x_ref[
                border + a : border + a + 8, start : start + cols, :
            ].reshape(k, LANES)
        size = len(taps) * LANES
        part = lax.dot_general(
            xs_ref[:, :size], grad, (((0,), (0,)), ((), ())), preferred_element_type=jnp.float32
        )
        out_ref[at : at + len(taps)] = part.reshape(len(taps), LANES, part.shape[-1])
        at += len(taps)


def parts(place, plan, images, acts, grads):
    c = grads[0].shape[-1]
    count = sum(TAPS if conv else 1 for _, _, conv in plan)

    def act_spec(x):
        return pl.BlockSpec((*x.shape[:2], LANES), lambda i, b: (0, 0, b[0]))


    return pl.pallas_call(
        functools.partial(parts_kernel, plan, images),
        out_shape=jax.ShapeDtypeStruct((count, LANES, c), jnp.float32),
        grid_spec=pltpu.PrefetchScalarGridSpec(
            num_scalar_prefetch=1,
            grid=(1,),
            in_specs=[act_spec(x) for x in acts] + [VMEM_SPEC] * len(grads),
            out_specs=VMEM_SPEC,
            scratch_shapes=[pltpu.VMEM((8 * 16 * images, TAPS * LANES), jnp.bfloat16)],
        ),
        compiler_params=pltpu.CompilerParams(vmem_limit_bytes=12 * MIB),
        name="parts",
    )(place.rep.astype(jnp.int32)[None], *acts, *grads)


def spread_kernel(groups, sources_per, skip, *refs):
    sources, targets = refs[: groups * sources_per], refs[groups * sources_per + skip :]
    at = 0
    places = [(target, i) for target in targets for i in range(target.shape[0])]
    for s in range(sources_per):
        for i in range(sources[0].shape[3]):
            target, m = places[s * sources[0].shape[3] + i]
            for g in range(groups):
                source = sources[s * groups + g]
                rows, _, _, _, per, _ = source.shape
                for r in range(rows):
                    at = (r * groups + g) * per
                    target[m, at : at + per, :] = source[r, 0, 0, i].astype(jnp.float32)


def spread(place, gathered, start, counts, step, into=None):
    rows, groups, _, _, per, c = gathered.shape
    block = rows * groups * per
    sources = 1 if len(counts) == 1 else sum(counts) // step

    def source(s, g):
        return pl.BlockSpec(
            (rows, 1, 1, step, per, c),
            lambda i, b: (0, g, b, start // step + s + i, 0, 0),
        )

    takes = [step] if len(counts) == 1 else counts
    old = [] if into is None else [into]
    at = into.shape[0] - counts[0] if old else 0
    return pl.pallas_call(
        functools.partial(spread_kernel, groups, sources, len(old)),
        out_shape=[jax.ShapeDtypeStruct((n + at, REP * block, c), jnp.float32) for n in counts],
        grid=(sum(counts) // (step * sources), REP),
        in_specs=[source(s, g) for s in range(sources) for g in range(groups)]
        + [pl.BlockSpec(memory_space=pl.ANY)] * len(old),
        out_specs=[pl.BlockSpec((n, block, c), lambda i, b: (at // step + i, b, 0)) for n in takes],
        input_output_aliases={groups * sources: 0} if old else {},
        compiler_params=pltpu.CompilerParams(vmem_limit_bytes=58 * MIB),
        cost_estimate=pl.CostEstimate(
            flops=0, bytes_accessed=6 * sum(counts) * REP * block * c, transcendentals=0
        ),
        name="spread",
    )(*([gathered] * (groups * sources)), *old)


def place_kernel(place_ref, *refs):
    *sources, target = refs
    per, half = sources[0].shape[-2:]
    row, col = place_ref[0], place_ref[1]
    for r in range(4):
        for q in range(8):
            apart_r, apart_q = r ^ row, q ^ col
            y, x, high, low = apart_r // 2, apart_q % 2, apart_q // 4, apart_q // 2 % 2
            same = apart_r % 2 == 0
            at = ((q % REP) * 8 + r * 2 + q // REP) * per
            first = jnp.where(same, sources[0][x, y, high, low], sources[1][x, y, high, low])
            last = jnp.where(same, sources[2][y, x, high, low], sources[3][y, x, high, low])
            target[:, at : at + per, :half] = first.astype(jnp.float32)
            target[:, at : at + per, half:] = last.astype(jnp.float32)


def place_swapped(place, swapped, total, step):
    m, per, half = swapped[0].shape[-3:]
    rows = place.rows * place.cols * per
    here = jnp.stack([place.row, place.col]).astype(jnp.int32)

    def source(part):
        return pl.BlockSpec(
            (*part.shape[:4], step, per, half), lambda i, here: (0, 0, 0, 0, i, 0, 0)
        )

    return pl.pallas_call(
        place_kernel,
        out_shape=jax.ShapeDtypeStruct((total, rows, 2 * half), jnp.float32),
        grid_spec=pltpu.PrefetchScalarGridSpec(
            num_scalar_prefetch=1,
            grid=(m // step,),
            in_specs=[source(p) for p in swapped],
            out_specs=pl.BlockSpec((step, rows, 2 * half), lambda i, here: (i, 0, 0)),
        ),
        compiler_params=pltpu.CompilerParams(vmem_limit_bytes=32 * MIB),
        cost_estimate=pl.CostEstimate(
            flops=0, bytes_accessed=12 * m * rows * half, transcendentals=0
        ),
        name="place",
    )(here, *swapped)


def gather_rows(place, chunk):
    whole = lax.all_gather(chunk, BOTH)
    return whole.reshape(place.rows, place.groups, REP, *chunk.shape)


VMEM_SPEC = pl.BlockSpec(memory_space=pltpu.VMEM)
SMEM_SPEC = pl.BlockSpec(memory_space=pltpu.SMEM)
HBM_SPEC = pl.BlockSpec(memory_space=pltpu.HBM)


def call(kernel, name, ins, outs, shift=None, weights=0, back=False, extra=(), limit=32):
    specs = {"v": VMEM_SPEC, "s": SMEM_SPEC, "a": HBM_SPEC}
    c = outs[0][0][-1]
    scratch = []
    if shift:
        scratch.append(pltpu.VMEM(shift, jnp.bfloat16))
    for _ in range(weights):
        taps = (3, c, 3 * c) if back else (3, 3 * c, c)
        scratch += [pltpu.VMEM(taps, jnp.bfloat16), pltpu.SemaphoreType.DMA((TAPS,))]
    scratch += [pltpu.VMEM(e, jnp.float32) for e in extra]
    return pl.pallas_call(
        kernel,
        out_shape=[jax.ShapeDtypeStruct(*o) for o in outs],
        in_specs=[specs[k] for _, k in ins],
        out_specs=[VMEM_SPEC] * len(outs),
        scratch_shapes=scratch,
        compiler_params=pltpu.CompilerParams(vmem_limit_bytes=limit * MIB),
        name=name,
    )(*[a for a, _ in ins])


def body(
    features,
    priors,
    domain,
    shared_w,
    shared_gain,
    shared_bias,
    first_w,
    second_w,
    task_conv,
    task_gain,
    task_bias,
    shared_cot,
    task_cot,
):
    place = Place()
    images, height, breadth, c = features.shape
    wide = breadth * REP
    f32, bf16 = jnp.float32, jnp.bfloat16
    member = (domain[:, None] == jnp.arange(DOMAINS, dtype=jnp.int32)[None, :]).astype(f32)
    named = jnp.sum(member, axis=0)
    number = named * (height * wide)
    counts = number * (place.rows * place.groups)
    scal = jnp.concatenate(
        [
            1.0 / number,
            1.0 / counts,
            (place.row > 0).astype(f32)[None],
            (place.row < place.rows - 1).astype(f32)[None],
        ]
    )

    rows0, rows1, rows2 = wide * images, wide * images + PAD, wide * images + 2 * PAD
    tile0, tile1, tile2 = (
        (height, rows0, c), (height + 2, rows1, c), (height + 4, rows2, c),
    )
    shift1 = ((height + 2) * rows0, 3 * c)
    shift2 = ((height + 4) * rows1, 3 * c)

    def selectors(rows, border):
        r = jnp.arange(rows)
        w, image = r // images - border, r % images
        of = member[image]
        own = ((w >= 0) & (w < wide)).astype(f32)
        col = place.group * wide + w
        seen = (col >= 0) & (col < wide * place.groups) & (w < wide + border)
        table = jnp.stack([of[:, 0], of[:, 0] * own, of[:, 1] * own, seen.astype(f32)])
        return jnp.broadcast_to(table[:, :, None], (4, rows, LANES))

    sel0, sel1 = selectors(rows0, 0), selectors(rows1, 1)
    gains = jnp.stack([shared_gain, shared_bias], axis=1)
    task_gains = jnp.stack([task_gain, task_bias], axis=2)
    gb1 = gains[0][None]
    gb2 = jnp.stack([gains[1], task_gains[0, 0], task_gains[1, 0]])
    gb3 = jnp.stack([gains[2], task_gains[0, 1], task_gains[1, 1]])
    gbr = task_gains[:, 2]
    shared_taps = shared_w.reshape(CONVS * TAPS, c, c)
    task_taps = task_conv.reshape(TASKS * TAPS, c, c)

    features = features.transpose(1, 2, 0, 3).reshape(height, breadth * images, c)
    (features,) = place.halo([place.gather(features, 1)], 2, images)
    priors = priors.transpose(0, 2, 3, 1, 4).reshape(TASKS, height, breadth * images, c)
    priors = place.pieces(priors)
    half_h, half_w = height // 2, breadth // 2

    def spreader(rows, border):
        r = jnp.arange(rows)
        source = (r // images + border) // 2 * images + r % images
        size = (REP * half_w) * images + border * PAD
        return (0.25 * (source[:, None] == jnp.arange(size)[None])).astype(bf16)

    up0, up1 = spreader(rows0, 0), spreader(rows1, 1)

    p1, local = call(
        functools.partial(first_kernel, images, 0), "first",
        [(features, "v"), (shared_taps, "a"), (sel1, "v"), (scal, "s")],
        [(tile1, f32), ((2, 1, DOMAINS, c), f32)],
        shift=shift2, weights=1, limit=46,
    )
    p1, priors = lax.optimization_barrier((p1, priors))
    (priors,) = place.halo([place.join(priors, 2)], 1, images)
    stats1 = total_stats(place, local, number[None, :, None])

    act1, p2, local = call(
        functools.partial(second_kernel, images), "second",
        [
            (p1, "v"), (shared_taps, "a"), (stats1, "v"), (gb1, "v"), (sel1, "v"), (sel0, "v"),
            (scal, "s"),
        ],
        [(tile1, bf16), (tile0, f32), ((2, 1, DOMAINS, c), f32)],
        shift=shift1, weights=1, limit=44,
    )
    h0, h1, local_h = call(
        hidden_kernel, "hidden",
        [(act1, "v"), (priors, "v"), (first_w, "v"), (sel1, "v"), (scal, "s")],
        [(tile1, f32), (tile1, f32), ((2, TASKS, DOMAINS, c), f32)], limit=12,
    )
    local = jnp.concatenate([local, local_h], axis=1)
    stats2 = total_stats(place, local, number[None, :, None])
    stats2, task_cot, shared_cot = lax.optimization_barrier((stats2, task_cot, shared_cot))
    (act2,) = call(
        functools.partial(act_kernel, 0), "act",
        [(p2, "v"), (stats2, "v"), (gb2, "v"), (sel0, "v")],
        [(tile0, bf16)], limit=4,
    )
    (act2,) = place.halo([act2], 2, images)
    act2, task_cot, shared_cot = lax.optimization_barrier((act2, task_cot, shared_cot))
    cots = jnp.concatenate([task_cot, shared_cot[None]]).transpose(0, 2, 3, 1, 4)
    cots = place.pieces(cots.reshape(TASKS + 1, half_h, half_w * images, c))
    hidden0, hidden1, g0, g1, local_g = call(
        gate_kernel, "gate",
        [
            (h0, "v"), (h1, "v"), (second_w, "v"), (stats2, "v"), (gb2, "v"), (sel1, "v"),
            (scal, "s"),
        ],
        [
            (tile1, bf16), (tile1, bf16), (tile1, f32), (tile1, f32),
            ((2, TASKS, DOMAINS, c), f32),
        ],
        limit=10,
    )

    p3, local = call(
        functools.partial(first_kernel, images, 2 * TAPS), "third",
        [(act2, "v"), (shared_taps, "a"), (sel1, "v"), (scal, "s")],
        [(tile1, f32), ((2, 1, DOMAINS, c), f32)],
        shift=shift2, weights=1, limit=46,
    )
    stats3 = total_stats(
        place, jnp.concatenate([local, local_g], axis=1), number[None, :, None]
    )

    m0, m1, r0, r1, local = call(
        functools.partial(fourth_kernel, images), "fourth",
        [
            (p3, "v"), (g0, "v"), (g1, "v"), (task_taps, "a"), (stats3, "v"), (gb3, "v"),
            (sel1, "v"), (sel0, "v"), (scal, "s"),
        ],
        [
            (tile1, bf16), (tile1, bf16), (tile0, f32), (tile0, f32),
            ((2, TASKS, DOMAINS, c), f32),
        ],
        shift=shift1, weights=2, limit=44,
    )
    local, cots = lax.optimization_barrier((local, cots))
    cots = place.join(cots, 2)
    statsr = total_stats(place, local, number[None, :, None])

    local, dy_r = call(
        refined_sums_kernel, "refined_sums",
        [
            (r0, "v"), (r1, "v"), (cots[0], "v"), (cots[1], "v"), (up0, "v"), (statsr, "v"),
            (gbr, "v"), (sel0, "v"),
        ],
        [((TASKS, 2, DOMAINS, c), f32), ((TASKS, *tile0), f32)],
        extra=[(half_h, rows0, c)], limit=6,
    )
    sums_r = total_sums(place, local)
    dv_r = call(
        refined_back_kernel, "refined_back",
        [
            (r0, "v"), (r1, "v"), (dy_r, "v"), (statsr, "v"), (gbr, "v"), (sums_r, "v"),
            (sel0, "v"), (scal, "s"),
        ],
        [(tile0, bf16), (tile0, bf16)], limit=4,
    )
    (shared_low,) = place.halo([cots[TASKS]], 1, images)
    dv_halo = place.halo(dv_r, 2, images)
    part = parts(
        place, ((0, 2, True), (1, 3, True)), images, [m0, m1], dv_r
    )
    part = place.scatter_core(part)
    dv_halo, part, shared_low = lax.optimization_barrier((dv_halo, part, shared_low))
    (grad0,) = call(
        functools.partial(conv_back_kernel, images, 0), "masked_back0",
        [(dv_halo[0], "v"), (task_taps, "a")], [(tile1, f32)],
        shift=shift2, weights=1, back=True, limit=44,
    )
    task_chunk, grad0 = place.scatter_chips(part, grad0)
    dy3, dyg0, dyg1, local = call(
        functools.partial(masked_back_kernel, images), "masked_back1",
        [
            (dv_halo[1], "v"), (task_taps, "a"), (grad0, "v"), (p3, "v"), (g0, "v"), (g1, "v"),
            (shared_low, "v"), (up1, "v"), (stats3, "v"), (gb3, "v"), (sel1, "v"),
        ],
        [(tile1, f32), (tile1, f32), (tile1, f32), ((3, 2, DOMAINS, c), f32)],
        shift=shift2, weights=1, back=True, extra=[(half_h + 2, rows1, c)], limit=40,
    )
    local, task_chunk = lax.optimization_barrier((local, task_chunk))
    task_rows = gather_rows(place, task_chunk)

    sums3 = total_sums(place, local)
    dv3, dy2, local = call(
        functools.partial(third_back_kernel, images), "third_back",
        [
            (dy3, "v"), (p3, "v"), (p2, "v"), (shared_taps, "a"), (stats3, "v"), (gb3, "v"),
            (sums3, "v"), (stats2, "v"), (gb2, "v"), (sel1, "v"), (sel0, "v"), (scal, "s"),
        ],
        [(tile1, bf16), (tile0, f32), ((1, 2, DOMAINS, c), f32)],
        shift=shift1, weights=1, back=True, limit=40,
    )
    dvg0, dvg1, dyh0, dyh1, local_h = call(
        gate_back_kernel, "gate_back",
        [
            (dyg0, "v"), (dyg1, "v"), (g0, "v"), (g1, "v"), (h0, "v"), (h1, "v"),
            (second_w, "v"), (stats3, "v"), (gb3, "v"), (sums3, "v"), (stats2, "v"), (gb2, "v"),
            (sel1, "v"), (scal, "s"),
        ],
        [
            (tile1, bf16), (tile1, bf16), (tile1, f32), (tile1, f32),
            ((TASKS, 2, DOMAINS, c), f32),
        ],
        limit=10,
    )
    part3 = parts(
        place, ((0, 3, False), (1, 4, False), (2, 5, True)), images,
        [hidden0, hidden1, act2], [dvg0, dvg1, dv3],
    )
    part3 = place.scatter_core(part3)

    sums2 = total_sums(place, jnp.concatenate([local, local_h]))
    (dv2,) = call(
        functools.partial(back_kernel, 0, False), "second_dv",
        [
            (dy2, "v"), (p2, "v"), (stats2, "v"), (gb2, "v"), (sums2, "v"), (sel0, "v"),
            (scal, "s"),
        ],
        [(tile0, bf16)], limit=4,
    )
    (dv2_halo,) = place.halo([dv2], 2, images)
    dvh0, dvh1, grad_hidden = call(
        hidden_back_kernel, "hidden_back",
        [
            (dyh0, "v"), (dyh1, "v"), (h0, "v"), (h1, "v"), (first_w, "v"), (stats2, "v"),
            (gb2, "v"), (sums2, "v"), (sel1, "v"), (scal, "s"),
        ],
        [(tile1, bf16), (tile1, bf16), (tile1, f32)], limit=10,
    )
    part2 = parts(
        place,
        ((0, 5, True), (0, 3, False), (1, 3, False), (0, 4, False), (2, 4, False)),
        images, [act1, priors[0], priors[1]], [dvh0, dvh1, dv2],
    )
    part2 = place.scatter_core(part2)
    dv2_halo, grad_hidden, part2, part3 = lax.optimization_barrier(
        (dv2_halo, grad_hidden, part2, part3)
    )
    part = jnp.concatenate([part2[:TAPS], part3[TASKS:], part2[TAPS:], part3[:TASKS]])
    part, _ = place.scatter_chips(part)
    dy1, local = call(
        functools.partial(second_back_kernel, images), "second_back",
        [
            (dv2_halo, "v"), (shared_taps, "a"), (grad_hidden, "v"), (p1, "v"), (stats1, "v"),
            (gb1, "v"), (sel1, "v"),
        ],
        [(tile1, f32), ((1, 2, DOMAINS, c), f32)],
        shift=shift2, weights=1, back=True, limit=40,
    )

    sums1 = total_sums(place, local)
    sums1, part = lax.optimization_barrier((sums1, part))
    rest_rows = gather_rows(place, part)
    (dv1,) = call(
        functools.partial(back_kernel, 0, True), "first_dv",
        [
            (dy1, "v"), (p1, "v"), (stats1, "v"), (gb1, "v"), (sums1, "v"), (sel1, "v"),
            (scal, "s"),
        ],
        [(tile1, bf16)], limit=4,
    )
    part1 = place.scatter_core(parts(place, ((0, 1, True),), images, [features], [dv1]))
    chunk1, _ = place.scatter_chips(part1)
    chunk1, dv1, p3, r0, r1, dvh0, dvh1 = lax.optimization_barrier(
        (chunk1, dv1, p3, r0, r1, dvh0, dvh1)
    )

    def own(tile, border):
        width = (breadth + 2 * border) * images
        return lax.dynamic_slice_in_dim(tile, place.rep * breadth * images, width, tile.ndim - 2)

    def pooled(value, stat, gb):
        of = jnp.tile(member, (breadth, 1))
        average = jnp.where(of[:, :1] > 0.5, stat[0, :1], stat[0, 1:])
        inverse = lax.rsqrt(jnp.where(of[:, :1] > 0.5, stat[1, :1], stat[1, 1:]) + EPSILON)
        normed = (value - average) * inverse * gb[0] + gb[1]
        out = jax.nn.silu(normed).reshape(half_h, 2, half_w, 2, images, c)
        return jnp.mean(out, axis=(1, 3)).transpose(2, 0, 1, 3).astype(bf16)

    own3 = own(p3[1:-1, images : images + rows0], 0)
    shared_out = pooled(own3, stats3[:, 0], gb3[0])
    task_out = jnp.stack([pooled(own((r0, r1)[t], 0), statsr[:, t], gbr[t]) for t in range(TASKS)])

    near = own(dv1[:, : rows0 + 2 * images], 1).reshape(height + 2, breadth + 2, images, c)
    grad_features = lax.conv_general_dilated(
        near,
        jnp.flip(shared_w[0], (0, 1)),
        (1, 1),
        "VALID",
        dimension_numbers=("HWNC", "HWOI", "HWNC"),
        preferred_element_type=f32,
    ).transpose(2, 0, 1, 3)
    grad_priors = []
    for t, dv in enumerate((dvh0, dvh1)):
        mine = own(dv[1:-1, images : images + rows0], 0)
        value = jnp.einsum("hrd,cd->hrc", mine, first_w[t, c:], preferred_element_type=f32)
        grad_priors.append(value.reshape(height, breadth, images, c).transpose(2, 0, 1, 3))

    (grad_task,) = spread(place, task_rows, 0, [TASKS * TAPS], 9)
    beside = (shared_out, task_out, grad_features, grad_priors)
    late = (CONVS - 1) * TAPS
    if place.rows == 4 and place.cols == 8:
        grad_task, beside, *swapped = place.gather_swaps(chunk1, grad_task, beside)
        shared_out, task_out, grad_features, grad_priors = beside
        grad_shared = place_swapped(place, swapped, CONVS * TAPS, 3)
    else:
        (grad_shared,) = spread(place, gather_rows(place, chunk1), 0, [TAPS], 9)
        grad_shared = jnp.pad(grad_shared, ((0, late), (0, 0), (0, 0)))
    (grad_shared,) = spread(place, rest_rows, 0, [late], 9, grad_shared)
    grad_first, grad_second = spread(place, rest_rows, late, [2 * TASKS, TASKS], 3)

    shared_sums = jnp.sum(jnp.stack([sums1[0], sums2[0], sums3[0]]), axis=2)
    task_sums = jnp.sum(jnp.stack([sums2[1:], sums3[1:], sums_r], axis=1), axis=3)
    return (
        shared_out,
        task_out,
        grad_features,
        jnp.stack(grad_priors),
        grad_shared.reshape(shared_w.shape),
        shared_sums[:, 1],
        shared_sums[:, 0],
        grad_first.reshape(first_w.shape),
        grad_second.reshape(second_w.shape),
        grad_task.reshape(task_conv.shape),
        task_sums[:, :, 1],
        task_sums[:, :, 0],
    )


def solution(mesh):
    return jax.shard_map(
        body,
        mesh=mesh,
        in_specs=(
            P(None, "row", "col", None),
            P(None, None, "row", "col", None),
            P(),
            P(),
            P(),
            P(),
            P(),
            P(),
            P(),
            P(),
            P(),
            P(None, "row", "col", None),
            P(None, None, "row", "col", None),
        ),
        out_specs=(
            P(None, "row", "col", None),
            P(None, None, "row", "col", None),
            P(None, "row", "col", None),
            P(None, None, "row", "col", None),
            P(),
            P(),
            P(),
            P(),
            P(),
            P(),
            P(),
            P(),
        ),
        check_vma=False,
    )
```

```python
import functools

import jax
import jax.numpy as jnp
from jax import lax
from jax.experimental import pallas as pl
from jax.experimental.pallas import tpu as pltpu
from jax.sharding import PartitionSpec as P

TASKS = 2
CONVS = 3
DOMAINS = 2
CORES = 2
REP = 4
TAPS = 9
LANES = 128
ROWS = 16
PAD = 16

EPSILON = 1e-05
BOTH = ("row", "col")
MIB = 1024 * 1024


class Place:
    def __init__(self):
        self.rows, self.cols = lax.axis_size("row"), lax.axis_size("col")
        self.groups = self.cols // REP
        self.row, self.col = lax.axis_index("row"), lax.axis_index("col")
        self.group, self.rep = self.col // REP, self.col % REP

    def swap(self, value, row_bits, col_bits):
        pairs = [
            (i, ((i // self.cols) ^ row_bits) * self.cols + ((i % self.cols) ^ col_bits))
            for i in range(self.rows * self.cols)
        ]
        return lax.ppermute(value, BOTH, pairs)

    def stages(self):
        bits = []
        k = 2
        while k < self.rows:
            bits.append((k, 0))
            k *= 2
        k = 1
        while k < self.groups:
            bits.append((0, k * REP))
            k *= 2
        steps = [[(1, 0)]]
        for i in range(0, len(bits), 2):
            pair = bits[i : i + 2]
            if len(pair) == 2:
                (a, b), (c, d) = pair
                pair = [(a, b), (c, d), (a ^ c, b ^ d)]
            steps.append(pair)
        return steps

    def pieces(self, tile):
        return [tile] + [self.swap(tile, 0, k) for k in range(1, REP)]

    def gather(self, tile, axis):
        return self.join(self.pieces(tile), axis)

    def join(self, pieces, axis):
        bit = 1
        while bit < REP:
            odd = (self.rep & bit) != 0
            pieces = [jnp.where(odd, pieces[j ^ bit], pieces[j]) for j in range(REP)]
            bit *= 2
        return jnp.concatenate(pieces, axis=axis)

    def halo_rows(self, low, high):
        even = self.row % 2 == 0
        near = lax.ppermute(
            jnp.where(even, high, low), "row", [(i, i ^ 1) for i in range(self.rows)]
        )
        pairs = []
        for i in range(1, self.rows - 1, 2):
            pairs += [(i, i + 1), (i + 1, i)]
        far = lax.ppermute(jnp.where(even, low, high), "row", pairs)
        return jnp.where(even, far, near), jnp.where(even, near, far)

    def halo_cols(self, low, high):
        even = self.group % 2 == 0
        near = self.swap(jnp.where(even, high, low), 0, REP)
        far = jnp.zeros_like(near)
        if self.groups > 2:
            pairs = []
            for i in range(self.cols - REP):
                if (i // REP) % 2:
                    pairs += [(i, i + REP), (i + REP, i)]
            far = lax.ppermute(jnp.where(even, low, high), "col", pairs)
        return jnp.where(even, far, near), jnp.where(even, near, far)

    def halo(self, tiles, pad, images):
        size = pad * images
        count = len(tiles)

        def columns(tiles):
            def edge(at):
                edges = [t[..., at, :].reshape(-1, size, t.shape[-1]) for t in tiles]
                extra = -(size * count) % 8
                if extra:
                    edges.append(jnp.zeros((edges[0].shape[0], extra, edges[0].shape[-1]), edges[0].dtype))
                edges = jnp.concatenate(edges, axis=1)
                return edges.reshape(-1, edges.shape[-1])

            got = self.halo_cols(edge(slice(0, size)), edge(slice(-size, None)))
            shape = tiles[0].shape
            width = -(-(size * count) // 8) * 8
            got = [x.reshape(-1, width, x.shape[-1]) for x in got]
            return [
                [x[:, t * size : (t + 1) * size].reshape(*shape[:-2], size, shape[-1]) for x in got]
                for t in range(count)
            ]

        sides = columns(tiles)
        ends = self.halo_rows(
            jnp.stack([t[..., :pad, :, :] for t in tiles]),
            jnp.stack([t[..., -pad:, :, :] for t in tiles]),
        )
        ends = [(ends[0][t], ends[1][t]) for t in range(count)]
        corners = columns([jnp.concatenate(e, axis=-3) for e in ends])
        whole = []
        for tile, (above, below), side, corner in zip(tiles, ends, sides, corners):
            tile = jnp.concatenate([above, tile, below], axis=-3)
            before, after = (
                jnp.concatenate([x[..., :pad, :, :], y, x[..., pad:, :, :]], axis=-3)
                for x, y in zip(corner, side)
            )
            fill = jnp.zeros((*tile.shape[:-2], pad * PAD - 2 * size, tile.shape[-1]), tile.dtype)
            whole.append(jnp.concatenate([before, tile, after, fill], axis=-2))
        return whole

    def scatter_core(self, parts):
        m, rows, c = parts.shape
        per = rows // (self.rows * self.groups)
        parts = parts.reshape(m, self.rows // CORES, CORES, self.groups, per, c)
        core = self.row % CORES
        other = lax.dynamic_index_in_dim(parts, 1 - core, 2, keepdims=False)
        other = self.swap(other.astype(jnp.bfloat16), 1, 0)
        mine = lax.dynamic_index_in_dim(parts, core, 2, keepdims=False)
        return mine + other.astype(jnp.float32)

    def scatter_chips(self, parts, beside=(), share=2 / 3):
        halves = self.rows // CORES
        cut = round(parts.shape[0] * share)

        def along_row(parts, axis=1):
            half = self.row // CORES
            got = []
            for a in range(halves):
                piece = lax.dynamic_index_in_dim(parts, half ^ a, axis, keepdims=False)
                if a:
                    piece = self.swap(piece.astype(jnp.bfloat16), a * CORES, 0)
                got.append(piece.astype(jnp.float32))
            return tree_sum(got)

        def along_col(parts, axis):
            got = []
            for b in range(self.groups):
                piece = lax.dynamic_index_in_dim(parts, self.group ^ b, axis, keepdims=False)
                if b:
                    piece = self.swap(piece.astype(jnp.bfloat16), 0, b * REP)
                got.append(piece.astype(jnp.float32))
            return tree_sum(got)

        parts = along_row(parts[:cut]), along_col(parts[cut:], 2)
        parts, beside = lax.optimization_barrier((parts, beside))
        parts = along_col(parts[0], 1), along_row(parts[1])
        return jnp.concatenate(parts).astype(jnp.bfloat16), beside

    def gather_swaps(self, chunk, early, beside):
        half = chunk.shape[-1] // 2
        line = jnp.stack([chunk, self.swap(chunk, 0, 2)])
        line, early = lax.optimization_barrier((line, early))
        line = jnp.stack([line, self.swap(line, 0, 4)])
        first, last = line[..., :half], line[..., half:]
        along_y, along_x = self.swap(first, 2, 0), self.swap(last, 0, 1)
        first, last = jnp.stack([first, along_y]), jnp.stack([last, along_x])
        along_x, along_y = self.swap(first, 0, 1), self.swap(last, 2, 0)
        first, last = jnp.stack([first, along_x]), jnp.stack([last, along_y])
        first, last, beside = lax.optimization_barrier((first, last, beside))
        return early, beside, first, self.swap(first, 1, 0), last, self.swap(last, 1, 0)


def tree_sum(values):
    while len(values) > 1:
        values = [a + b for a, b in zip(values[::2], values[1::2])]
    return values[0]


def total_stats(place, local, number):
    for step in place.stages():
        both = [local] + [place.swap(local, *bits) for bits in step]
        averages = [b[0] for b in both]
        average = tree_sum(averages) * (1.0 / len(both))
        squares = tree_sum([b[1] for b in both]) + number * tree_sum(
            [(a - average) * (a - average) for a in averages]
        )
        local = jnp.stack([average, squares])
        number = number * len(both)
    return jnp.stack([local[0], local[1] / number])


def total_sums(place, value):
    for step in place.stages():
        value = tree_sum([value] + [place.swap(value, *bits) for bits in step])
    return value


def row_blocks(i):
    return pl.ds(pl.multiple_of(i * ROWS, ROWS), ROWS)


def sweep(rows, c, setup):
    for lane in range(0, c, LANES):
        step = setup(slice(lane, lane + LANES))

        @pl.loop(0, rows // ROWS)
        def block(i):
            step(row_blocks(i))


def sweep_sums(sel_ref, rows, c, count, setup, store):
    for lane in range(0, c, LANES):
        lanes = slice(lane, lane + LANES)
        step = setup(lanes)

        def block(i, sums):
            at = row_blocks(i)
            added = []
            for j, value in enumerate(step(at)):
                for k in range(DOMAINS):
                    part = value * sel_ref[1 + k, at]
                    added.append(sums[j * DOMAINS + k] + tree_sum([part[r : r + 8] for r in range(0, ROWS, 8)]))
            return tuple(added)

        zero = jnp.zeros((8, LANES), jnp.float32)
        sums = lax.fori_loop(0, rows // ROWS, block, (zero,) * (count * DOMAINS))
        for j in range(count):
            for k in range(DOMAINS):
                store(j, k, lanes, jnp.sum(sums[j * DOMAINS + k], axis=0, keepdims=True))


def own_lines(tile_ref):
    h = tile_ref.shape[0]
    border = (h - 8) // 2
    return border, h - border


class Norm:
    def __init__(self, stat_ref, gb_ref, i, lanes):
        self.average = [stat_ref[0, i, k : k + 1, lanes] for k in range(DOMAINS)]
        self.inverse = [
            lax.rsqrt(stat_ref[1, i, k : k + 1, lanes] + EPSILON) for k in range(DOMAINS)
        ]
        self.gain = gb_ref[i, 0:1, lanes]
        self.half_gain, self.half_bias = 0.5 * self.gain, 0.5 * gb_ref[i, 1:2, lanes]
        self.lanes = lanes

    def half(self, form):
        return form * self.half_gain + self.half_bias

    def forms(self, first):
        average, inverse = jnp.where(first, *self.average), jnp.where(first, *self.inverse)
        return lambda value: (value - average) * inverse

    def halves(self, first):
        times = [inverse * self.half_gain for inverse in self.inverse]
        plus = [self.half_bias - a * t for a, t in zip(self.average, times)]
        times, plus = jnp.where(first, *times), jnp.where(first, *plus)
        return lambda value: value * times + plus

    def backs(self, first, sums_ref, scal_ref, i):
        scale = [inverse * self.gain for inverse in self.inverse]
        plain, cross = (
            [sums_ref[i, j, k : k + 1, self.lanes] * scal_ref[2 + k] for k in range(DOMAINS)]
            for j in range(2)
        )
        slant = [s * x * inverse for s, x, inverse in zip(scale, cross, self.inverse)]
        plus = [a * e - s * p for a, e, s, p in zip(self.average, slant, scale, plain)]
        scale, slant, plus = (jnp.where(first, *pair) for pair in (scale, slant, plus))
        return lambda dy, value: scale * dy + (plus - slant * value)


def is_first(sel_ref, rows):
    return sel_ref[0, rows] > 0.5


def sigmoid(t):
    return 0.5 * jnp.tanh(t) + 0.5


def silu(t):
    return t + t * jnp.tanh(t)


def silu_slope(t, h):
    return (0.5 + 0.5 * h) * (1.0 + t * (1.0 - h))


def slope(t):
    return silu_slope(t, jnp.tanh(t))


def seen(sel_ref, scal_ref, rows, lines):
    column = sel_ref[3, rows]
    return [column * scal_ref[4]] + [column] * (lines - 2) + [column * scal_ref[5]]


def local_stats(tile_ref, sel_ref, scal_ref, out_ref, i):
    _, r, c = tile_ref.shape
    lines = range(*own_lines(tile_ref))

    def total(lanes):
        return lambda rows: [tree_sum([tile_ref[h, rows, lanes] for h in lines])]

    def keep_average(_, k, lanes, value):
        out_ref[0, i, k : k + 1, lanes] = value * scal_ref[k]

    sweep_sums(sel_ref, r, c, 1, total, keep_average)

    def square(lanes):
        averages = [out_ref[0, i, k : k + 1, lanes] for k in range(DOMAINS)]

        def step(rows):
            average = jnp.where(is_first(sel_ref, rows), *averages)
            apart = [tile_ref[h, rows, lanes] - average for h in lines]
            return [tree_sum([a * a for a in apart])]

        return step

    def keep_square(_, k, lanes, value):
        out_ref[1, i, k : k + 1, lanes] = value

    sweep_sums(sel_ref, r, c, 1, square, keep_square)


def fetch(w_ref, wv_ref, sem, start, back=False):
    c = w_ref.shape[-1]
    copies = []
    for t in range(TAPS):
        part = pl.ds((t % 3) * c, c)
        if back:
            source, target = w_ref.at[start + TAPS - 1 - t], wv_ref.at[t // 3, :, part]
        else:
            source, target = w_ref.at[start + t], wv_ref.at[t // 3, part, :]
        copies.append(pltpu.make_async_copy(source, target, sem.at[t]))
        copies[-1].start()
    return copies


def convolve(x_ref, xs_ref, wv_ref, copies, o_ref, images, back=False):
    hp, rp, c = x_ref.shape
    r = rp - PAD
    m = (hp - 2) * r
    for b in range(3):
        xs_ref[:, b * c : (b + 1) * c] = x_ref[:, b * images : b * images + r, :].reshape(hp * r, c)
    for a in range(3):
        for b in range(3):
            copies[3 * a + b].wait()
        part = lax.dot_general(
            xs_ref[a * r : a * r + m, :],
            wv_ref[a],
            (((1,), (1 if back else 0,)), ((), ())),
            preferred_element_type=jnp.float32,
        ).reshape(o_ref.shape)
        o_ref[...] = part if a == 0 else o_ref[...] + part


def flat(ref):
    h, r, c = ref.shape
    return ref[...].reshape(h * r, c)


def matmul(a, b):
    return jnp.dot(a, b, preferred_element_type=jnp.float32)


def matmul_back(a, b):
    return lax.dot_general(a, b, (((1,), (1,)), ((), ())), preferred_element_type=jnp.float32)


def first_kernel(images, tap, x_ref, w_ref, sel_ref, scal_ref, p_ref, st_ref, xs_ref, wv_ref, sem):
    copies = fetch(w_ref, wv_ref, sem, tap)
    convolve(x_ref, xs_ref, wv_ref, copies, p_ref, images)
    local_stats(p_ref, sel_ref, scal_ref, st_ref, 0)


def second_kernel(
    images, p1_ref, w_ref, st1_ref, gb_ref, sel_ref, sel0_ref, scal_ref,
    act_ref, p2_ref, st_ref, xs_ref, wv_ref, sem,
):
    copies = fetch(w_ref, wv_ref, sem, TAPS)
    lines, r, c = p1_ref.shape

    def activate(lanes):
        norm = Norm(st1_ref, gb_ref, 0, lanes)

        def step(rows):
            half = norm.halves(is_first(sel_ref, rows))
            for h, inside in enumerate(seen(sel_ref, scal_ref, rows, lines)):
                act_ref[h, rows, lanes] = (silu(half(p1_ref[h, rows, lanes])) * inside).astype(
                    jnp.bfloat16
                )

        return step

    sweep(r, c, activate)
    convolve(act_ref, xs_ref, wv_ref, copies, p2_ref, images)
    local_stats(p2_ref, sel0_ref, scal_ref, st_ref, 0)


def hidden_kernel(act_ref, pr_ref, fw_ref, sel_ref, scal_ref, h0_ref, h1_ref, st_ref):
    lines, r, c = act_ref.shape
    for t, h_ref in enumerate((h0_ref, h1_ref)):
        value = matmul(flat(act_ref), fw_ref[t, :c])
        h_ref[...] = (value + matmul(pr_ref[t].reshape(lines * r, c), fw_ref[t, c:])).reshape(
            h_ref.shape
        )
        local_stats(h_ref, sel_ref, scal_ref, st_ref, t)


def act_kernel(which, p_ref, st_ref, gb_ref, sel_ref, act_ref):
    lines, r, c = p_ref.shape

    def activate(lanes):
        norm = Norm(st_ref, gb_ref, which, lanes)

        def step(rows):
            half = norm.halves(is_first(sel_ref, rows))
            for h in range(lines):
                act_ref[h, rows, lanes] = silu(half(p_ref[h, rows, lanes])).astype(jnp.bfloat16)

        return step

    sweep(r, c, activate)


def gate_kernel(
    h0_ref, h1_ref, sw_ref, st2_ref, gb_ref, sel_ref, scal_ref, a0_ref, a1_ref, g0_ref, g1_ref, st_ref,
):
    for t, (h_ref, a_ref, g_ref) in enumerate(((h0_ref, a0_ref, g0_ref), (h1_ref, a1_ref, g1_ref))):
        act_kernel(1 + t, h_ref, st2_ref, gb_ref, sel_ref, a_ref)
        g_ref[...] = matmul(flat(a_ref), sw_ref[t]).reshape(g_ref.shape)
        local_stats(g_ref, sel_ref, scal_ref, st_ref, t)


def fourth_kernel(
    images, p3_ref, g0_ref, g1_ref, w_ref, st3_ref, gb_ref, sel_ref, sel0_ref, scal_ref,
    m0_ref, m1_ref, r0_ref, r1_ref, st_ref, xs_ref, wv_ref, sem, wv2_ref, sem2,
):
    copies = [fetch(w_ref, wv_ref, sem, 0), fetch(w_ref, wv2_ref, sem2, TAPS)]
    lines, r, c = p3_ref.shape

    def mask(lanes):
        norms = [Norm(st3_ref, gb_ref, i, lanes) for i in range(1 + TASKS)]

        def step(rows):
            first = is_first(sel_ref, rows)
            half, *gates = [norm.halves(first) for norm in norms]
            for h, inside in enumerate(seen(sel_ref, scal_ref, rows, lines)):
                last = silu(half(p3_ref[h, rows, lanes])) * inside
                for gate, g_ref, m_ref in zip(gates, (g0_ref, g1_ref), (m0_ref, m1_ref)):
                    attention = sigmoid(gate(g_ref[h, rows, lanes]))
                    m_ref[h, rows, lanes] = (attention * last).astype(jnp.bfloat16)

        return step

    sweep(r, c, mask)
    convolve(m0_ref, xs_ref, wv_ref, copies[0], r0_ref, images)
    convolve(m1_ref, xs_ref, wv2_ref, copies[1], r1_ref, images)
    local_stats(r0_ref, sel0_ref, scal_ref, st_ref, 0)
    local_stats(r1_ref, sel0_ref, scal_ref, st_ref, 1)


def dy_sums(dys, forms):
    return [tree_sum(list(dys)), tree_sum([dy * form for dy, form in zip(dys, forms)])]


def keep_sums(out_ref, at):
    def store(j, k, lanes, value):
        out_ref[at + j // 2, j % 2, k : k + 1, lanes] = value

    return store


def upsample(up_ref, low_ref, out_ref):
    for h in range(low_ref.shape[0]):
        out_ref[h] = matmul(up_ref[...], low_ref[h])


def refined_sums_kernel(
    r0_ref, r1_ref, c0_ref, c1_ref, up_ref, st_ref, gb_ref, sel_ref, out_ref, dy_ref, low_ref
):
    lines, r, c = r0_ref.shape
    for t, (r_ref, c_ref) in enumerate(((r0_ref, c0_ref), (r1_ref, c1_ref))):
        upsample(up_ref, c_ref, low_ref)

        def sums(lanes):
            norm = Norm(st_ref, gb_ref, t, lanes)

            def step(rows):
                form_of = norm.forms(is_first(sel_ref, rows))
                dys, forms = [], []
                for h in range(lines):
                    forms.append(form_of(r_ref[h, rows, lanes]))
                    dys.append(low_ref[h // 2, rows, lanes] * slope(norm.half(forms[-1])))
                    dy_ref[t, h, rows, lanes] = dys[-1]
                return dy_sums(dys, forms)

            return step

        sweep_sums(sel_ref, r, c, 2, sums, keep_sums(out_ref, t))


def refined_back_kernel(
    r0_ref, r1_ref, dy_ref, st_ref, gb_ref, sums_ref, sel_ref, scal_ref, dv0_ref, dv1_ref
):
    for t, (r_ref, dv_ref) in enumerate(((r0_ref, dv0_ref), (r1_ref, dv1_ref))):
        back_kernel(
            t, False, dy_ref.at[t], r_ref, st_ref, gb_ref, sums_ref, sel_ref, scal_ref, dv_ref
        )


def conv_back_kernel(images, start, x_ref, w_ref, o_ref, xs_ref, wv_ref, sem):
    copies = fetch(w_ref, wv_ref, sem, start, True)
    convolve(x_ref, xs_ref, wv_ref, copies, o_ref, images, True)


def masked_back_kernel(
    images, dv_ref, w_ref, grad_ref, p3_ref, g0_ref, g1_ref, cot_ref, up_ref, st3_ref, gb_ref,
    sel_ref, dy3_ref, dy0_ref, dy1_ref, sums_ref, xs_ref, wv_ref, sem, low_ref,
):
    copies = fetch(w_ref, wv_ref, sem, TAPS, True)
    convolve(dv_ref, xs_ref, wv_ref, copies, dy1_ref, images, True)
    lines, r, c = p3_ref.shape
    own = slice(*own_lines(p3_ref))
    upsample(up_ref, cot_ref, low_ref)

    def setup(lanes):
        norms = [Norm(st3_ref, gb_ref, i, lanes) for i in range(1 + TASKS)]

        def step(rows):
            first = is_first(sel_ref, rows)
            form_of = [norm.forms(first) for norm in norms]
            dys, forms = [[], [], []], [[], [], []]
            for h in range(lines):
                form = form_of[0](p3_ref[h, rows, lanes])
                half = norms[0].half(form)
                tanh = jnp.tanh(half)
                last = half + half * tanh
                grad_last = low_ref[(h + 1) // 2, rows, lanes]
                for i, (g_ref, from_ref, d_ref) in enumerate(
                    ((g0_ref, grad_ref, dy0_ref), (g1_ref, dy1_ref, dy1_ref)), 1
                ):
                    gate_form = form_of[i](g_ref[h, rows, lanes])
                    attention = sigmoid(norms[i].half(gate_form))
                    grad = from_ref[h, rows, lanes] * attention
                    grad_last = grad_last + grad
                    dy = grad * last * (1.0 - attention)
                    d_ref[h, rows, lanes] = dy
                    dys[i].append(dy)
                    forms[i].append(gate_form)
                dy = grad_last * silu_slope(half, tanh)
                dy3_ref[h, rows, lanes] = dy
                dys[0].append(dy)
                forms[0].append(form)
            return [x for d, f in zip(dys, forms) for x in dy_sums(d[own], f[own])]

        return step

    sweep_sums(sel_ref, r, c, 6, setup, keep_sums(sums_ref, 0))


def slope_sums(which, out_at, grad_ref, add_ref, p_ref, st_ref, gb_ref, sel_ref, sums_ref):
    lines, r, c = p_ref.shape
    own = slice(*own_lines(p_ref))

    def setup(lanes):
        norm = Norm(st_ref, gb_ref, which, lanes)

        def step(rows):
            form_of = norm.forms(is_first(sel_ref, rows))
            dys, forms = [], []
            for h in range(lines):
                form = form_of(p_ref[h, rows, lanes])
                grad = grad_ref[h, rows, lanes]
                if add_ref is not None:
                    grad = grad + add_ref[h, rows, lanes]
                dy = grad * slope(norm.half(form))
                grad_ref[h, rows, lanes] = dy
                dys.append(dy)
                forms.append(form)
            return dy_sums(dys[own], forms[own])

        return step

    sweep_sums(sel_ref, r, c, 2, setup, keep_sums(sums_ref, out_at))


def back_kernel(which, masked, dy_ref, p_ref, st_ref, gb_ref, sums_ref, sel_ref, scal_ref, dv_ref):
    lines, r, c = p_ref.shape

    def setup(lanes):
        norm = Norm(st_ref, gb_ref, which, lanes)

        def step(rows):
            back = norm.backs(is_first(sel_ref, rows), sums_ref, scal_ref, which)
            inside = seen(sel_ref, scal_ref, rows, lines)
            for h in range(lines):
                dv = back(dy_ref[h, rows, lanes], p_ref[h, rows, lanes])
                if masked:
                    dv = dv * inside[h]
                dv_ref[h, rows, lanes] = dv.astype(jnp.bfloat16)

        return step

    sweep(r, c, setup)


def third_back_kernel(
    images, dy3_ref, p3_ref, p2_ref, w_ref, st3_ref, gb3_ref, sums_ref, st2_ref, gb2_ref,
    sel_ref, sel0_ref, scal_ref, dv3_ref, dy2_ref, out_ref, xs_ref, wv_ref, sem,
):
    copies = fetch(w_ref, wv_ref, sem, 2 * TAPS, True)
    back_kernel(0, True, dy3_ref, p3_ref, st3_ref, gb3_ref, sums_ref, sel_ref, scal_ref, dv3_ref)
    convolve(dv3_ref, xs_ref, wv_ref, copies, dy2_ref, images, True)
    slope_sums(0, 0, dy2_ref, None, p2_ref, st2_ref, gb2_ref, sel0_ref, out_ref)


def gate_back_kernel(
    dy0_ref, dy1_ref, g0_ref, g1_ref, h0_ref, h1_ref, sw_ref, st3_ref, gb3_ref, sums_ref,
    st2_ref, gb2_ref, sel_ref, scal_ref, dv0_ref, dv1_ref, dh0_ref, dh1_ref, out_ref,
):
    for t, (dy_ref, g_ref, dv_ref, h_ref, dh_ref) in enumerate(
        (
            (dy0_ref, g0_ref, dv0_ref, h0_ref, dh0_ref),
            (dy1_ref, g1_ref, dv1_ref, h1_ref, dh1_ref),
        )
    ):
        back_kernel(
            1 + t, False, dy_ref, g_ref, st3_ref, gb3_ref, sums_ref, sel_ref, scal_ref, dv_ref
        )
        dh_ref[...] = matmul_back(flat(dv_ref), sw_ref[t]).reshape(dh_ref.shape)
        slope_sums(1 + t, t, dh_ref, None, h_ref, st2_ref, gb2_ref, sel_ref, out_ref)


def hidden_back_kernel(
    dyh0_ref, dyh1_ref, h0_ref, h1_ref, fw_ref, st_ref, gb_ref, sums_ref, sel_ref, scal_ref,
    dv0_ref, dv1_ref, grad_ref,
):
    _, _, c = h0_ref.shape
    for t, (dy_ref, h_ref, dv_ref) in enumerate(
        ((dyh0_ref, h0_ref, dv0_ref), (dyh1_ref, h1_ref, dv1_ref))
    ):
        back_kernel(1 + t, False, dy_ref, h_ref, st_ref, gb_ref, sums_ref, sel_ref, scal_ref, dv_ref)
        value = matmul_back(flat(dv_ref), fw_ref[t, :c]).reshape(grad_ref.shape)
        grad_ref[...] = value if t == 0 else grad_ref[...] + value


def second_back_kernel(
    images, dv2_ref, w_ref, add_ref, p1_ref, st_ref, gb_ref, sel_ref,
    dy_ref, sums_ref, xs_ref, wv_ref, sem,
):
    copies = fetch(w_ref, wv_ref, sem, TAPS, True)
    convolve(dv2_ref, xs_ref, wv_ref, copies, dy_ref, images, True)
    slope_sums(0, 0, dy_ref, add_ref, p1_ref, st_ref, gb_ref, sel_ref, sums_ref)


def parts_kernel(plan, images, block_ref, *refs):
    *sources, out_ref, xs_ref = refs
    at = 0
    for x, g, conv in plan:
        x_ref, g_ref = sources[x], sources[g]
        border = (g_ref.shape[0] - 8) // 2
        cols = g_ref.shape[1] - border * PAD
        k = 8 * cols
        grad = g_ref[border : border + 8, border * images : border * images + cols, :]
        grad = grad.reshape(k, grad.shape[-1])
        border = (x_ref.shape[0] - 8) // 2
        taps = [(a, b) for a in (-1, 0, 1) for b in (-1, 0, 1)] if conv else [(0, 0)]
        for t, (a, b) in enumerate(taps):
            start = (border + b) * images
            xs_ref[:, t * LANES : (t + 1) * LANES] = x_ref[
                border + a : border + a + 8, start : start + cols, :
            ].reshape(k, LANES)
        size = len(taps) * LANES
        part = lax.dot_general(
            xs_ref[:, :size], grad, (((0,), (0,)), ((), ())), preferred_element_type=jnp.float32
        )
        out_ref[at : at + len(taps)] = part.reshape(len(taps), LANES, part.shape[-1])
        at += len(taps)


def parts(place, plan, images, acts, grads):
    c = grads[0].shape[-1]
    count = sum(TAPS if conv else 1 for _, _, conv in plan)

    def act_spec(x):
        return pl.BlockSpec((*x.shape[:2], LANES), lambda i, b: (0, 0, b[0]))


    return pl.pallas_call(
        functools.partial(parts_kernel, plan, images),
        out_shape=jax.ShapeDtypeStruct((count, LANES, c), jnp.float32),
        grid_spec=pltpu.PrefetchScalarGridSpec(
            num_scalar_prefetch=1,
            grid=(1,),
            in_specs=[act_spec(x) for x in acts] + [VMEM_SPEC] * len(grads),
            out_specs=VMEM_SPEC,
            scratch_shapes=[pltpu.VMEM((8 * 16 * images, TAPS * LANES), jnp.bfloat16)],
        ),
        compiler_params=pltpu.CompilerParams(vmem_limit_bytes=12 * MIB),
        name="parts",
    )(place.rep.astype(jnp.int32)[None], *acts, *grads)


def spread_kernel(groups, sources_per, skip, *refs):
    sources, targets = refs[: groups * sources_per], refs[groups * sources_per + skip :]
    at = 0
    places = [(target, i) for target in targets for i in range(target.shape[0])]
    for s in range(sources_per):
        for i in range(sources[0].shape[3]):
            target, m = places[s * sources[0].shape[3] + i]
            for g in range(groups):
                source = sources[s * groups + g]
                rows, _, _, _, per, _ = source.shape
                for r in range(rows):
                    at = (r * groups + g) * per
                    target[m, at : at + per, :] = source[r, 0, 0, i].astype(jnp.float32)


def spread(place, gathered, start, counts, step, into=None):
    rows, groups, _, _, per, c = gathered.shape
    block = rows * groups * per
    sources = 1 if len(counts) == 1 else sum(counts) // step

    def source(s, g):
        return pl.BlockSpec(
            (rows, 1, 1, step, per, c),
            lambda i, b: (0, g, b, start // step + s + i, 0, 0),
        )

    takes = [step] if len(counts) == 1 else counts
    old = [] if into is None else [into]
    at = into.shape[0] - counts[0] if old else 0
    return pl.pallas_call(
        functools.partial(spread_kernel, groups, sources, len(old)),
        out_shape=[jax.ShapeDtypeStruct((n + at, REP * block, c), jnp.float32) for n in counts],
        grid=(sum(counts) // (step * sources), REP),
        in_specs=[source(s, g) for s in range(sources) for g in range(groups)]
        + [pl.BlockSpec(memory_space=pl.ANY)] * len(old),
        out_specs=[pl.BlockSpec((n, block, c), lambda i, b: (at // step + i, b, 0)) for n in takes],
        input_output_aliases={groups * sources: 0} if old else {},
        compiler_params=pltpu.CompilerParams(vmem_limit_bytes=58 * MIB),
        cost_estimate=pl.CostEstimate(
            flops=0, bytes_accessed=6 * sum(counts) * REP * block * c, transcendentals=0
        ),
        name="spread",
    )(*([gathered] * (groups * sources)), *old)


def place_kernel(place_ref, *refs):
    *sources, target = refs
    per, half = sources[0].shape[-2:]
    row, col = place_ref[0], place_ref[1]
    for r in range(4):
        for q in range(8):
            apart_r, apart_q = r ^ row, q ^ col
            y, x, high, low = apart_r // 2, apart_q % 2, apart_q // 4, apart_q // 2 % 2
            same = apart_r % 2 == 0
            at = ((q % REP) * 8 + r * 2 + q // REP) * per
            first = jnp.where(same, sources[0][x, y, high, low], sources[1][x, y, high, low])
            last = jnp.where(same, sources[2][y, x, high, low], sources[3][y, x, high, low])
            target[:, at : at + per, :half] = first.astype(jnp.float32)
            target[:, at : at + per, half:] = last.astype(jnp.float32)


def place_swapped(place, swapped, total, step):
    m, per, half = swapped[0].shape[-3:]
    rows = place.rows * place.cols * per
    here = jnp.stack([place.row, place.col]).astype(jnp.int32)

    def source(part):
        return pl.BlockSpec(
            (*part.shape[:4], step, per, half), lambda i, here: (0, 0, 0, 0, i, 0, 0)
        )

    return pl.pallas_call(
        place_kernel,
        out_shape=jax.ShapeDtypeStruct((total, rows, 2 * half), jnp.float32),
        grid_spec=pltpu.PrefetchScalarGridSpec(
            num_scalar_prefetch=1,
            grid=(m // step,),
            in_specs=[source(p) for p in swapped],
            out_specs=pl.BlockSpec((step, rows, 2 * half), lambda i, here: (i, 0, 0)),
        ),
        compiler_params=pltpu.CompilerParams(vmem_limit_bytes=32 * MIB),
        cost_estimate=pl.CostEstimate(
            flops=0, bytes_accessed=12 * m * rows * half, transcendentals=0
        ),
        name="place",
    )(here, *swapped)


def gather_rows(place, chunk):
    whole = lax.all_gather(chunk, BOTH)
    return whole.reshape(place.rows, place.groups, REP, *chunk.shape)


VMEM_SPEC = pl.BlockSpec(memory_space=pltpu.VMEM)
SMEM_SPEC = pl.BlockSpec(memory_space=pltpu.SMEM)
HBM_SPEC = pl.BlockSpec(memory_space=pltpu.HBM)


def call(kernel, name, ins, outs, shift=None, weights=0, back=False, extra=(), limit=32):
    specs = {"v": VMEM_SPEC, "s": SMEM_SPEC, "a": HBM_SPEC}
    c = outs[0][0][-1]
    scratch = []
    if shift:
        scratch.append(pltpu.VMEM(shift, jnp.bfloat16))
    for _ in range(weights):
        taps = (3, c, 3 * c) if back else (3, 3 * c, c)
        scratch += [pltpu.VMEM(taps, jnp.bfloat16), pltpu.SemaphoreType.DMA((TAPS,))]
    scratch += [pltpu.VMEM(e, jnp.float32) for e in extra]
    return pl.pallas_call(
        kernel,
        out_shape=[jax.ShapeDtypeStruct(*o) for o in outs],
        in_specs=[specs[k] for _, k in ins],
        out_specs=[VMEM_SPEC] * len(outs),
        scratch_shapes=scratch,
        compiler_params=pltpu.CompilerParams(vmem_limit_bytes=limit * MIB),
        name=name,
    )(*[a for a, _ in ins])


def body(
    features,
    priors,
    domain,
    shared_w,
    shared_gain,
    shared_bias,
    first_w,
    second_w,
    task_conv,
    task_gain,
    task_bias,
    shared_cot,
    task_cot,
):
    place = Place()
    images, height, breadth, c = features.shape
    wide = breadth * REP
    f32, bf16 = jnp.float32, jnp.bfloat16
    member = (domain[:, None] == jnp.arange(DOMAINS, dtype=jnp.int32)[None, :]).astype(f32)
    named = jnp.sum(member, axis=0)
    number = named * (height * wide)
    counts = number * (place.rows * place.groups)
    scal = jnp.concatenate(
        [
            1.0 / number,
            1.0 / counts,
            (place.row > 0).astype(f32)[None],
            (place.row < place.rows - 1).astype(f32)[None],
        ]
    )

    rows0, rows1, rows2 = wide * images, wide * images + PAD, wide * images + 2 * PAD
    tile0, tile1, tile2 = (
        (height, rows0, c), (height + 2, rows1, c), (height + 4, rows2, c),
    )
    shift1 = ((height + 2) * rows0, 3 * c)
    shift2 = ((height + 4) * rows1, 3 * c)

    def selectors(rows, border):
        r = jnp.arange(rows)
        w, image = r // images - border, r % images
        of = member[image]
        own = ((w >= 0) & (w < wide)).astype(f32)
        col = place.group * wide + w
        seen = (col >= 0) & (col < wide * place.groups) & (w < wide + border)
        table = jnp.stack([of[:, 0], of[:, 0] * own, of[:, 1] * own, seen.astype(f32)])
        return jnp.broadcast_to(table[:, :, None], (4, rows, LANES))

    sel0, sel1 = selectors(rows0, 0), selectors(rows1, 1)
    gains = jnp.stack([shared_gain, shared_bias], axis=1)
    task_gains = jnp.stack([task_gain, task_bias], axis=2)
    gb1 = gains[0][None]
    gb2 = jnp.stack([gains[1], task_gains[0, 0], task_gains[1, 0]])
    gb3 = jnp.stack([gains[2], task_gains[0, 1], task_gains[1, 1]])
    gbr = task_gains[:, 2]
    shared_taps = shared_w.reshape(CONVS * TAPS, c, c)
    task_taps = task_conv.reshape(TASKS * TAPS, c, c)

    features = features.transpose(1, 2, 0, 3).reshape(height, breadth * images, c)
    (features,) = place.halo([place.gather(features, 1)], 2, images)
    priors = priors.transpose(0, 2, 3, 1, 4).reshape(TASKS, height, breadth * images, c)
    priors = place.pieces(priors)
    half_h, half_w = height // 2, breadth // 2

    def spreader(rows, border):
        r = jnp.arange(rows)
        source = (r // images + border) // 2 * images + r % images
        size = (REP * half_w) * images + border * PAD
        return (0.25 * (source[:, None] == jnp.arange(size)[None])).astype(bf16)

    up0, up1 = spreader(rows0, 0), spreader(rows1, 1)

    p1, local = call(
        functools.partial(first_kernel, images, 0), "first",
        [(features, "v"), (shared_taps, "a"), (sel1, "v"), (scal, "s")],
        [(tile1, f32), ((2, 1, DOMAINS, c), f32)],
        shift=shift2, weights=1, limit=46,
    )
    p1, priors = lax.optimization_barrier((p1, priors))
    (priors,) = place.halo([place.join(priors, 2)], 1, images)
    stats1 = total_stats(place, local, number[None, :, None])

    act1, p2, local = call(
        functools.partial(second_kernel, images), "second",
        [
            (p1, "v"), (shared_taps, "a"), (stats1, "v"), (gb1, "v"), (sel1, "v"), (sel0, "v"),
            (scal, "s"),
        ],
        [(tile1, bf16), (tile0, f32), ((2, 1, DOMAINS, c), f32)],
        shift=shift1, weights=1, limit=44,
    )
    h0, h1, local_h = call(
        hidden_kernel, "hidden",
        [(act1, "v"), (priors, "v"), (first_w, "v"), (sel1, "v"), (scal, "s")],
        [(tile1, f32), (tile1, f32), ((2, TASKS, DOMAINS, c), f32)], limit=12,
    )
    local = jnp.concatenate([local, local_h], axis=1)
    stats2 = total_stats(place, local, number[None, :, None])
    stats2, task_cot, shared_cot = lax.optimization_barrier((stats2, task_cot, shared_cot))
    (act2,) = call(
        functools.partial(act_kernel, 0), "act",
        [(p2, "v"), (stats2, "v"), (gb2, "v"), (sel0, "v")],
        [(tile0, bf16)], limit=4,
    )
    (act2,) = place.halo([act2], 2, images)
    act2, task_cot, shared_cot = lax.optimization_barrier((act2, task_cot, shared_cot))
    cots = jnp.concatenate([task_cot, shared_cot[None]]).transpose(0, 2, 3, 1, 4)
    cots = place.pieces(cots.reshape(TASKS + 1, half_h, half_w * images, c))
    hidden0, hidden1, g0, g1, local_g = call(
        gate_kernel, "gate",
        [
            (h0, "v"), (h1, "v"), (second_w, "v"), (stats2, "v"), (gb2, "v"), (sel1, "v"),
            (scal, "s"),
        ],
        [
            (tile1, bf16), (tile1, bf16), (tile1, f32), (tile1, f32),
            ((2, TASKS, DOMAINS, c), f32),
        ],
        limit=10,
    )

    p3, local = call(
        functools.partial(first_kernel, images, 2 * TAPS), "third",
        [(act2, "v"), (shared_taps, "a"), (sel1, "v"), (scal, "s")],
        [(tile1, f32), ((2, 1, DOMAINS, c), f32)],
        shift=shift2, weights=1, limit=46,
    )
    stats3 = total_stats(
        place, jnp.concatenate([local, local_g], axis=1), number[None, :, None]
    )

    m0, m1, r0, r1, local = call(
        functools.partial(fourth_kernel, images), "fourth",
        [
            (p3, "v"), (g0, "v"), (g1, "v"), (task_taps, "a"), (stats3, "v"), (gb3, "v"),
            (sel1, "v"), (sel0, "v"), (scal, "s"),
        ],
        [
            (tile1, bf16), (tile1, bf16), (tile0, f32), (tile0, f32),
            ((2, TASKS, DOMAINS, c), f32),
        ],
        shift=shift1, weights=2, limit=44,
    )
    local, cots = lax.optimization_barrier((local, cots))
    cots = place.join(cots, 2)
    statsr = total_stats(place, local, number[None, :, None])

    local, dy_r = call(
        refined_sums_kernel, "refined_sums",
        [
            (r0, "v"), (r1, "v"), (cots[0], "v"), (cots[1], "v"), (up0, "v"), (statsr, "v"),
            (gbr, "v"), (sel0, "v"),
        ],
        [((TASKS, 2, DOMAINS, c), f32), ((TASKS, *tile0), f32)],
        extra=[(half_h, rows0, c)], limit=6,
    )
    sums_r = total_sums(place, local)
    dv_r = call(
        refined_back_kernel, "refined_back",
        [
            (r0, "v"), (r1, "v"), (dy_r, "v"), (statsr, "v"), (gbr, "v"), (sums_r, "v"),
            (sel0, "v"), (scal, "s"),
        ],
        [(tile0, bf16), (tile0, bf16)], limit=4,
    )
    (shared_low,) = place.halo([cots[TASKS]], 1, images)
    dv_halo = place.halo(dv_r, 2, images)
    part = parts(
        place, ((0, 2, True), (1, 3, True)), images, [m0, m1], dv_r
    )
    part = place.scatter_core(part)
    dv_halo, part, shared_low = lax.optimization_barrier((dv_halo, part, shared_low))
    (grad0,) = call(
        functools.partial(conv_back_kernel, images, 0), "masked_back0",
        [(dv_halo[0], "v"), (task_taps, "a")], [(tile1, f32)],
        shift=shift2, weights=1, back=True, limit=44,
    )
    task_chunk, grad0 = place.scatter_chips(part, grad0)
    dy3, dyg0, dyg1, local = call(
        functools.partial(masked_back_kernel, images), "masked_back1",
        [
            (dv_halo[1], "v"), (task_taps, "a"), (grad0, "v"), (p3, "v"), (g0, "v"), (g1, "v"),
            (shared_low, "v"), (up1, "v"), (stats3, "v"), (gb3, "v"), (sel1, "v"),
        ],
        [(tile1, f32), (tile1, f32), (tile1, f32), ((3, 2, DOMAINS, c), f32)],
        shift=shift2, weights=1, back=True, extra=[(half_h + 2, rows1, c)], limit=40,
    )
    local, task_chunk = lax.optimization_barrier((local, task_chunk))
    task_rows = gather_rows(place, task_chunk)

    sums3 = total_sums(place, local)
    dv3, dy2, local = call(
        functools.partial(third_back_kernel, images), "third_back",
        [
            (dy3, "v"), (p3, "v"), (p2, "v"), (shared_taps, "a"), (stats3, "v"), (gb3, "v"),
            (sums3, "v"), (stats2, "v"), (gb2, "v"), (sel1, "v"), (sel0, "v"), (scal, "s"),
        ],
        [(tile1, bf16), (tile0, f32), ((1, 2, DOMAINS, c), f32)],
        shift=shift1, weights=1, back=True, limit=40,
    )
    dvg0, dvg1, dyh0, dyh1, local_h = call(
        gate_back_kernel, "gate_back",
        [
            (dyg0, "v"), (dyg1, "v"), (g0, "v"), (g1, "v"), (h0, "v"), (h1, "v"),
            (second_w, "v"), (stats3, "v"), (gb3, "v"), (sums3, "v"), (stats2, "v"), (gb2, "v"),
            (sel1, "v"), (scal, "s"),
        ],
        [
            (tile1, bf16), (tile1, bf16), (tile1, f32), (tile1, f32),
            ((TASKS, 2, DOMAINS, c), f32),
        ],
        limit=10,
    )
    part3 = parts(
        place, ((0, 3, False), (1, 4, False), (2, 5, True)), images,
        [hidden0, hidden1, act2], [dvg0, dvg1, dv3],
    )
    part3 = place.scatter_core(part3)

    sums2 = total_sums(place, jnp.concatenate([local, local_h]))
    (dv2,) = call(
        functools.partial(back_kernel, 0, False), "second_dv",
        [
            (dy2, "v"), (p2, "v"), (stats2, "v"), (gb2, "v"), (sums2, "v"), (sel0, "v"),
            (scal, "s"),
        ],
        [(tile0, bf16)], limit=4,
    )
    (dv2_halo,) = place.halo([dv2], 2, images)
    dvh0, dvh1, grad_hidden = call(
        hidden_back_kernel, "hidden_back",
        [
            (dyh0, "v"), (dyh1, "v"), (h0, "v"), (h1, "v"), (first_w, "v"), (stats2, "v"),
            (gb2, "v"), (sums2, "v"), (sel1, "v"), (scal, "s"),
        ],
        [(tile1, bf16), (tile1, bf16), (tile1, f32)], limit=10,
    )
    part2 = parts(
        place,
        ((0, 5, True), (0, 3, False), (1, 3, False), (0, 4, False), (2, 4, False)),
        images, [act1, priors[0], priors[1]], [dvh0, dvh1, dv2],
    )
    part2 = place.scatter_core(part2)
    dv2_halo, grad_hidden, part2, part3 = lax.optimization_barrier(
        (dv2_halo, grad_hidden, part2, part3)
    )
    part = jnp.concatenate([part2[:TAPS], part3[TASKS:], part2[TAPS:], part3[:TASKS]])
    part, _ = place.scatter_chips(part, share=0.8)
    dy1, local = call(
        functools.partial(second_back_kernel, images), "second_back",
        [
            (dv2_halo, "v"), (shared_taps, "a"), (grad_hidden, "v"), (p1, "v"), (stats1, "v"),
            (gb1, "v"), (sel1, "v"),
        ],
        [(tile1, f32), ((1, 2, DOMAINS, c), f32)],
        shift=shift2, weights=1, back=True, limit=40,
    )

    sums1 = total_sums(place, local)
    sums1, part = lax.optimization_barrier((sums1, part))
    rest_rows = gather_rows(place, part)
    (dv1,) = call(
        functools.partial(back_kernel, 0, True), "first_dv",
        [
            (dy1, "v"), (p1, "v"), (stats1, "v"), (gb1, "v"), (sums1, "v"), (sel1, "v"),
            (scal, "s"),
        ],
        [(tile1, bf16)], limit=4,
    )
    part1 = place.scatter_core(parts(place, ((0, 1, True),), images, [features], [dv1]))
    chunk1, _ = place.scatter_chips(part1)
    chunk1, dv1, p3, r0, r1, dvh0, dvh1 = lax.optimization_barrier(
        (chunk1, dv1, p3, r0, r1, dvh0, dvh1)
    )

    def own(tile, border):
        width = (breadth + 2 * border) * images
        return lax.dynamic_slice_in_dim(tile, place.rep * breadth * images, width, tile.ndim - 2)

    def pooled(value, stat, gb):
        of = jnp.tile(member, (breadth, 1))
        average = jnp.where(of[:, :1] > 0.5, stat[0, :1], stat[0, 1:])
        inverse = lax.rsqrt(jnp.where(of[:, :1] > 0.5, stat[1, :1], stat[1, 1:]) + EPSILON)
        normed = (value - average) * inverse * gb[0] + gb[1]
        out = jax.nn.silu(normed).reshape(half_h, 2, half_w, 2, images, c)
        return jnp.mean(out, axis=(1, 3)).transpose(2, 0, 1, 3).astype(bf16)

    own3 = own(p3[1:-1, images : images + rows0], 0)
    shared_out = pooled(own3, stats3[:, 0], gb3[0])
    task_out = jnp.stack([pooled(own((r0, r1)[t], 0), statsr[:, t], gbr[t]) for t in range(TASKS)])

    near = own(dv1[:, : rows0 + 2 * images], 1).reshape(height + 2, breadth + 2, images, c)
    grad_features = lax.conv_general_dilated(
        near,
        jnp.flip(shared_w[0], (0, 1)),
        (1, 1),
        "VALID",
        dimension_numbers=("HWNC", "HWOI", "HWNC"),
        preferred_element_type=f32,
    ).transpose(2, 0, 1, 3)
    grad_priors = []
    for t, dv in enumerate((dvh0, dvh1)):
        mine = own(dv[1:-1, images : images + rows0], 0)
        value = jnp.einsum("hrd,cd->hrc", mine, first_w[t, c:], preferred_element_type=f32)
        grad_priors.append(value.reshape(height, breadth, images, c).transpose(2, 0, 1, 3))

    (grad_task,) = spread(place, task_rows, 0, [TASKS * TAPS], 9)
    beside = (shared_out, task_out, grad_features, grad_priors)
    late = (CONVS - 1) * TAPS
    if place.rows == 4 and place.cols == 8:
        grad_task, beside, *swapped = place.gather_swaps(chunk1, grad_task, beside)
        shared_out, task_out, grad_features, grad_priors = beside
        grad_shared = place_swapped(place, swapped, CONVS * TAPS, 3)
    else:
        (grad_shared,) = spread(place, gather_rows(place, chunk1), 0, [TAPS], 9)
        grad_shared = jnp.pad(grad_shared, ((0, late), (0, 0), (0, 0)))
    (grad_shared,) = spread(place, rest_rows, 0, [late], 9, grad_shared)
    grad_first, grad_second = spread(place, rest_rows, late, [2 * TASKS, TASKS], 3)

    shared_sums = jnp.sum(jnp.stack([sums1[0], sums2[0], sums3[0]]), axis=2)
    task_sums = jnp.sum(jnp.stack([sums2[1:], sums3[1:], sums_r], axis=1), axis=3)
    return (
        shared_out,
        task_out,
        grad_features,
        jnp.stack(grad_priors),
        grad_shared.reshape(shared_w.shape),
        shared_sums[:, 1],
        shared_sums[:, 0],
        grad_first.reshape(first_w.shape),
        grad_second.reshape(second_w.shape),
        grad_task.reshape(task_conv.shape),
        task_sums[:, :, 1],
        task_sums[:, :, 0],
    )


def solution(mesh):
    return jax.shard_map(
        body,
        mesh=mesh,
        in_specs=(
            P(None, "row", "col", None),
            P(None, None, "row", "col", None),
            P(),
            P(),
            P(),
            P(),
            P(),
            P(),
            P(),
            P(),
            P(),
            P(None, "row", "col", None),
            P(None, None, "row", "col", None),
        ),
        out_specs=(
            P(None, "row", "col", None),
            P(None, None, "row", "col", None),
            P(None, "row", "col", None),
            P(None, None, "row", "col", None),
            P(),
            P(),
            P(),
            P(),
            P(),
            P(),
            P(),
            P(),
        ),
        check_vma=False,
    )
```
